32 devices in a mesh: dp: 4 (over x, core), chan: 8 (over z, y).
Axes of the slice: x: 2, y: 2, z: 4, core: 2. Of those that a mesh axis runs over, the one named last changes fastest.
Arguments:
- features: bfloat16 [512, 2, 128, 256], P('chan', None, 'dp'), may hold values from -6 to 6
- latent: bfloat16 [2, 512], replicated, may hold values from -6 to 6
- affine: bfloat16 [512, 512], replicated, may hold values from -0.25 to 0.25
- affine_bias: float32 [512], replicated, may hold values from 0.5 to 1.5
- weight: bfloat16 [3, 3, 512, 512], P(None, None, 'chan'), may hold values from -0.09375 to 0.09375
- out_bias: float32 [512], P('chan'), may hold values from -3 to 3
- cotangent: bfloat16 [512, 2, 128, 256], P('chan', None, 'dp'), may hold values from -6 to 6
- latents_all: bfloat16 [2048, 512], P(('dp', 'chan')), may hold values from -6 to 6
- labels: int32 [2048], P(('dp', 'chan')), may hold values from 0 to 999
- class_means: float32 [1000, 512], replicated, may hold values from -6 to 6
Outputs:
- output: bfloat16 [512, 2, 128, 256], P('chan', None, 'dp')
- grad_features: float32 [512, 2, 128, 256], P('chan', None, 'dp')
- grad_latent: float32 [2, 512], replicated
- grad_affine: float32 [512, 512], replicated
- grad_affine_bias: float32 [512], replicated
- grad_weight: float32 [3, 3, 512, 512], P(None, None, 'chan')
- grad_bias: float32 [512], P('chan')
- class_target: float32 [1000, 512], replicated
The draws below stay inside these ranges and needn't reach their ends.
All inputs are finite; a program needn't handle non-finite values.
Results may differ from the reference program's by a relative error of at most 0.0053.
Values may be sent and summed in bfloat16 or wider, within the bound.
No kernel may reach another device: no remote copies, remote signals or barrier semaphores. Data moves between devices by JAX's collectives and lax.ppermute only.
A program may use at most 512 MiB of HBM per device.

```python
import math
import jax
import jax.numpy as jnp
import numpy as np
from jax import lax

CH = 512
WDIM = 512
NCLS = 1000
ITEMS = 2
WPX = 256
HEIGHT = 128
LATENTS = 2048


def with_ends(values, own_key, low, high):
    place = [jax.random.randint(jax.random.fold_in(own_key, axis), (), 0, length) for axis, length in enumerate(values.shape)]
    longest = values.shape.index(max(values.shape))
    neighbour = place[:longest] + [(place[longest] + 1) % values.shape[longest]] + place[longest + 1:]
    return values.at[tuple(place)].set(low).at[tuple(neighbour)].set(high)


def level_of(stream_key, extent, cuts, smallest, top_value):
    level, own = 1.0, jax.random.fold_in(stream_key, 6)
    for position, blocks in cuts:
        steps = jnp.exp(jax.random.uniform(jax.random.fold_in(own, position), (blocks,), jnp.float32, smallest / len(cuts), top_value / len(cuts)))
        level = level * jnp.repeat(steps, extent[position] // blocks).reshape([-1 if axis == position else 1 for axis in range(len(extent))])
    return level


def cumulative_ranks(count, lean):
    loads = [(1 << 20) // math.isqrt(grade ** lean) + 1 for grade in range(1, count + 1)]
    scale = 1 + sum(loads) // (1 << 30)
    return np.cumsum(np.array([max(1, weight // scale) for weight in loads]))


def ranked_ids(stream_key, dims, count, slope):
    table = cumulative_ranks(count, slope)
    lot = jax.random.randint(jax.random.fold_in(stream_key, 1), dims, 0, int(table[count - 1]))
    grade = jnp.searchsorted(jnp.asarray(table, jnp.int32), lot, side="right")
    return jax.random.permutation(jax.random.fold_in(stream_key, 2), count)[grade].astype(jnp.int32)


def bell_draw(own_key, extent, spread, reach, split=(), held_as=jnp.bfloat16):
    entries = jax.random.normal(own_key, extent, jnp.float32) * spread
    if len(split) > 0:
        entries = level_of(own_key, extent, split, -0.22, 0.18) * entries
    return jnp.clip(entries, min=-reach, max=reach).astype(held_as)


def setup_inputs(seed: int = 0) -> dict:
    arg_keys = jax.random.split(jax.random.key(seed), 11)
    return {
        "features": bell_draw(arg_keys[0], (CH, ITEMS, HEIGHT, WPX), 1.0, 6.0, ((0, 8), (2, 4))),
        "latent": bell_draw(arg_keys[1], (ITEMS, WDIM), 1.0, 6.0),
        "affine": bell_draw(arg_keys[2], (WDIM, CH), WDIM ** -0.5, 0.25),
        "affine_bias": jnp.clip(1.0 + 0.1 * jax.random.normal(arg_keys[3], (CH,), jnp.float32), 0.5, 1.5),
        "weight": bell_draw(arg_keys[4], (3, 3, CH, CH), (9 * CH) ** -0.5, 0.09375, ((2, 8),)),
        "out_bias": bell_draw(arg_keys[5], (CH,), 0.5, 3.0, ((0, 8),), jnp.float32),
        "cotangent": bell_draw(arg_keys[6], (CH, ITEMS, HEIGHT, WPX), 1.0, 6.0, ((0, 8), (2, 4))),
        "latents_all": bell_draw(arg_keys[7], (LATENTS, WDIM), 1.0, 6.0, ((0, 32),)),
        "labels": with_ends(ranked_ids(arg_keys[8], (LATENTS,), NCLS, 3), jax.random.fold_in(arg_keys[8], 3), 0, NCLS - 1).astype(jnp.int32),
        "class_means": bell_draw(arg_keys[9], (NCLS, WDIM), 1.0, 6.0, (), jnp.float32),
    }


@jax.custom_vjp
def low(v):
    return lax.optimization_barrier(v.astype(jnp.bfloat16)).astype(jnp.float32)

@jax.custom_vjp
def low_back(v):
    return v

def low_keep(v):
    return (low(v), None)

def low_pass(kept, grad):
    return (grad,)

def back_keep(v):
    return (v, None)

def back_low(kept, grad):
    return (low(grad),)
low.defvjp(low_keep, low_pass)
low_back.defvjp(back_keep, back_low)

def sinc_taps():
    offset = jnp.arange(12).astype(jnp.float32) - 5.5
    window = 0.5 + 0.5 * jnp.cos(jnp.pi * offset / 6.0)
    values = jnp.sinc(offset * 0.5) * window
    return values / jnp.sum(values)

def band_table(row_total, col_total, row_mult, col_mult, shift, factor):
    row_ids = jnp.arange(row_total).astype(jnp.int32)[:, None, None]
    col_ids = jnp.arange(col_total).astype(jnp.int32)[None, :, None]
    tap_ids = jnp.arange(12).astype(jnp.int32)[None, None, :]
    hit_mask = row_mult * row_ids + col_mult * col_ids + shift == tap_ids
    return factor * lax.optimization_barrier(jnp.sum(jnp.where(hit_mask, sinc_taps()[None, None, :], 0.0), axis=2))

def reference(features, latent, affine, affine_bias, weight, out_bias, cotangent, latents_all, labels, class_means):
    highest = lax.Precision.HIGHEST
    height = features.shape[2]
    row_width = features.shape[3]
    up_cols = band_table(2 * row_width, row_width, 1, -2, 5, 2.0)
    down_cols = band_table(row_width, 2 * row_width, -2, 1, 5, 1.0)
    up_rows = band_table(2 * height, height, 1, -2, 5, 2.0)
    down_rows = band_table(height, 2 * height, -2, 1, 5, 1.0)

    def forward(feat_in, lat_in, aff_in, abias_in, wgt_in, bias_in):
        styles = jnp.dot(lat_in, aff_in, precision=highest) + abias_in
        weight_sq = lax.optimization_barrier(jnp.sum(wgt_in * wgt_in, axis=(0, 1)))
        demod_scale = lax.rsqrt(jnp.dot(styles * styles, weight_sq.T, precision=highest) + 1e-08)

        def one_item(triple):
            feat_item, style_item, demod_item = triple
            modded = low(feat_item * style_item[:, None, None])
            padded = jnp.pad(modded, ((0, 0), (1, 1), (1, 1)))
            raw_conv = jnp.zeros(feat_item.shape, jnp.float32)
            for tap_row in range(3):
                for tap_col in range(3):
                    raw_conv = raw_conv + jnp.einsum('oi,ihw->ohw', wgt_in[tap_row, tap_col], padded[:, tap_row:tap_row + height, tap_col:tap_col + row_width], precision=highest)
            raw_conv = low_back(raw_conv)
            biased = raw_conv * demod_item[:, None, None] + bias_in[:, None, None]
            wide_rows = jnp.einsum('chw,vw->chv', biased, up_cols, precision=highest)
            upsampled = jnp.einsum('chv,oh->cov', wide_rows, up_rows, precision=highest)
            active = jax.nn.silu(upsampled)
            narrow = jnp.einsum('cov,io->civ', active, down_rows, precision=highest)
            return jnp.einsum('civ,jv->cij', narrow, down_cols, precision=highest)
        stacked = lax.map(jax.checkpoint(one_item), (jnp.transpose(feat_in, (1, 0, 2, 3)), styles, demod_scale))
        return jnp.transpose(stacked, (1, 0, 2, 3))
    primals = (features.astype(jnp.float32), latent.astype(jnp.float32), affine.astype(jnp.float32), affine_bias, weight.astype(jnp.float32), out_bias)
    result, pullback = jax.vjp(forward, *primals)
    gradients = pullback(cotangent.astype(jnp.float32))
    class_total = class_means.shape[0]
    class_sums = jax.ops.segment_sum(latents_all.astype(jnp.float32), labels, num_segments=class_total)
    counts = jax.ops.segment_sum(jnp.ones(labels.shape, jnp.float32), labels, num_segments=class_total)
    target = jnp.where(counts[:, None] > 0, class_sums / jnp.maximum(counts, 1.0)[:, None], class_means)
    return (result.astype(jnp.bfloat16), gradients[0], gradients[1], gradients[2], gradients[3], gradients[4], gradients[5], target)
```

```python
import functools

import jax
import jax.numpy as jnp
import ml_dtypes
import numpy as np
from jax import lax
from jax.experimental import pallas as pl
from jax.experimental.pallas import tpu as pltpu
from jax.sharding import PartitionSpec as P

F32 = jnp.float32
BF16 = jnp.bfloat16
IN_VMEM = pl.BlockSpec(memory_space=pltpu.VMEM)
IN_SMEM = pl.BlockSpec(memory_space=pltpu.SMEM)
PARAMS = pltpu.CompilerParams(vmem_limit_bytes=56 << 20)
RIM = 6
GROUP = 16


def struct(shape, dtype):
    return jax.ShapeDtypeStruct(shape, dtype)


def sinc_taps():
    offset = np.arange(12) - 5.5
    values = np.sinc(offset * 0.5) * (0.5 + 0.5 * np.cos(np.pi * offset / 6.0))
    return values / values.sum()


def up_table(size):
    tap = np.arange(2 * size)[None, :] - 2 * np.arange(size)[:, None] + 5
    held = (tap >= 0) & (tap < 12)
    return np.where(held, 2.0 * sinc_taps()[np.clip(tap, 0, 11)], 0.0).astype(np.float32)


def halves(table):
    high = table.astype(ml_dtypes.bfloat16)
    return high, (table - high.astype(np.float32)).astype(ml_dtypes.bfloat16)


def from_neighbours(value, axis, dim, width):
    size, length = lax.axis_size(axis), value.shape[dim]
    up = [(i, i + 1) for i in range(size - 1)]
    down = [(j, i) for i, j in up]
    last = lax.slice_in_dim(value, length - width, length, axis=dim)
    first = lax.slice_in_dim(value, 0, width, axis=dim)
    return lax.ppermute(last, axis, up), lax.ppermute(first, axis, down)


def exchange(parts, axis):
    size = lax.axis_size(axis)
    return [parts[0]] + [
        lax.ppermute(parts[x], axis, [(i, i ^ x) for i in range(size)]) for x in range(1, size)
    ]


def row_parts(rows, me, blocks, span, halo):
    parts = []
    for x in range(lax.axis_size("chan")):
        dest = me ^ x
        part = lax.dynamic_slice(
            rows,
            (dest // blocks, (dest % blocks) * span, 0, 0),
            (1, span + halo, rows.shape[2], rows.shape[3]),
        )
        parts.append(part[0])
    return parts


def fill_shifted(me, parts, scales, shifted, count):
    split = len(parts) // count
    for h in range(split):
        for x in range(count):
            part = parts[h * count + x]
            rows, width, columns = part.shape
            source = me ^ x
            spot = pl.ds(h * width, width)
            column = lax.broadcasted_iota(jnp.int32, (width, columns), 1)
            scale = None if scales is None else scales[source]

            def row_step(row, carry, part=part, source=source, spot=spot, column=column, scale=scale):
                value = part[row].astype(F32)
                if scale is not None:
                    value = (value * scale).astype(BF16).astype(F32)
                before = jnp.where(column == 0, 0.0, pltpu.roll(value, 1, 1))
                after = jnp.where(column == columns - 1, 0.0, pltpu.roll(value, columns - 1, 1))
                shifted[row, 0, source, spot] = before.astype(BF16)
                shifted[row, 1, source, spot] = value.astype(BF16)
                shifted[row, 2, source, spot] = after.astype(BF16)
                return carry

            lax.fori_loop(0, rows, row_step, 0)


def convolved(taps, shifted, row, channels, columns):
    total = None
    for i in range(3):
        for j in range(3):
            term = jnp.dot(
                taps[3 * i + j],
                shifted[row + i, j].reshape(channels, columns),
                preferred_element_type=F32,
            )
            total = term if total is None else total + term
    return total


def forward_kernel(count, split, me_ref, taps, scales, *refs):
    parts, outs = refs[:count], refs[count : count + split * count]
    shifted, sums = refs[-2:]
    me = me_ref[0]
    _, _, _, own, columns = shifted.shape
    width = own // split
    fill_shifted(me, parts, scales, shifted, count)

    def row_step(row, carry):
        total = convolved(taps, shifted, row, count * own, columns)
        sums[...] = total.astype(BF16).reshape(sums.shape)
        for h in range(split):
            for x in range(count):
                outs[h * count + x][row] = sums[me ^ x, h * width : (h + 1) * width]
        return carry

    lax.fori_loop(0, outs[0].shape[0], row_step, 0)


def conv_forward(me, taps, scales, parts, split):
    count = len(parts)
    rows, own, columns = parts[0].shape
    outs = pl.pallas_call(
        functools.partial(forward_kernel, count, split),
        out_shape=[struct((rows - 2, own // split, columns), BF16)] * (count * split),
        in_specs=[IN_SMEM] + [IN_VMEM] * (2 + count),
        out_specs=[IN_VMEM] * (count * split),
        scratch_shapes=[
            pltpu.VMEM((rows, 3, count, own, columns), BF16),
            pltpu.VMEM((count, own, columns), BF16),
        ],
        compiler_params=PARAMS,
        name="conv_forward",
    )(me, taps, scales, *parts)
    return [outs[h * count : (h + 1) * count] for h in range(split)]


def backward_kernel(count, split, me_ref, taps, *refs):
    grads, feats = refs[: count * split], refs[count * split : count * (split + 1)]
    outs = refs[count * (split + 1) : count * (split + 2)]
    style_ref, shifted, sums = refs[count * (split + 2) :]
    me = me_ref[0]
    _, _, _, own, columns = shifted.shape
    fill_shifted(me, grads, None, shifted, count)
    style_ref[...] = jnp.zeros_like(style_ref)

    def row_step(row, carry):
        total = convolved(taps, shifted, row, count * own, columns)
        sums[...] = total.reshape(sums.shape)
        for x in range(count):
            value = sums[me ^ x]
            outs[x][row] = value.astype(BF16)
            product = value * feats[x][row + 1].astype(F32)
            style_ref[me ^ x] += jnp.sum(product, axis=1, keepdims=True)
        return carry

    lax.fori_loop(0, outs[0].shape[0], row_step, 0)


def conv_backward(me, taps, grads, feats):
    count = len(feats)
    split = len(grads) // count
    rows, own, columns = feats[0].shape
    outs = pl.pallas_call(
        functools.partial(backward_kernel, count, split),
        out_shape=[struct((rows - 2, own, columns), BF16)] * count + [struct((count, own, 1), F32)],
        in_specs=[IN_SMEM] + [IN_VMEM] * (1 + len(grads) + count),
        out_specs=[IN_VMEM] * (count + 1),
        scratch_shapes=[
            pltpu.VMEM((rows, 3, count, own, columns), BF16),
            pltpu.VMEM((count, own, columns), F32),
        ],
        compiler_params=PARAMS,
        name="conv_backward",
    )(me, taps, *grads, *feats)
    return outs[:-1], outs[-1]


def weight_kernel(count, split, me_ref, scales, *refs):
    grads, feats = refs[: count * split], refs[count * split : count * (split + 1)]
    out, shifted, rows_ref = refs[count * (split + 1) :]
    me = me_ref[0]
    rows, _, _, own, columns = shifted.shape
    width = own // split
    channels = count * own
    fill_shifted(me, feats, scales, shifted, count)
    for h in range(split):
        for x in range(count):
            rows_ref[:, me ^ x, h * width : (h + 1) * width] = grads[h * count + x][1 : rows - 1]

    def tap_step(tap, carry):
        i, j = lax.div(tap, 3), lax.rem(tap, 3)
        total = None
        for row in range(rows - 2):
            term = lax.dot_general(
                rows_ref[row].reshape(channels, columns),
                shifted[row + i, j].reshape(channels, columns),
                (((1,), (1,)), ((), ())),
                preferred_element_type=F32,
            )
            total = term if total is None else total + term
        out[tap] = total.astype(BF16)
        return carry

    lax.fori_loop(0, 9, tap_step, 0)


def conv_weight(me, scales, grads, feats):
    count = len(feats)
    split = len(grads) // count
    rows, own, columns = feats[0].shape
    return pl.pallas_call(
        functools.partial(weight_kernel, count, split),
        out_shape=struct((9, count * own, count * own), BF16),
        in_specs=[IN_SMEM] + [IN_VMEM] * (1 + len(grads) + count),
        out_specs=IN_VMEM,
        scratch_shapes=[
            pltpu.VMEM((rows, 3, count, own, columns), BF16),
            pltpu.VMEM((rows - 2, count, own, columns), BF16),
        ],
        compiler_params=PARAMS,
        name="conv_weight",
    )(me, scales, *grads, *feats)


def gather_kernel(count, me_ref, *refs):
    parts, (out, first, last) = refs[:count], refs[count:]
    me = me_ref[0]
    items, rows, _, _ = out.shape
    blocks = count // items
    span = rows // blocks
    for x in range(count):
        source = me ^ x
        out[source // blocks, pl.ds((source % blocks) * span, span)] = parts[x][...]
    first[...] = out[:, :RIM]
    last[...] = out[:, rows - RIM :]


def gather_rows(me, parts, items):
    count = len(parts)
    span, width, columns = parts[0].shape
    rows = span * count // items
    rim = struct((items, RIM, width, columns), BF16)
    return pl.pallas_call(
        functools.partial(gather_kernel, count),
        out_shape=[struct((items, rows, width, columns), BF16), rim, rim],
        in_specs=[IN_SMEM] + [IN_VMEM] * count,
        out_specs=[IN_VMEM] * 3,
        compiler_params=PARAMS,
        name="gather_rows",
    )(me, *parts)


def sinc_kernel(
    edge_ref,
    raw,
    before,
    after,
    cotangent,
    demod,
    bias,
    up_high,
    up_low,
    down_high,
    down_low,
    up_sums,
    out,
    grad_raw,
    grad_bias,
    grad_demod,
    wide,
    wide_grad,
    narrow,
    narrow_grad,
):
    items, rows, width, columns = raw.shape
    extent = rows + 2 * RIM
    first, last = edge_ref[0], edge_ref[1]
    tap = [float(value) for value in sinc_taps()[:6]]
    lane_tiles = 2 * columns // 128

    def widened(values):
        flat = values.reshape(-1, columns)
        total = jnp.dot(flat, up_high[...], preferred_element_type=F32)
        total = total + jnp.dot(flat, up_low[...], preferred_element_type=F32)
        return total.reshape(-1, GROUP, 2 * columns)

    def narrowed(values):
        flat = values.reshape(rows * GROUP, 2 * columns)
        high = flat.astype(BF16)
        low = (flat - high.astype(F32)).astype(BF16)
        total = jnp.dot(high, down_high[...], preferred_element_type=F32)
        total = total + jnp.dot(high, down_low[...], preferred_element_type=F32)
        total = total + jnp.dot(low, down_high[...], preferred_element_type=F32)
        return total.reshape(rows, GROUP, columns)

    def tile_step(index, carry):
        lanes = pl.ds(pl.multiple_of(lax.rem(index, lane_tiles) * 128, 128), 128)
        subs = pl.ds(pl.multiple_of(lax.div(index, lane_tiles) * 8, 8), 8)
        sums, picked = [{}, {}], [{}, {}]
        for row in range(extent):
            for which, ref in ((0, wide), (1, wide_grad)):
                value = ref[row, subs, lanes]
                products = [value * (2.0 * tap[t]) for t in range(6)]
                for offset in range(-3, 4):
                    pair = row - RIM + offset
                    for parity in range(2):
                        t = 2 * offset + parity + 5
                        if -3 <= pair < rows + 3 and 0 <= t < 12:
                            term = products[min(t, 11 - t)]
                            key = 2 * pair + parity
                            sums[which][key] = sums[which][key] + term if key in sums[which] else term
            pair = row - RIM - 3
            if pair < -3:
                continue
            for key in (2 * pair, 2 * pair + 1):
                value, grad = sums[0].pop(key), sums[1].pop(key)
                sigmoid = 1.0 / (1.0 + jnp.exp(-value))
                active = value * sigmoid
                grad = grad * (sigmoid + active * (1.0 - sigmoid))
                if pair < 0:
                    active, grad = active * first, grad * first
                if pair >= rows:
                    active, grad = active * last, grad * last
                picked[0][key], picked[1][key] = active, grad
            centre = pair - 3
            if centre >= 0:
                for which, ref in ((0, narrow), (1, narrow_grad)):
                    store = picked[which]
                    total = None
                    for t in range(6):
                        term = tap[t] * (store[2 * centre + t - 5] + store[2 * centre + 6 - t])
                        total = term if total is None else total + term
                    ref[centre, subs, lanes] = total
                    store.pop(2 * centre - 5)
                    store.pop(2 * centre - 4)
        return carry

    for item in range(items):
        for group in range(width // GROUP):
            at = slice(group * GROUP, (group + 1) * GROUP)
            scale = demod[item, at]
            shift = bias[at] * up_sums[...]
            wide[:RIM] = widened(before[item, :, at]) * scale + shift * first
            wide[RIM : RIM + rows] = widened(raw[item, :, at]) * scale + shift
            wide[RIM + rows :] = widened(after[item, :, at]) * scale + shift * last
            wide_grad[...] = widened(cotangent[item, :, at])
            lax.fori_loop(0, GROUP // 8 * lane_tiles, tile_step, 0)
            result = narrowed(narrow[...])
            out[at, item] = jnp.swapaxes(result, 0, 1).astype(BF16)
            grad = narrowed(narrow_grad[...])
            grad_raw[item, :, at] = (grad * scale).astype(BF16)
            own = raw[item, :, at].astype(F32)
            grad_bias[item, at] = jnp.sum(jnp.sum(grad, axis=0), axis=1, keepdims=True)
            grad_demod[item, at] = jnp.sum(jnp.sum(grad * own, axis=0), axis=1, keepdims=True)


def sinc_both(edges, raw, before, after, cotangent, demod, bias, tables):
    items, rows, width, columns = raw.shape
    wide = pltpu.VMEM((rows + 2 * RIM, GROUP, 2 * columns), F32)
    narrow = pltpu.VMEM((rows, GROUP, 2 * columns), F32)
    return pl.pallas_call(
        sinc_kernel,
        out_shape=[
            struct((width, items, rows, columns), BF16),
            struct((items, rows, width, columns), BF16),
            struct((items, width, 1), F32),
            struct((items, width, 1), F32),
        ],
        in_specs=[IN_SMEM] + [IN_VMEM] * 11,
        out_specs=[IN_VMEM] * 4,
        scratch_shapes=[wide, wide, narrow, narrow],
        compiler_params=PARAMS,
        name="sinc_both",
    )(edges, raw, before, after, cotangent, demod, bias, *tables)


def scale_kernel(count, me_ref, scales, *refs):
    parts, (out, gathered) = refs[:count], refs[count:]
    me = me_ref[0]
    width, items, rows, columns = out.shape
    blocks = count // items
    span = rows // blocks
    for x in range(count):
        source = me ^ x
        gathered[source // blocks, pl.ds((source % blocks) * span, span)] = parts[x][...]
    for item in range(items):
        for group in range(width // GROUP):
            at = slice(group * GROUP, (group + 1) * GROUP)
            value = gathered[item, :, at].astype(F32) * scales[item, at]
            out[at, item] = jnp.swapaxes(value, 0, 1)


def scaled(me, scales, parts, items):
    count = len(parts)
    span, width, columns = parts[0].shape
    rows = span * count // items
    return pl.pallas_call(
        functools.partial(scale_kernel, count),
        out_shape=struct((width, items, rows, columns), F32),
        in_specs=[IN_SMEM] + [IN_VMEM] * (1 + count),
        out_specs=IN_VMEM,
        scratch_shapes=[pltpu.VMEM((items, rows, width, columns), BF16)],
        compiler_params=PARAMS,
        name="scale_features",
    )(me, scales, *parts)


def summed_over_dp(values, me):
    bit = 1
    while bit < lax.axis_size("dp"):
        pairs = values.reshape((values.shape[0] // 2, 2) + values.shape[1:])
        side = (me // bit) % 2
        keep = lax.dynamic_index_in_dim(pairs, side, 1, keepdims=False)
        send = lax.dynamic_index_in_dim(pairs, 1 - side, 1, keepdims=False)
        got = lax.ppermute(send, "dp", [(i, i ^ bit) for i in range(lax.axis_size("dp"))])
        values = (keep.astype(F32) + got.astype(F32)).astype(BF16)
        bit *= 2
    return values[0]


def per_device(
    features,
    latent,
    affine,
    affine_bias,
    weight,
    out_bias,
    cotangent,
    latents_all,
    labels,
    class_means,
):
    highest = lax.Precision.HIGHEST
    own, items, rows, columns = features.shape
    channels = weight.shape[3]
    count = lax.axis_size("chan")
    dp_total = lax.axis_size("dp")
    me = lax.axis_index("chan")
    me_dp = lax.axis_index("dp")
    me_ref = me.astype(jnp.int32)[None]
    blocks = count // items
    span = rows // blocks
    split = max(1, min(2, own // GROUP))
    width = own // split

    before, after = from_neighbours(features, "dp", 2, 1)
    extended = jnp.transpose(jnp.concatenate([before, features, after], axis=2), (1, 2, 0, 3))
    feats = exchange(row_parts(extended, me, blocks, span, 2), "chan")
    gathered = lax.all_gather(weight, "chan", axis=2, tiled=True)
    taps_forward = gathered.reshape(9, channels, channels)
    taps_backward = jnp.transpose(gathered[::-1, ::-1], (0, 1, 3, 2)).reshape(9, channels, channels)

    styles = jnp.dot(latent, affine, preferred_element_type=F32) + affine_bias
    own_style = lax.dynamic_slice_in_dim(styles, me * own, own, 1)
    weight_full = weight.astype(F32)
    weight_sq = jnp.sum(weight_full * weight_full, axis=(0, 1))
    demod = lax.rsqrt(jnp.dot(styles * styles, weight_sq.T, precision=highest) + 1e-08)
    item = me // blocks
    item_scales = lax.dynamic_index_in_dim(styles, item, 0, keepdims=False).reshape(count, own, 1)

    cot_before, cot_after = from_neighbours(cotangent, "dp", 2, RIM)
    cot = jnp.transpose(jnp.concatenate([cot_before, cotangent, cot_after], axis=2), (1, 2, 0, 3))
    table = up_table(columns)
    tables = halves(table) + halves(0.5 * table.T) + (np.sum(table, axis=0)[None],)
    edges = jnp.stack([me_dp > 0, me_dp < dp_total - 1]).astype(F32)

    raw_parts = conv_forward(me_ref, taps_forward, item_scales, feats, split)
    results, grad_parts, bias_parts, demod_parts = [], [], [], []
    for h in range(split):
        at = slice(h * width, (h + 1) * width)
        raw, head, tail = gather_rows(me_ref, exchange(raw_parts[h], "chan"), items)
        size = dp_total
        up = [(i, i + 1) for i in range(size - 1)]
        before = lax.ppermute(tail, "dp", up)
        after = lax.ppermute(head, "dp", [(j, i) for i, j in up])
        result, grad_raw, bias_part, demod_part = sinc_both(
            edges,
            raw,
            before,
            after,
            cot[:, :, at],
            demod[:, at, None],
            out_bias[at, None],
            tables,
        )
        results.append(result)
        bias_parts.append(bias_part)
        demod_parts.append(demod_part)
        before, after = from_neighbours(grad_raw, "dp", 1, 1)
        grad_extended = jnp.concatenate([before, grad_raw, after], axis=1)
        grad_parts += exchange(row_parts(grad_extended, me, blocks, span, 2), "chan")
    output = jnp.concatenate(results, axis=0)
    bias_part = jnp.sum(jnp.concatenate(bias_parts, axis=1)[:, :, 0], axis=0)
    g_demod = jnp.concatenate(demod_parts, axis=1)[:, :, 0]

    modded_parts, style_part = conv_backward(me_ref, taps_backward, grad_parts, feats)
    modded_parts = exchange(modded_parts, "chan")
    grad_features = scaled(me_ref, own_style[:, :, None], modded_parts, items)

    grad_bias, g_demod_sum = lax.psum((bias_part, g_demod), "dp")
    cube = demod * demod * demod
    g_style_part = 2.0 * styles * jnp.dot(-0.5 * g_demod * cube, weight_sq, precision=highest)
    g_style_part = g_style_part + jnp.where(
        jnp.arange(items)[:, None] == item, style_part.reshape(1, channels), 0.0
    )
    g_wsq = jnp.dot((-0.5 * g_demod_sum * cube).T, styles * styles, precision=highest)

    g_weight = conv_weight(me_ref, item_scales, grad_parts, feats)
    share = channels // dp_total
    g_weight = jnp.moveaxis(g_weight.reshape(9, count, own, dp_total, share), 3, 0)
    g_weight = summed_over_dp(g_weight, me_dp)
    sent = [lax.dynamic_index_in_dim(g_weight, me ^ x, 1, keepdims=False) for x in range(count)]
    g_weight = sum(part.astype(F32) for part in exchange(sent, "chan"))
    g_weight = lax.all_gather(g_weight, "dp", axis=2, tiled=True).reshape(weight.shape)
    grad_weight = g_weight + 2.0 * weight_full * g_wsq

    all_latents = lax.all_gather(latents_all, ("dp", "chan"), axis=0, tiled=True)
    all_labels = lax.all_gather(labels, ("dp", "chan"), axis=0, tiled=True)
    one_hot = all_labels[None, :] == jnp.arange(class_means.shape[0])[:, None]
    class_sums = jnp.dot(one_hot.astype(BF16), all_latents, preferred_element_type=F32)
    counts = jnp.sum(one_hot.astype(F32), axis=1)
    target = jnp.where(
        counts[:, None] > 0, class_sums / jnp.maximum(counts, 1.0)[:, None], class_means
    )

    g_style = lax.psum(g_style_part, ("dp", "chan"))
    grad_affine_bias = jnp.sum(g_style, axis=0)
    grad_affine = jnp.dot(latent.astype(F32).T, g_style, precision=highest)
    grad_latent = jnp.dot(g_style, affine.astype(F32).T, precision=highest)
    return (
        output,
        grad_features,
        grad_latent,
        grad_affine,
        grad_affine_bias,
        grad_weight,
        grad_bias,
        target,
    )


def solution(mesh):
    in_specs = (
        P("chan", None, "dp", None),
        P(),
        P(),
        P(),
        P(None, None, "chan", None),
        P("chan"),
        P("chan", None, "dp", None),
        P(("dp", "chan"), None),
        P(("dp", "chan")),
        P(),
    )
    out_specs = (
        P("chan", None, "dp", None),
        P("chan", None, "dp", None),
        P(),
        P(),
        P(),
        P(None, None, "chan", None),
        P("chan"),
        P(),
    )
    return jax.shard_map(
        per_device, mesh=mesh, in_specs=in_specs, out_specs=out_specs, check_vma=False
    )
```

```python
import functools

import jax
import jax.numpy as jnp
import ml_dtypes
import numpy as np
from jax import lax
from jax.experimental import pallas as pl
from jax.experimental.pallas import tpu as pltpu
from jax.sharding import PartitionSpec as P

F32 = jnp.float32
BF16 = jnp.bfloat16
IN_VMEM = pl.BlockSpec(memory_space=pltpu.VMEM)
IN_HBM = pl.BlockSpec(memory_space=pltpu.HBM)
IN_SMEM = pl.BlockSpec(memory_space=pltpu.SMEM)
PARAMS = pltpu.CompilerParams(vmem_limit_bytes=60 << 20)
RIM = 7
GROUP = 16


def struct(shape, dtype):
    return jax.ShapeDtypeStruct(shape, dtype)


def sinc_taps():
    offset = np.arange(12) - 5.5
    values = np.sinc(offset * 0.5) * (0.5 + 0.5 * np.cos(np.pi * offset / 6.0))
    return values / values.sum()


def up_table(size):
    tap = np.arange(2 * size)[None, :] - 2 * np.arange(size)[:, None] + 5
    held = (tap >= 0) & (tap < 12)
    return np.where(held, 2.0 * sinc_taps()[np.clip(tap, 0, 11)], 0.0).astype(np.float32)


def halves(table):
    high = table.astype(ml_dtypes.bfloat16)
    return high, (table - high.astype(np.float32)).astype(ml_dtypes.bfloat16)


def from_neighbours(value, axis, dim, width):
    size, length = lax.axis_size(axis), value.shape[dim]
    up = [(i, i + 1) for i in range(size - 1)]
    down = [(j, i) for i, j in up]
    last = lax.slice_in_dim(value, length - width, length, axis=dim)
    first = lax.slice_in_dim(value, 0, width, axis=dim)
    return lax.ppermute(last, axis, up), lax.ppermute(first, axis, down)


def swapped(value, axis, bits):
    return lax.ppermute(value, axis, [(i, i ^ bits) for i in range(lax.axis_size(axis))])


def once(value, *others):
    return lax.optimization_barrier((value,) + others)[0]


def exchange(parts, axis):
    size = lax.axis_size(axis)
    return [parts[0]] + [swapped(parts[x], axis, x) for x in range(1, size)]


def started(sems, first, pairs):
    copies = [
        pltpu.make_async_copy(source, target, sems.at[first + index])
        for index, (source, target) in enumerate(pairs)
    ]
    for copy in copies:
        copy.start()
    return copies


def finished(copies):
    for copy in copies:
        copy.wait()


def rows_kernel(count, me_ref, before, value, after, *refs):
    parts, (arrived, rows_first, sems) = refs[:count], refs[count:]
    me = me_ref[0]
    width, items, rows, _ = value.shape
    blocks = count // items
    span = rows // blocks
    finished(started(sems, 0, [(value, arrived)]))
    for item in range(items):
        for group in range(width // GROUP):
            at = slice(group * GROUP, (group + 1) * GROUP)
            rows_first[item, 1 : rows + 1, at] = jnp.swapaxes(arrived[at, item], 0, 1)
        rows_first[item, 0] = before[:, item, 0]
        rows_first[item, rows + 1] = after[:, item, 0]
    pairs = []
    for x in range(count):
        dest = me ^ x
        start = (dest % blocks) * span
        pairs.append((rows_first.at[dest // blocks, pl.ds(start, span + 2)], parts[x]))
    finished(started(sems, 1, pairs))


def row_parts(me, before, value, after, count):
    width, items, rows, columns = value.shape
    span = rows * items // count
    return pl.pallas_call(
        functools.partial(rows_kernel, count),
        out_shape=[struct((span + 2, width, columns), BF16)] * count,
        in_specs=[IN_SMEM, IN_VMEM, IN_HBM, IN_VMEM],
        out_specs=[IN_HBM] * count,
        scratch_shapes=[
            pltpu.VMEM((width, items, rows, columns), BF16),
            pltpu.VMEM((items, rows + 2, width, columns), BF16),
            pltpu.SemaphoreType.DMA((1 + count,)),
        ],
        compiler_params=PARAMS,
        name="row_parts",
    )(me, before, value, after)


def weight_pieces(weight, me_dp, feats):
    size = lax.axis_size("chan")
    shares = min(lax.axis_size("dp"), weight.shape[3] // 128)
    share = weight.shape[3] // shares
    held = lax.dynamic_slice_in_dim(weight, me_dp % shares * share, share, 3).reshape(1, 9, -1, share)
    places = [(0, 0)]
    bit = size // 2
    while bit >= 4:
        held = jnp.concatenate([held, swapped(held, "chan", bit)], axis=0)
        places += [(chan ^ bit, dp) for chan, dp in places]
        bit //= 2
    pieces = [(held, places)]
    for x in range(1, min(size, 4)):
        pieces.append((swapped(held, "chan", x), [(chan ^ x, dp) for chan, dp in places]))
    waits = [feats[-1:], (), feats[-2:-1], (), feats[-3:-2], (), feats[-4:-3], ()]
    bit = shares // 2
    while bit:
        met = []
        for piece, places in pieces:
            got = swapped(once(piece, *(waits.pop(0) if waits else ())), "dp", bit)
            moved = [(chan, dp ^ bit) for chan, dp in places]
            if bit > 1:
                met.append((jnp.concatenate([piece, got], axis=0), places + moved))
            else:
                met += [(piece, places), (got, moved)]
        pieces = met
        bit //= 2
    return [piece for piece, _ in pieces], tuple(tuple(places) for _, places in pieces)


def tap_blocks(me, part, pieces, places, taps):
    share = pieces[0].shape[3]
    pairs = []
    for piece, blocks in zip(pieces, places):
        for index, (chan, dp) in enumerate(blocks):
            lanes = pl.ds(pl.multiple_of((part ^ dp) * share, share), share)
            pairs.append((piece.at[index], taps.at[:, me ^ chan, :, lanes]))
    return pairs


def transposed_kernel(places, me_ref, part_ref, *refs):
    pieces, (out, taps, turned, sems) = refs[:-4], refs[-4:]
    pairs = tap_blocks(me_ref[0], part_ref[0], pieces, places, taps)
    finished(started(sems, 0, pairs))
    channels = taps.shape[3]
    copies = []
    for tap in range(9):
        turned[8 - tap] = jnp.transpose(taps[tap].reshape(channels, channels))
        copies += started(sems, len(pairs) + tap, [(turned.at[8 - tap], out.at[8 - tap])])
    finished(copies)


def transposed_taps(me, part, pieces, places, channels):
    own = pieces[0].shape[2]
    blocks = sum(len(place) for place in places)
    return pl.pallas_call(
        functools.partial(transposed_kernel, places),
        out_shape=struct((9, channels, channels), BF16),
        in_specs=[IN_SMEM, IN_SMEM] + [IN_HBM] * len(pieces),
        out_specs=IN_HBM,
        scratch_shapes=[
            pltpu.VMEM((9, channels // own, own, channels), BF16),
            pltpu.VMEM((9, channels, channels), BF16),
            pltpu.SemaphoreType.DMA((blocks + 9,)),
        ],
        compiler_params=PARAMS,
        name="transposed_taps",
    )(me, part, *pieces)


def arrivals(me, parts, arrived):
    count = arrived.shape[0]
    width = parts[0].shape[1]
    return [
        (part, arrived.at[me ^ (index % count), :, pl.ds(index // count * width, width)])
        for index, part in enumerate(parts)
    ]


def departures(me, results, outs):
    count = results.shape[1]
    width = outs[0].shape[1]
    return [
        (results.at[:, me ^ (index % count), pl.ds(index // count * width, width)], out)
        for index, out in enumerate(outs)
    ]


def fill_shifted(arrived, scales, shifted):
    count, rows, own, columns = arrived.shape

    def row_step(row, carry):
        column = lax.broadcasted_iota(jnp.int32, (own, columns), 1)
        for source in range(count):
            value = arrived[source, row].astype(F32)
            if scales is not None:
                value = (value * scales[source]).astype(BF16).astype(F32)
            before = jnp.where(column == 0, 0.0, pltpu.roll(value, 1, 1))
            after = jnp.where(column == columns - 1, 0.0, pltpu.roll(value, columns - 1, 1))
            shifted[row, 0, source] = before.astype(BF16)
            shifted[row, 1, source] = value.astype(BF16)
            shifted[row, 2, source] = after.astype(BF16)
        return carry

    lax.fori_loop(0, rows, row_step, 0)


def convolved(taps, shifted, row, channels, columns):
    total = None
    for i in range(3):
        for j in range(3):
            term = jnp.dot(
                taps[3 * i + j].reshape(channels, channels),
                shifted[row + i, j].reshape(channels, columns),
                preferred_element_type=F32,
            )
            total = term if total is None else total + term
    return total


def forward_kernel(count, places, me_ref, part_ref, scales, *refs):
    pieces, refs = refs[: len(places)], refs[len(places) :]
    parts, outs = refs[:count], refs[count:-6]
    arrived, shifted, taps, results, wide_scales, sems = refs[-6:]
    me = me_ref[0]
    rows, _, own, columns = results.shape
    arriving = started(sems, 0, arrivals(me, parts, arrived))
    tapping = started(sems, count, tap_blocks(me, part_ref[0], pieces, places, taps))
    wide_scales[...] = jnp.broadcast_to(scales[...], wide_scales.shape)
    finished(arriving)
    fill_shifted(arrived, wide_scales, shifted)
    finished(tapping)

    def row_step(row, carry):
        total = convolved(taps, shifted, row, count * own, columns)
        results[row] = total.astype(BF16).reshape(count, own, columns)
        return carry

    lax.fori_loop(0, rows, row_step, 0)
    finished(started(sems, 0, departures(me, results, outs)))


def conv_forward(me, part, pieces, places, scales, parts, split):
    count = len(parts)
    rows, own, columns = parts[0].shape
    blocks = sum(len(place) for place in places)
    outs = pl.pallas_call(
        functools.partial(forward_kernel, count, places),
        out_shape=[struct((rows - 2, own // split, columns), BF16)] * (count * split),
        in_specs=[IN_SMEM, IN_SMEM, IN_VMEM] + [IN_HBM] * (len(pieces) + count),
        out_specs=[IN_HBM] * (count * split),
        scratch_shapes=[
            pltpu.VMEM((count, rows, own, columns), BF16),
            pltpu.VMEM((rows, 3, count, own, columns), BF16),
            pltpu.VMEM((9, count, own, count * own), BF16),
            pltpu.VMEM((rows - 2, count, own, columns), BF16),
            pltpu.VMEM((count, own, columns), F32),
            pltpu.SemaphoreType.DMA((count * split + blocks,)),
        ],
        compiler_params=PARAMS,
        name="conv_forward",
    )(me, part, scales, *pieces, *parts)
    return [outs[h * count : (h + 1) * count] for h in range(split)]


def backward_kernel(count, split, me_ref, _, taps_ref, *refs):
    grads, refs = refs[: count * split], refs[count * split :]
    feats, outs, style_ref = refs[:count], refs[count : 2 * count], refs[2 * count]
    arrived, arrived_feats, shifted, taps, results, sems = refs[2 * count + 1 :]
    me = me_ref[0]
    rows, _, own, columns = results.shape
    arriving = started(sems, 0, arrivals(me, grads, arrived))
    tapping = started(
        sems,
        count * split,
        [(taps_ref, taps)] + arrivals(me, feats, arrived_feats),
    )
    finished(arriving)
    fill_shifted(arrived, None, shifted)
    finished(tapping)
    style_ref[...] = jnp.zeros_like(style_ref)

    def row_step(row, carry):
        total = convolved(taps, shifted, row, count * own, columns).reshape(count, own, columns)
        results[row] = total.astype(BF16)
        product = total * arrived_feats[:, row + 1].astype(F32)
        style_ref[...] += jnp.sum(product, axis=2, keepdims=True)
        return carry

    lax.fori_loop(0, rows, row_step, 0)
    finished(started(sems, 0, departures(me, results, outs)))


def conv_backward(me, earlier, taps, grads, feats):
    count = len(feats)
    split = len(grads) // count
    rows, own, columns = feats[0].shape
    channels = count * own
    outs = pl.pallas_call(
        functools.partial(backward_kernel, count, split),
        out_shape=[struct((rows - 2, own, columns), BF16)] * count + [struct((count, own, 1), F32)],
        in_specs=[IN_SMEM] + [IN_HBM] * (2 + len(grads) + count),
        out_specs=[IN_HBM] * count + [IN_VMEM],
        scratch_shapes=[
            pltpu.VMEM((count, rows, own, columns), BF16),
            pltpu.VMEM((count, rows, own, columns), BF16),
            pltpu.VMEM((rows, 3, count, own, columns), BF16),
            pltpu.VMEM((9, channels, channels), BF16),
            pltpu.VMEM((rows - 2, count, own, columns), BF16),
            pltpu.SemaphoreType.DMA((len(grads) + count + 1,)),
        ],
        compiler_params=PARAMS,
        name="conv_backward",
    )(me, earlier, taps, *grads, *feats)
    return outs[:-1], outs[-1]


def weight_kernel(count, split, me_ref, core_ref, scales, *refs):
    grads, refs = refs[: count * split], refs[count * split :]
    feats, (keep, send) = refs[:count], refs[count : count + 2]
    arrived, arrived_feats, shifted, rows_ref, results, wide_scales, sems = refs[count + 2 :]
    me, core = me_ref[0], core_ref[0]
    rows, _, own, columns = rows_ref.shape
    channels = count * own
    half = channels // 2
    arriving = started(sems, 0, arrivals(me, feats, arrived_feats))
    arriving_grads = started(sems, count, arrivals(me, grads, arrived))
    wide_scales[...] = jnp.broadcast_to(scales[...], wide_scales.shape)
    finished(arriving)
    fill_shifted(arrived_feats, wide_scales, shifted)
    finished(arriving_grads)
    for source in range(count):
        rows_ref[:, source] = arrived[source, 1 : rows + 1]

    def leaving(tap):
        return [
            pltpu.make_async_copy(results.at[core, tap], keep.at[tap], sems.at[2 * tap]),
            pltpu.make_async_copy(results.at[1 - core, tap], send.at[tap], sems.at[2 * tap + 1]),
        ]

    def tap_step(tap, carry):
        i, j = lax.div(tap, 3), lax.rem(tap, 3)
        total = None
        for row in range(rows):
            term = lax.dot_general(
                rows_ref[row].reshape(channels, columns),
                shifted[row + i, j].reshape(channels, columns),
                (((1,), (1,)), ((), ())),
                preferred_element_type=F32,
            )
            total = term if total is None else total + term
        total = total.astype(BF16)
        results[0, tap], results[1, tap] = total[:, :half], total[:, half:]
        for copy in leaving(tap):
            copy.start()
        return carry

    lax.fori_loop(0, 9, tap_step, 0)
    for tap in range(9):
        finished(leaving(tap))


def conv_weight(me, core, scales, grads, feats):
    count = len(feats)
    split = len(grads) // count
    rows, own, columns = feats[0].shape
    channels = count * own
    return pl.pallas_call(
        functools.partial(weight_kernel, count, split),
        out_shape=[struct((9, channels, channels // 2), BF16)] * 2,
        in_specs=[IN_SMEM, IN_SMEM, IN_VMEM] + [IN_HBM] * (len(grads) + count),
        out_specs=[IN_HBM] * 2,
        scratch_shapes=[
            pltpu.VMEM((count, rows, own, columns), BF16),
            pltpu.VMEM((count, rows, own, columns), BF16),
            pltpu.VMEM((rows, 3, count, own, columns), BF16),
            pltpu.VMEM((rows - 2, count, own, columns), BF16),
            pltpu.VMEM((2, 9, channels, channels // 2), BF16),
            pltpu.VMEM((count, own, columns), F32),
            pltpu.SemaphoreType.DMA((max(18, len(grads) + count),)),
        ],
        compiler_params=PARAMS,
        name="conv_weight",
    )(me, core, scales, *grads, *feats)


def row_blocks(me, parts, rows_ref, start):
    count = len(parts)
    blocks = count // rows_ref.shape[0]
    span = parts[0].shape[0]
    pairs = []
    for x, part in enumerate(parts):
        source = me ^ x
        at = pl.ds(start + (source % blocks) * span, span)
        pairs.append((part, rows_ref.at[source // blocks, at]))
    return pairs


def rims_kernel(count, me_ref, *refs):
    parts, (first, last, arrived, sems) = refs[:count], refs[count:]
    rows = arrived.shape[1]
    finished(started(sems, 0, row_blocks(me_ref[0], parts, arrived, 0)))
    pairs = [
        (arrived.at[:, pl.ds(0, RIM)], first),
        (arrived.at[:, pl.ds(rows - RIM, RIM)], last),
    ]
    finished(started(sems, count, pairs))


def rims(me, parts, items):
    count = len(parts)
    span, width, columns = parts[0].shape
    rim = struct((items, RIM, width, columns), BF16)
    return pl.pallas_call(
        functools.partial(rims_kernel, count),
        out_shape=[rim, rim],
        in_specs=[IN_SMEM] + [IN_HBM] * count,
        out_specs=[IN_HBM] * 2,
        scratch_shapes=[
            pltpu.VMEM((items, span * count // items, width, columns), BF16),
            pltpu.SemaphoreType.DMA((count + 2,)),
        ],
        compiler_params=PARAMS,
        name="rims",
    )(me, *parts)


def sinc_kernel(count, first_channel, me_ref, edge_ref, demod, bias, up_sums, *refs):
    (before, after, cotangent), table_refs, parts = refs[:3], refs[3:7], refs[7 : 7 + count]
    refs = refs[7 + count + (first_channel > 0) :]
    (out, grad_bias, grad_demod), grad_parts = refs[:3], refs[3 : 3 + count]
    raw, cot, tables, out_rows, grad_raw = refs[3 + count : 8 + count]
    wide, wide_grad, narrow, narrow_grad, sems = refs[8 + count :]
    me = me_ref[0]
    items, extent, width, columns = raw.shape
    rows = extent - 2 * RIM
    first, last = edge_ref[0], edge_ref[1]
    tap = [float(value) for value in sinc_taps()[:6]]
    lane_tiles = 2 * columns // 128
    own_channels = pl.ds(first_channel, width)
    up_high, up_low, down_high, down_low = tables
    pairs = row_blocks(me, parts, raw, RIM) + list(zip(table_refs, tables))
    pairs += [
        (before, raw.at[:, pl.ds(0, RIM)]),
        (after, raw.at[:, pl.ds(RIM + rows, RIM)]),
        (cotangent.at[:, :, own_channels], cot),
    ]
    finished(started(sems, 0, pairs))

    def widened(values):
        flat = values.reshape(-1, columns)
        total = jnp.dot(flat, up_high[...], preferred_element_type=F32)
        total = total + jnp.dot(flat, up_low[...], preferred_element_type=F32)
        return total.reshape(-1, GROUP, 2 * columns)

    def narrowed(values):
        flat = values.reshape(-1, 2 * columns)
        high = flat.astype(BF16)
        low = (flat - high.astype(F32)).astype(BF16)
        total = jnp.dot(high, down_high[...], preferred_element_type=F32)
        total = total + jnp.dot(high, down_low[...], preferred_element_type=F32)
        total = total + jnp.dot(low, down_high[...], preferred_element_type=F32)
        return total.reshape(-1, GROUP, columns)

    def tile_step(index, carry):
        lanes = pl.ds(pl.multiple_of(lax.rem(index, lane_tiles) * 128, 128), 128)
        subs = pl.ds(pl.multiple_of(lax.div(index, lane_tiles) * 8, 8), 8)
        sums, picked = [{}, {}], [{}, {}]
        for row in range(extent):
            for which, ref in ((0, wide), (1, wide_grad)):
                value = ref[row, subs, lanes]
                products = [value * (2.0 * tap[t]) for t in range(6)]
                for offset in range(-3, 4):
                    pair = row - RIM + offset
                    for parity in range(2):
                        t = 2 * offset + parity + 5
                        if -4 <= pair < rows + 4 and 0 <= t < 12:
                            term = products[min(t, 11 - t)]
                            key = 2 * pair + parity
                            sums[which][key] = sums[which][key] + term if key in sums[which] else term
            pair = row - RIM - 3
            if pair < -4:
                continue
            for key in (2 * pair, 2 * pair + 1):
                value, grad = sums[0].pop(key), sums[1].pop(key)
                sigmoid = 1.0 / (1.0 + jnp.exp(-value))
                active = value * sigmoid
                grad = grad * (sigmoid + active * (1.0 - sigmoid))
                if pair < 0:
                    active, grad = active * first, grad * first
                if pair >= rows:
                    active, grad = active * last, grad * last
                picked[0][key], picked[1][key] = active, grad
            centre = pair - 3
            if centre >= -1:
                for which, ref in ((0, narrow), (1, narrow_grad)):
                    store = picked[which]
                    if which == 1 or 0 <= centre < rows:
                        total = None
                        for t in range(6):
                            term = tap[t] * (store[2 * centre + t - 5] + store[2 * centre + 6 - t])
                            total = term if total is None else total + term
                        ref[centre + which, subs, lanes] = total
                    for key in (2 * centre - 6, 2 * centre - 5, 2 * centre - 4):
                        store.pop(key, None)
        return carry

    leaving = []
    for item in range(items):
        for group in range(width // GROUP):
            at = slice(group * GROUP, (group + 1) * GROUP)
            scale = demod[item, at]
            shift = bias[at] * up_sums[...]
            spread = widened(raw[item, :, at]) * scale
            wide[:RIM] = spread[:RIM] + shift * first
            wide[RIM : RIM + rows] = spread[RIM : RIM + rows] + shift
            wide[RIM + rows :] = spread[RIM + rows :] + shift * last
            wide_grad[...] = widened(cot[item, :, at])
            lax.fori_loop(0, GROUP // 8 * lane_tiles, tile_step, 0)
            result = narrowed(narrow[...])
            out_rows[at, item] = jnp.swapaxes(result, 0, 1).astype(BF16)
            target = out.at[pl.ds(first_channel + group * GROUP, GROUP), item]
            source = out_rows.at[pl.ds(group * GROUP, GROUP), item]
            leaving += started(sems, len(leaving), [(source, target)])
            grad = narrowed(narrow_grad[...])
            scaled_grad = grad * scale
            grad_raw[item, 0, at] = (scaled_grad[0] * first).astype(BF16)
            grad_raw[item, 1 : rows + 1, at] = scaled_grad[1 : rows + 1].astype(BF16)
            grad_raw[item, rows + 1, at] = (scaled_grad[rows + 1] * last).astype(BF16)
            grad = grad[1 : rows + 1]
            own = raw[item, RIM : RIM + rows, at].astype(F32)
            grad_bias[item, at] = jnp.sum(jnp.sum(grad, axis=0), axis=1, keepdims=True)
            grad_demod[item, at] = jnp.sum(jnp.sum(grad * own, axis=0), axis=1, keepdims=True)
    blocks = count // items
    span = rows // blocks
    pairs = []
    for x in range(count):
        dest = me ^ x
        pairs.append((grad_raw.at[dest // blocks, pl.ds((dest % blocks) * span, span + 2)], grad_parts[x]))
    finished(leaving + started(sems, len(leaving), pairs))


def sinc_both(me, edges, demod, bias, tables, up_sums, before, after, cotangent, parts, out, first_channel):
    count = len(parts)
    items, extent, own, columns = cotangent.shape
    span, width, _ = parts[0].shape
    rows = extent - 2 * RIM
    wide = pltpu.VMEM((extent, GROUP, 2 * columns), F32)
    outs = pl.pallas_call(
        functools.partial(sinc_kernel, count, first_channel),
        out_shape=[
            struct((own, items, rows, columns), BF16),
            struct((items, width, 1), F32),
            struct((items, width, 1), F32),
        ]
        + [struct((span + 2, width, columns), BF16)] * count,
        in_specs=[IN_SMEM, IN_SMEM] + [IN_VMEM] * 3 + [IN_HBM] * (7 + count + len(out)),
        out_specs=[IN_HBM, IN_VMEM, IN_VMEM] + [IN_HBM] * count,
        input_output_aliases={12 + count: 0} if out else {},
        scratch_shapes=[
            pltpu.VMEM((items, extent, width, columns), BF16),
            pltpu.VMEM((items, extent, width, columns), BF16),
            [pltpu.VMEM(table.shape, BF16) for table in tables],
            pltpu.VMEM((width, items, rows, columns), BF16),
            pltpu.VMEM((items, rows + 2, width, columns), BF16),
            wide,
            wide,
            pltpu.VMEM((rows, GROUP, 2 * columns), F32),
            pltpu.VMEM((rows + 2, GROUP, 2 * columns), F32),
            pltpu.SemaphoreType.DMA((count + max(7, items * width // GROUP),)),
        ],
        compiler_params=PARAMS,
        name="sinc_both",
    )(me, edges, demod, bias, up_sums, before, after, cotangent, *tables, *parts, *out)
    return outs[0], outs[1], outs[2], outs[3:]


def scale_kernel(count, me_ref, scales, *refs):
    parts, (out, arrived, results, sems) = refs[:count], refs[count:]
    width, items, _, _ = out.shape
    finished(started(sems, 0, row_blocks(me_ref[0], parts, arrived, 0)))
    leaving = []
    for item in range(items):
        for group in range(width // GROUP):
            at = slice(group * GROUP, (group + 1) * GROUP)
            value = arrived[item, :, at].astype(F32) * scales[item, at]
            results[at, item] = jnp.swapaxes(value, 0, 1)
            spot = pl.ds(group * GROUP, GROUP)
            leaving += started(sems, len(leaving), [(results.at[spot, item], out.at[spot, item])])
    finished(leaving)


def scaled(me, scales, parts, items):
    count = len(parts)
    span, width, columns = parts[0].shape
    rows = span * count // items
    return pl.pallas_call(
        functools.partial(scale_kernel, count),
        out_shape=struct((width, items, rows, columns), F32),
        in_specs=[IN_SMEM, IN_VMEM] + [IN_HBM] * count,
        out_specs=IN_HBM,
        scratch_shapes=[
            pltpu.VMEM((items, rows, width, columns), BF16),
            pltpu.VMEM((width, items, rows, columns), F32),
            pltpu.SemaphoreType.DMA((max(count, items * width // GROUP),)),
        ],
        compiler_params=PARAMS,
        name="scale_features",
    )(me, scales, *parts)


def summed_everywhere(value):
    for axis in ("dp", "chan"):
        size = lax.axis_size(axis)
        bit = 1
        while bit < size:
            value = value + lax.ppermute(value, axis, [(i, i ^ bit) for i in range(size)])
            bit *= 2
    return value


def per_device(
    features,
    latent,
    affine,
    affine_bias,
    weight,
    out_bias,
    cotangent,
    latents_all,
    labels,
    class_means,
):
    highest = lax.Precision.HIGHEST
    own, items, rows, columns = features.shape
    channels = weight.shape[3]
    count = lax.axis_size("chan")
    dp_total = lax.axis_size("dp")
    me = lax.axis_index("chan")
    me_dp = lax.axis_index("dp")
    me_ref = me.astype(jnp.int32)[None]
    blocks = count // items
    span = rows // blocks
    split = max(1, min(2, own // GROUP))
    width = own // split

    before, after = from_neighbours(features, "dp", 2, 1)
    prepared = row_parts(me_ref, before, features, after, count)
    feats = exchange(prepared, "chan")
    core = (me_dp % 2).astype(jnp.int32)[None]
    pieces, places = weight_pieces(weight, me_dp, feats)
    part = (me_dp % (channels // pieces[0].shape[3])).astype(jnp.int32)[None]

    styles = jnp.dot(latent, affine, preferred_element_type=F32) + affine_bias
    own_style = lax.dynamic_slice_in_dim(styles, me * own, own, 1)
    weight_full = weight.astype(F32)
    weight_sq = jnp.sum(weight_full * weight_full, axis=(0, 1))
    demod = lax.rsqrt(jnp.dot(styles * styles, weight_sq.T, precision=highest) + 1e-08)
    item = me // blocks
    item_scales = lax.dynamic_index_in_dim(styles, item, 0, keepdims=False).reshape(count, own, 1)

    cot_before, cot_after = from_neighbours(cotangent, "dp", 2, RIM)
    cot = jnp.transpose(jnp.concatenate([cot_before, cotangent, cot_after], axis=2), (1, 2, 0, 3))
    table = up_table(columns)
    tables = halves(table) + halves(0.5 * table.T)
    up_sums = np.sum(table, axis=0)[None]
    edges = jnp.stack([me_dp > 0, me_dp < dp_total - 1]).astype(F32)

    raw_parts = conv_forward(me_ref, part, pieces, places, item_scales, feats, split)
    taps_backward = transposed_taps(
        me_ref, part, [once(piece, raw_parts[0][0]) for piece in pieces], places, channels
    )
    output, grad_parts, bias_parts, demod_parts = [], [], [], []
    up = [(i, i + 1) for i in range(dp_total - 1)]
    down = [(j, i) for i, j in up]
    for h in range(split):
        at = slice(h * width, (h + 1) * width)
        arrived = exchange(raw_parts[h], "chan")
        head, tail = rims(me_ref, arrived, items)
        result, bias_part, demod_part, parts = sinc_both(
            me_ref,
            edges,
            demod[:, at, None],
            out_bias[at, None],
            tables,
            up_sums,
            lax.ppermute(tail, "dp", up),
            lax.ppermute(head, "dp", down),
            cot,
            arrived,
            output,
            h * width,
        )
        output = [result]
        bias_parts.append(bias_part)
        demod_parts.append(demod_part)
        grad_parts += exchange(parts, "chan")
    output = output[0]
    bias_part = jnp.sum(jnp.concatenate(bias_parts, axis=1)[:, :, 0], axis=0)
    g_demod = jnp.concatenate(demod_parts, axis=1)[:, :, 0]

    keep, send = conv_weight(me_ref, core, item_scales, grad_parts, feats)
    modded_parts, style_part = conv_backward(me_ref, keep, taps_backward, grad_parts, feats)
    modded_parts = exchange(modded_parts, "chan")
    grad_features = scaled(me_ref, own_style[:, :, None], modded_parts, items)

    grad_bias, g_demod_sum = lax.psum((bias_part, g_demod), "dp")
    cube = demod * demod * demod
    g_style_part = 2.0 * styles * jnp.dot(-0.5 * g_demod * cube, weight_sq, precision=highest)
    g_style_part = g_style_part + jnp.where(
        jnp.arange(items)[:, None] == item, style_part.reshape(1, channels), 0.0
    )
    g_wsq = jnp.dot((-0.5 * g_demod_sum * cube).T, styles * styles, precision=highest)

    lane = channels // 2
    bit = 1
    while True:
        got = lax.ppermute(send, "dp", [(i, i ^ bit) for i in range(dp_total)])
        g_weight = keep.astype(F32) + got.astype(F32)
        bit *= 2
        if bit >= dp_total:
            break
        lane //= 2
        side = (me_dp // bit) % 2
        keep = lax.dynamic_slice_in_dim(g_weight, side * lane, lane, 2).astype(BF16)
        send = lax.dynamic_slice_in_dim(g_weight, (1 - side) * lane, lane, 2).astype(BF16)
    g_weight = g_weight.astype(BF16)
    g_weight = once(g_weight, *modded_parts)
    sent = [lax.dynamic_slice_in_dim(g_weight, (me ^ x) * own, own, 1) for x in range(count)]
    g_weight = sum(part.astype(F32) for part in exchange(sent, "chan"))
    while bit > 1:
        bit //= 2
        got = lax.ppermute(g_weight, "dp", [(i, i ^ bit) for i in range(dp_total)])
        upper = (me_dp // bit) % 2 == 1
        g_weight = jnp.concatenate(
            [jnp.where(upper, got, g_weight), jnp.where(upper, g_weight, got)], axis=2
        )
    grad_weight = g_weight.reshape(weight.shape) + 2.0 * weight_full * g_wsq

    tags = jnp.stack([labels // 64, labels % 64], axis=1).astype(BF16)
    tagged = jnp.concatenate([once(latents_all, head), jnp.pad(tags, ((0, 0), (0, 126)))], axis=1)
    tagged = lax.all_gather(tagged, ("dp", "chan"), axis=0, tiled=True)
    all_latents, tags = tagged[:, :-128], tagged[:, -128:-126].astype(F32)
    all_labels = (tags[:, 0] * 64.0 + tags[:, 1]).astype(jnp.int32)
    one_hot = all_labels[None, :] == jnp.arange(class_means.shape[0])[:, None]
    class_sums = jnp.dot(one_hot.astype(BF16), all_latents, preferred_element_type=F32)
    counts = jnp.sum(one_hot.astype(F32), axis=1)
    target = jnp.where(
        counts[:, None] > 0, class_sums / jnp.maximum(counts, 1.0)[:, None], class_means
    )

    g_style = summed_everywhere(g_style_part)
    grad_affine_bias = jnp.sum(g_style, axis=0)
    grad_affine = jnp.dot(latent.astype(F32).T, g_style, precision=highest)
    grad_latent = jnp.dot(g_style, affine.astype(F32).T, precision=highest)
    return (
        output,
        grad_features,
        grad_latent,
        grad_affine,
        grad_affine_bias,
        grad_weight,
        grad_bias,
        target,
    )


def solution(mesh):
    in_specs = (
        P("chan", None, "dp", None),
        P(),
        P(),
        P(),
        P(None, None, "chan", None),
        P("chan"),
        P("chan", None, "dp", None),
        P(("dp", "chan"), None),
        P(("dp", "chan")),
        P(),
    )
    out_specs = (
        P("chan", None, "dp", None),
        P("chan", None, "dp", None),
        P(),
        P(),
        P(),
        P(None, None, "chan", None),
        P("chan"),
        P(),
    )
    return jax.shard_map(
        per_device, mesh=mesh, in_specs=in_specs, out_specs=out_specs, check_vma=False
    )
```

```python
import functools

import jax
import jax.numpy as jnp
import ml_dtypes
import numpy as np
from jax import lax
from jax.experimental import pallas as pl
from jax.experimental.pallas import tpu as pltpu
from jax.sharding import PartitionSpec as P

F32 = jnp.float32
BF16 = jnp.bfloat16
IN_VMEM = pl.BlockSpec(memory_space=pltpu.VMEM)
IN_HBM = pl.BlockSpec(memory_space=pltpu.HBM)
IN_SMEM = pl.BlockSpec(memory_space=pltpu.SMEM)
PARAMS = pltpu.CompilerParams(vmem_limit_bytes=60 << 20)
RIM = 7
GROUP = 16


def struct(shape, dtype):
    return jax.ShapeDtypeStruct(shape, dtype)


def sinc_taps():
    offset = np.arange(12) - 5.5
    values = np.sinc(offset * 0.5) * (0.5 + 0.5 * np.cos(np.pi * offset / 6.0))
    return values / values.sum()


def up_table(size):
    tap = np.arange(2 * size)[None, :] - 2 * np.arange(size)[:, None] + 5
    held = (tap >= 0) & (tap < 12)
    return np.where(held, 2.0 * sinc_taps()[np.clip(tap, 0, 11)], 0.0).astype(np.float32)


def halves(table):
    high = table.astype(ml_dtypes.bfloat16)
    return high, (table - high.astype(np.float32)).astype(ml_dtypes.bfloat16)


def from_neighbours(value, axis, dim, width):
    size, length = lax.axis_size(axis), value.shape[dim]
    up = [(i, i + 1) for i in range(size - 1)]
    down = [(j, i) for i, j in up]
    last = lax.slice_in_dim(value, length - width, length, axis=dim)
    first = lax.slice_in_dim(value, 0, width, axis=dim)
    return lax.ppermute(last, axis, up), lax.ppermute(first, axis, down)


def swapped(value, axis, bits):
    return lax.ppermute(value, axis, [(i, i ^ bits) for i in range(lax.axis_size(axis))])


def once(value, *others):
    return lax.optimization_barrier((value,) + others)[0]


def order(count, halved=False):
    return list(range(count)) if halved else [0] + list(range(4, count)) + list(range(1, min(4, count)))


def exchange(parts, axis, halved=False):
    steps = order(lax.axis_size(axis), halved)
    return [parts[0]] + [swapped(part, axis, x) for part, x in zip(parts[1:], steps[1:])]


def started(sems, first, pairs):
    copies = [
        pltpu.make_async_copy(source, target, sems.at[first + index])
        for index, (source, target) in enumerate(pairs)
    ]
    for copy in copies:
        copy.start()
    return copies


def finished(copies):
    for copy in copies:
        copy.wait()


def rows_kernel(count, me_ref, before, value, after, *refs):
    parts, (arrived, rows_first, sems) = refs[:count], refs[count:]
    me = me_ref[0]
    width, items, rows, _ = value.shape
    blocks = count // items
    span = rows // blocks
    finished(started(sems, 0, [(value, arrived)]))
    for item in range(items):
        for group in range(width // GROUP):
            at = slice(group * GROUP, (group + 1) * GROUP)
            rows_first[item, 1 : rows + 1, at] = jnp.swapaxes(arrived[at, item], 0, 1)
        rows_first[item, 0] = before[:, item, 0]
        rows_first[item, rows + 1] = after[:, item, 0]
    pairs = []
    for x, part in zip(order(count), parts):
        dest = me ^ x
        start = (dest % blocks) * span
        pairs.append((rows_first.at[dest // blocks, pl.ds(start, span + 2)], part))
    finished(started(sems, 1, pairs))


def row_parts(me, before, value, after, count):
    width, items, rows, columns = value.shape
    span = rows * items // count
    return pl.pallas_call(
        functools.partial(rows_kernel, count),
        out_shape=[struct((span + 2, width, columns), BF16)] * count,
        in_specs=[IN_SMEM, IN_VMEM, IN_HBM, IN_VMEM],
        out_specs=[IN_HBM] * count,
        scratch_shapes=[
            pltpu.VMEM((width, items, rows, columns), BF16),
            pltpu.VMEM((items, rows + 2, width, columns), BF16),
            pltpu.SemaphoreType.DMA((1 + count,)),
        ],
        compiler_params=PARAMS,
        name="row_parts",
    )(me, before, value, after)


def weight_pieces(weight, me_dp, feats):
    size = lax.axis_size("chan")
    shares = min(lax.axis_size("dp"), weight.shape[3] // 128)
    share = weight.shape[3] // shares
    held = lax.dynamic_slice_in_dim(weight, me_dp % shares * share, share, 3).reshape(1, 9, -1, share)
    places = [(0, 0)]
    bit = size // 2
    while bit >= 4:
        held = jnp.concatenate([held, swapped(held, "chan", bit)], axis=0)
        places += [(chan ^ bit, dp) for chan, dp in places]
        bit //= 2
    pieces = [(held, places)]
    for x in range(1, min(size, 4)):
        pieces.append((swapped(held, "chan", x), [(chan ^ x, dp) for chan, dp in places]))
    waits = [feats[1:2], (), feats[2:3], (), feats[3:4], (), feats[4:5], ()]
    bit = shares // 2
    while bit:
        met = []
        for piece, places in pieces:
            got = swapped(once(piece, *(waits.pop(0) if waits else ())), "dp", bit)
            moved = [(chan, dp ^ bit) for chan, dp in places]
            if bit > 1:
                met.append((jnp.concatenate([piece, got], axis=0), places + moved))
            else:
                met += [(piece, places), (got, moved)]
        pieces = met
        bit //= 2
    return [piece for piece, _ in pieces], tuple(tuple(places) for _, places in pieces)


def tap_blocks(me, part, pieces, places, taps):
    share = pieces[0].shape[3]
    pairs = []
    for piece, blocks in zip(pieces, places):
        for index, (chan, dp) in enumerate(blocks):
            lanes = pl.ds(pl.multiple_of((part ^ dp) * share, share), share)
            pairs.append((piece.at[index], taps.at[:, me ^ chan, :, lanes]))
    return pairs


def transposed_kernel(places, me_ref, part_ref, *refs):
    pieces, (out, taps, turned, sems) = refs[:-4], refs[-4:]
    pairs = tap_blocks(me_ref[0], part_ref[0], pieces, places, taps)
    finished(started(sems, 0, pairs))
    channels = taps.shape[3]
    copies = []
    for tap in range(9):
        turned[8 - tap] = jnp.transpose(taps[tap].reshape(channels, channels))
        copies += started(sems, len(pairs) + tap, [(turned.at[8 - tap], out.at[8 - tap])])
    finished(copies)


def transposed_taps(me, part, pieces, places, channels):
    own = pieces[0].shape[2]
    blocks = sum(len(place) for place in places)
    return pl.pallas_call(
        functools.partial(transposed_kernel, places),
        out_shape=struct((9, channels, channels), BF16),
        in_specs=[IN_SMEM, IN_SMEM] + [IN_HBM] * len(pieces),
        out_specs=IN_HBM,
        scratch_shapes=[
            pltpu.VMEM((9, channels // own, own, channels), BF16),
            pltpu.VMEM((9, channels, channels), BF16),
            pltpu.SemaphoreType.DMA((blocks + 9,)),
        ],
        compiler_params=PARAMS,
        name="transposed_taps",
    )(me, part, *pieces)


def arrivals(me, parts, arrived):
    count, _, own, _ = arrived.shape
    width = parts[0].shape[1]
    steps = order(count, width < own)
    return [
        (part, arrived.at[me ^ steps[index % count], :, pl.ds(index // count * width, width)])
        for index, part in enumerate(parts)
    ]


def departures(me, results, outs):
    _, count, own, _ = results.shape
    width = outs[0].shape[1]
    steps = order(count, width < own)
    return [
        (results.at[:, me ^ steps[index % count], pl.ds(index // count * width, width)], out)
        for index, out in enumerate(outs)
    ]


def fill_shifted(arrived, scales, shifted):
    count, rows, own, columns = arrived.shape

    def row_step(row, carry):
        column = lax.broadcasted_iota(jnp.int32, (own, columns), 1)
        for source in range(count):
            value = arrived[source, row].astype(F32)
            if scales is not None:
                value = (value * scales[source]).astype(BF16).astype(F32)
            before = jnp.where(column == 0, 0.0, pltpu.roll(value, 1, 1))
            after = jnp.where(column == columns - 1, 0.0, pltpu.roll(value, columns - 1, 1))
            shifted[row, 0, source] = before.astype(BF16)
            shifted[row, 1, source] = value.astype(BF16)
            shifted[row, 2, source] = after.astype(BF16)
        return carry

    lax.fori_loop(0, rows, row_step, 0)


def convolved(taps, shifted, row, channels, columns):
    total = None
    for i in range(3):
        for j in range(3):
            term = jnp.dot(
                taps[3 * i + j].reshape(channels, channels),
                shifted[row + i, j].reshape(channels, columns),
                preferred_element_type=F32,
            )
            total = term if total is None else total + term
    return total


def forward_kernel(count, places, me_ref, part_ref, scales, *refs):
    pieces, refs = refs[: len(places)], refs[len(places) :]
    parts, outs = refs[:count], refs[count:-6]
    arrived, shifted, taps, results, wide_scales, sems = refs[-6:]
    me = me_ref[0]
    rows, _, own, columns = results.shape
    arriving = started(sems, 0, arrivals(me, parts, arrived))
    tapping = started(sems, count, tap_blocks(me, part_ref[0], pieces, places, taps))
    wide_scales[...] = jnp.broadcast_to(scales[...], wide_scales.shape)
    finished(arriving)
    fill_shifted(arrived, wide_scales, shifted)
    finished(tapping)

    def row_step(row, carry):
        total = convolved(taps, shifted, row, count * own, columns)
        results[row] = total.astype(BF16).reshape(count, own, columns)
        return carry

    lax.fori_loop(0, rows, row_step, 0)
    finished(started(sems, 0, departures(me, results, outs)))


def conv_forward(me, part, pieces, places, scales, parts):
    count = len(parts)
    rows, own, columns = parts[0].shape
    blocks = sum(len(place) for place in places)
    return pl.pallas_call(
        functools.partial(forward_kernel, count, places),
        out_shape=[struct((rows - 2, own, columns), BF16)] * count,
        in_specs=[IN_SMEM, IN_SMEM, IN_VMEM] + [IN_HBM] * (len(pieces) + count),
        out_specs=[IN_HBM] * count,
        scratch_shapes=[
            pltpu.VMEM((count, rows, own, columns), BF16),
            pltpu.VMEM((rows, 3, count, own, columns), BF16),
            pltpu.VMEM((9, count, own, count * own), BF16),
            pltpu.VMEM((rows - 2, count, own, columns), BF16),
            pltpu.VMEM((count, own, columns), F32),
            pltpu.SemaphoreType.DMA((count + blocks,)),
        ],
        compiler_params=PARAMS,
        name="conv_forward",
    )(me, part, scales, *pieces, *parts)


def backward_kernel(count, split, me_ref, scales, taps_ref, *refs):
    grads, refs = refs[: count * split], refs[count * split :]
    feats, outs, (style_ref, weight_out) = refs[:count], refs[count : 2 * count], refs[2 * count : 2 * count + 2]
    arrived, arrived_feats, shifted, modded, taps, results, weight_sums, wide_scales, sems = refs[2 * count + 2 :]
    me = me_ref[0]
    rows, _, own, columns = results.shape
    channels = count * own
    shares, _, _, share = weight_sums.shape
    arriving = started(sems, 0, arrivals(me, grads, arrived))
    tapping = started(
        sems,
        count * split,
        [(taps_ref, taps)] + arrivals(me, feats, arrived_feats),
    )
    wide_scales[...] = jnp.broadcast_to(scales[...], wide_scales.shape)
    finished(arriving)
    fill_shifted(arrived, None, shifted)
    finished(tapping)
    style_ref[...] = jnp.zeros_like(style_ref)

    def row_step(row, carry):
        total = convolved(taps, shifted, row, channels, columns).reshape(count, own, columns)
        results[row] = total.astype(BF16)
        product = total * arrived_feats[:, row + 1].astype(F32)
        style_ref[...] += jnp.sum(product, axis=2, keepdims=True)
        return carry

    lax.fori_loop(0, rows, row_step, 0)
    leaving = started(sems, 0, departures(me, results, outs))

    def modded_step(row, carry):
        for source in range(count):
            value = arrived_feats[source, row].astype(F32) * wide_scales[source]
            modded[row, source] = value.astype(BF16)
        return carry

    lax.fori_loop(0, rows + 2, modded_step, 0)

    def weight_leaving(tap):
        return pltpu.make_async_copy(weight_sums.at[:, tap], weight_out.at[:, tap], sems.at[count + tap])

    def tap_step(tap, carry):
        i, j = lax.div(tap, 3), lax.rem(tap, 3)
        total = None
        for row in range(rows):
            term = lax.dot_general(
                shifted[row + 1, 2 - j].reshape(channels, columns),
                modded[row + i].reshape(channels, columns),
                (((1,), (1,)), ((), ())),
                preferred_element_type=F32,
            )
            total = term if total is None else total + term
        total = total.astype(BF16)
        for index in range(shares):
            weight_sums[index, tap] = total[:, index * share : (index + 1) * share]
        weight_leaving(tap).start()
        return carry

    lax.fori_loop(0, 9, tap_step, 0)
    finished(leaving + [weight_leaving(tap) for tap in range(9)])


def conv_backward(me, scales, taps, grads, feats, shares):
    count = len(feats)
    split = len(grads) // count
    rows, own, columns = feats[0].shape
    channels = count * own
    share = channels // shares
    outs = pl.pallas_call(
        functools.partial(backward_kernel, count, split),
        out_shape=[struct((rows - 2, own, columns), BF16)] * count
        + [struct((count, own, 1), F32), struct((shares, 9, channels, share), BF16)],
        in_specs=[IN_SMEM, IN_VMEM] + [IN_HBM] * (1 + len(grads) + count),
        out_specs=[IN_HBM] * count + [IN_VMEM, IN_HBM],
        scratch_shapes=[
            pltpu.VMEM((count, rows, own, columns), BF16),
            pltpu.VMEM((count, rows, own, columns), BF16),
            pltpu.VMEM((rows, 3, count, own, columns), BF16),
            pltpu.VMEM((rows, count, own, columns), BF16),
            pltpu.VMEM((9, channels, channels), BF16),
            pltpu.VMEM((rows - 2, count, own, columns), BF16),
            pltpu.VMEM((shares, 9, channels, share), BF16),
            pltpu.VMEM((count, own, columns), F32),
            pltpu.SemaphoreType.DMA((count + max(9, len(grads) + 1),)),
        ],
        compiler_params=PARAMS,
        name="conv_backward",
    )(me, scales, taps, *grads, *feats)
    return outs[:-2], outs[-2], outs[-1]


def finish_kernel(shares, part_ref, weight, factors, *refs):
    pieces, (out, arrived, sems) = refs[:shares], refs[shares:]
    part = part_ref[0]
    share = pieces[0].shape[1]
    taps, own, _ = out.shape
    pairs = []
    for x, piece in enumerate(pieces):
        lanes = pl.ds(pl.multiple_of((part ^ x) * share, share), share)
        pairs.append((piece.at[pl.ds(0, taps * own)], arrived.at[:, lanes]))
    finished(started(sems, 0, pairs))
    twice = 2.0 * factors[...]
    for tap in range(taps):
        out[tap] = arrived[tap * own : (tap + 1) * own].astype(F32) + twice * weight[tap].astype(F32)


def finished_weight(part, weight, factors, pieces):
    _, own, channels = weight.shape
    shares = len(pieces)
    return pl.pallas_call(
        functools.partial(finish_kernel, shares),
        out_shape=struct((9, own, channels), F32),
        in_specs=[IN_SMEM, IN_VMEM, IN_VMEM] + [IN_HBM] * shares,
        out_specs=IN_VMEM,
        scratch_shapes=[
            pltpu.VMEM((9 * own, channels), BF16),
            pltpu.SemaphoreType.DMA((shares,)),
        ],
        compiler_params=PARAMS,
        name="finished_weight",
    )(part, weight, factors, *pieces)


def row_blocks(me, parts, rows_ref, start, first_channel=0):
    count = len(parts)
    blocks = count // rows_ref.shape[0]
    span = parts[0].shape[0]
    pairs = []
    channels = pl.ds(first_channel, rows_ref.shape[2])
    for x, part in zip(order(count), parts):
        source = me ^ x
        at = pl.ds(start + (source % blocks) * span, span)
        pairs.append((part.at[:, channels], rows_ref.at[source // blocks, at]))
    return pairs


def rims_kernel(count, me_ref, *refs):
    parts, (first, last, arrived, sems) = refs[:count], refs[-4:]
    rows = arrived.shape[1]
    finished(started(sems, 0, row_blocks(me_ref[0], parts, arrived, 0)))
    pairs = [
        (arrived.at[:, pl.ds(0, RIM)], first),
        (arrived.at[:, pl.ds(rows - RIM, RIM)], last),
    ]
    finished(started(sems, count, pairs))


def rims(me, parts, items, earlier):
    count = len(parts)
    span, width, columns = parts[0].shape
    rim = struct((items, RIM, width, columns), BF16)
    return pl.pallas_call(
        functools.partial(rims_kernel, count),
        out_shape=[rim, rim],
        in_specs=[IN_SMEM] + [IN_HBM] * (count + len(earlier)),
        out_specs=[IN_HBM] * 2,
        scratch_shapes=[
            pltpu.VMEM((items, span * count // items, width, columns), BF16),
            pltpu.SemaphoreType.DMA((count + 2,)),
        ],
        compiler_params=PARAMS,
        name="rims",
    )(me, *parts, *earlier)


def sinc_kernel(count, first_channel, me_ref, edge_ref, demod, bias, up_sums, *refs):
    (before, after, cotangent), table_refs, parts = refs[:3], refs[3:7], refs[7 : 7 + count]
    refs = refs[7 + count + (first_channel > 0) :]
    (out, grad_bias, grad_demod), grad_parts = refs[:3], refs[3 : 3 + count]
    raw, cot, tables, out_rows, grad_raw = refs[3 + count : 8 + count]
    wide, wide_grad, narrow, narrow_grad, sems = refs[8 + count :]
    me = me_ref[0]
    items, extent, width, columns = raw.shape
    rows = extent - 2 * RIM
    first, last = edge_ref[0], edge_ref[1]
    tap = [float(value) for value in sinc_taps()[:6]]
    lane_tiles = 2 * columns // 128
    own_channels = pl.ds(first_channel, width)
    up_high, up_low, down_high, down_low = tables
    pairs = row_blocks(me, parts, raw, RIM, first_channel) + list(zip(table_refs, tables))
    pairs += [
        (before.at[:, :, own_channels], raw.at[:, pl.ds(0, RIM)]),
        (after.at[:, :, own_channels], raw.at[:, pl.ds(RIM + rows, RIM)]),
        (cotangent.at[:, :, own_channels], cot),
    ]
    finished(started(sems, 0, pairs))

    def widened(values):
        flat = values.reshape(-1, columns)
        total = jnp.dot(flat, up_high[...], preferred_element_type=F32)
        total = total + jnp.dot(flat, up_low[...], preferred_element_type=F32)
        return total.reshape(-1, GROUP, 2 * columns)

    def narrowed(values):
        flat = values.reshape(-1, 2 * columns)
        high = flat.astype(BF16)
        low = (flat - high.astype(F32)).astype(BF16)
        total = jnp.dot(high, down_high[...], preferred_element_type=F32)
        total = total + jnp.dot(high, down_low[...], preferred_element_type=F32)
        total = total + jnp.dot(low, down_high[...], preferred_element_type=F32)
        return total.reshape(-1, GROUP, columns)

    def tile_step(index, carry):
        lanes = pl.ds(pl.multiple_of(lax.rem(index, lane_tiles) * 128, 128), 128)
        subs = pl.ds(pl.multiple_of(lax.div(index, lane_tiles) * 8, 8), 8)
        sums, picked = [{}, {}], [{}, {}]
        for row in range(extent):
            for which, ref in ((0, wide), (1, wide_grad)):
                value = ref[row, subs, lanes]
                products = [value * (2.0 * tap[t]) for t in range(6)]
                for offset in range(-3, 4):
                    pair = row - RIM + offset
                    for parity in range(2):
                        t = 2 * offset + parity + 5
                        if -4 <= pair < rows + 4 and 0 <= t < 12:
                            term = products[min(t, 11 - t)]
                            key = 2 * pair + parity
                            sums[which][key] = sums[which][key] + term if key in sums[which] else term
            pair = row - RIM - 3
            if pair < -4:
                continue
            for key in (2 * pair, 2 * pair + 1):
                value, grad = sums[0].pop(key), sums[1].pop(key)
                sigmoid = 0.5 + 0.5 * jnp.tanh(0.5 * value)
                active = value * sigmoid
                grad = grad * (sigmoid + active * (1.0 - sigmoid))
                if pair < 0:
                    active, grad = active * first, grad * first
                if pair >= rows:
                    active, grad = active * last, grad * last
                picked[0][key], picked[1][key] = active, grad
            centre = pair - 3
            if centre >= -1:
                for which, ref in ((0, narrow), (1, narrow_grad)):
                    store = picked[which]
                    if which == 1 or 0 <= centre < rows:
                        total = None
                        for t in range(6):
                            term = tap[t] * (store[2 * centre + t - 5] + store[2 * centre + 6 - t])
                            total = term if total is None else total + term
                        ref[centre + which, subs, lanes] = total
                    for key in (2 * centre - 6, 2 * centre - 5, 2 * centre - 4):
                        store.pop(key, None)
        return carry

    leaving = []
    for item in range(items):
        for group in range(width // GROUP):
            at = slice(group * GROUP, (group + 1) * GROUP)
            scale = demod[item, at]
            shift = bias[at] * up_sums[...]
            spread = widened(raw[item, :, at]) * scale
            wide[:RIM] = spread[:RIM] + shift * first
            wide[RIM : RIM + rows] = spread[RIM : RIM + rows] + shift
            wide[RIM + rows :] = spread[RIM + rows :] + shift * last
            wide_grad[...] = widened(cot[item, :, at])
            lax.fori_loop(0, GROUP // 8 * lane_tiles, tile_step, 0)
            result = narrowed(narrow[...])
            out_rows[at, item] = jnp.swapaxes(result, 0, 1).astype(BF16)
            target = out.at[pl.ds(first_channel + group * GROUP, GROUP), item]
            source = out_rows.at[pl.ds(group * GROUP, GROUP), item]
            leaving += started(sems, len(leaving), [(source, target)])
            grad = narrowed(narrow_grad[...])
            scaled_grad = grad * scale
            grad_raw[item, 0, at] = (scaled_grad[0] * first).astype(BF16)
            grad_raw[item, 1 : rows + 1, at] = scaled_grad[1 : rows + 1].astype(BF16)
            grad_raw[item, rows + 1, at] = (scaled_grad[rows + 1] * last).astype(BF16)
            grad = grad[1 : rows + 1]
            own = raw[item, RIM : RIM + rows, at].astype(F32)
            grad_bias[item, at] = jnp.sum(jnp.sum(grad, axis=0), axis=1, keepdims=True)
            grad_demod[item, at] = jnp.sum(jnp.sum(grad * own, axis=0), axis=1, keepdims=True)
    blocks = count // items
    span = rows // blocks
    pairs = []
    for x, part in zip(order(count, width < cotangent.shape[2]), grad_parts):
        dest = me ^ x
        pairs.append((grad_raw.at[dest // blocks, pl.ds((dest % blocks) * span, span + 2)], part))
    finished(leaving + started(sems, len(leaving), pairs))


def sinc_both(me, edges, demod, bias, tables, up_sums, before, after, cotangent, parts, out, first_channel):
    count = len(parts)
    items, extent, own, columns = cotangent.shape
    span, width = parts[0].shape[0], demod.shape[1]
    rows = extent - 2 * RIM
    wide = pltpu.VMEM((extent, GROUP, 2 * columns), F32)
    outs = pl.pallas_call(
        functools.partial(sinc_kernel, count, first_channel),
        out_shape=[
            struct((own, items, rows, columns), BF16),
            struct((items, width, 1), F32),
            struct((items, width, 1), F32),
        ]
        + [struct((span + 2, width, columns), BF16)] * count,
        in_specs=[IN_SMEM, IN_SMEM] + [IN_VMEM] * 3 + [IN_HBM] * (7 + count + len(out)),
        out_specs=[IN_HBM, IN_VMEM, IN_VMEM] + [IN_HBM] * count,
        input_output_aliases={12 + count: 0} if out else {},
        scratch_shapes=[
            pltpu.VMEM((items, extent, width, columns), BF16),
            pltpu.VMEM((items, extent, width, columns), BF16),
            [pltpu.VMEM(table.shape, BF16) for table in tables],
            pltpu.VMEM((width, items, rows, columns), BF16),
            pltpu.VMEM((items, rows + 2, width, columns), BF16),
            wide,
            wide,
            pltpu.VMEM((rows, GROUP, 2 * columns), F32),
            pltpu.VMEM((rows + 2, GROUP, 2 * columns), F32),
            pltpu.SemaphoreType.DMA((count + max(7, items * width // GROUP),)),
        ],
        compiler_params=PARAMS,
        name="sinc_both",
    )(me, edges, demod, bias, up_sums, before, after, cotangent, *tables, *parts, *out)
    return outs[0], outs[1], outs[2], outs[3:]


def scale_kernel(count, me_ref, scales, *refs):
    parts, (out, arrived, results, sems) = refs[:count], refs[count:]
    width, items, _, _ = out.shape
    finished(started(sems, 0, row_blocks(me_ref[0], parts, arrived, 0)))
    leaving = []
    for item in range(items):
        for group in range(width // GROUP):
            at = slice(group * GROUP, (group + 1) * GROUP)
            value = arrived[item, :, at].astype(F32) * scales[item, at]
            results[at, item] = jnp.swapaxes(value, 0, 1)
            spot = pl.ds(group * GROUP, GROUP)
            leaving += started(sems, len(leaving), [(results.at[spot, item], out.at[spot, item])])
    finished(leaving)


def scaled(me, scales, parts, items):
    count = len(parts)
    span, width, columns = parts[0].shape
    rows = span * count // items
    return pl.pallas_call(
        functools.partial(scale_kernel, count),
        out_shape=struct((width, items, rows, columns), F32),
        in_specs=[IN_SMEM, IN_VMEM] + [IN_HBM] * count,
        out_specs=IN_HBM,
        scratch_shapes=[
            pltpu.VMEM((items, rows, width, columns), BF16),
            pltpu.VMEM((width, items, rows, columns), F32),
            pltpu.SemaphoreType.DMA((max(count, items * width // GROUP),)),
        ],
        compiler_params=PARAMS,
        name="scale_features",
    )(me, scales, *parts)


def in_thirds(value, lanes):
    terms = []
    for _ in range(3):
        terms.append(lax.reduce_precision(value, 8, 7))
        value = value - terms[-1]
    rows = jnp.stack(terms).astype(BF16).reshape(-1, lanes)
    return jnp.pad(rows, ((0, -rows.shape[0] % 16), (0, 0)))


def from_thirds(rows, shape):
    terms = rows.astype(F32).reshape(-1)[: 3 * shape[0] * shape[1]].reshape((3,) + shape)
    return terms[0] + terms[1] + terms[2]


def tree_sum(values):
    while len(values) > 1:
        values = [a + b for a, b in zip(values[::2], values[1::2])]
    return values[0]


def per_device(
    features,
    latent,
    affine,
    affine_bias,
    weight,
    out_bias,
    cotangent,
    latents_all,
    labels,
    class_means,
):
    highest = lax.Precision.HIGHEST
    own, items, rows, columns = features.shape
    channels = weight.shape[3]
    count = lax.axis_size("chan")
    dp_total = lax.axis_size("dp")
    me = lax.axis_index("chan")
    me_dp = lax.axis_index("dp")
    me_ref = me.astype(jnp.int32)[None]
    blocks = count // items
    span = rows // blocks
    split = max(1, min(2, own // GROUP))
    width = own // split

    before, after = from_neighbours(features, "dp", 2, 1)
    prepared = row_parts(me_ref, before, features, after, count)
    feats = exchange(prepared, "chan")
    pieces, places = weight_pieces(weight, me_dp, feats)
    part = (me_dp % (channels // pieces[0].shape[3])).astype(jnp.int32)[None]

    styles = jnp.dot(latent, affine, preferred_element_type=F32) + affine_bias
    own_style = lax.dynamic_slice_in_dim(styles, me * own, own, 1)
    weight_full = weight.astype(F32)
    weight_sq = jnp.sum(weight_full * weight_full, axis=(0, 1))
    demod = lax.rsqrt(jnp.dot(styles * styles, weight_sq.T, precision=highest) + 1e-08)
    item = me // blocks
    item_scales = lax.dynamic_index_in_dim(styles, item, 0, keepdims=False).reshape(count, own, 1)

    cot_before, cot_after = from_neighbours(cotangent, "dp", 2, RIM)
    cot = jnp.transpose(jnp.concatenate([cot_before, cotangent, cot_after], axis=2), (1, 2, 0, 3))
    table = up_table(columns)
    tables = halves(table) + halves(0.5 * table.T)
    up_sums = np.sum(table, axis=0)[None]
    edges = jnp.stack([me_dp > 0, me_dp < dp_total - 1]).astype(F32)

    raw_parts = conv_forward(me_ref, part, pieces, places, item_scales, feats)
    taps_backward = transposed_taps(
        me_ref, part, [once(piece, raw_parts[0]) for piece in pieces], places, channels
    )
    output, grad_parts, bias_parts, demod_parts = [], [], [], []
    up = [(i, i + 1) for i in range(dp_total - 1)]
    down = [(j, i) for i, j in up]
    arrived = exchange(raw_parts, "chan")
    head, tail = rims(me_ref, arrived, items, [taps_backward, cot])
    before, after = lax.ppermute(tail, "dp", up), lax.ppermute(head, "dp", down)
    for h in range(split):
        at = slice(h * width, (h + 1) * width)
        result, bias_part, demod_part, parts = sinc_both(
            me_ref,
            edges,
            demod[:, at, None],
            out_bias[at, None],
            tables,
            up_sums,
            before,
            after,
            cot,
            arrived,
            output,
            h * width,
        )
        output = [result]
        bias_parts.append(bias_part)
        demod_parts.append(demod_part)
        if h:
            parts = [once(part, *grad_parts[-4:]) for part in parts]
        grad_parts += exchange(parts, "chan", split > 1)
    output = output[0]
    bias_part = jnp.sum(jnp.concatenate(bias_parts, axis=1)[:, :, 0], axis=0)
    g_demod = jnp.concatenate(demod_parts, axis=1)[:, :, 0]

    modded_parts, style_part, weight_sums = conv_backward(
        me_ref, item_scales, taps_backward, grad_parts, feats, dp_total
    )
    modded_parts = exchange(modded_parts, "chan")
    grad_features = scaled(me_ref, own_style[:, :, None], modded_parts, items)

    grad_bias, g_demod_sum = lax.psum((once(bias_part, style_part), g_demod), "dp")
    cube = demod * demod * demod
    g_style_part = 2.0 * styles * jnp.dot(-0.5 * g_demod * cube, weight_sq, precision=highest)
    g_style_part = g_style_part + jnp.where(
        jnp.arange(items)[:, None] == item, style_part.reshape(1, channels), 0.0
    )
    g_wsq = jnp.dot((-0.5 * g_demod_sum * cube).T, styles * styles, precision=highest)

    tags = jnp.stack([labels // 64, labels % 64], axis=1).astype(BF16)
    tagged = jnp.concatenate([once(latents_all, head), jnp.pad(tags, ((0, 0), (0, 126)))], axis=1)
    tagged = lax.all_gather(tagged, ("dp", "chan"), axis=0, tiled=True)
    all_latents, tags = tagged[:, :-128], tagged[:, -128:-126].astype(F32)
    all_labels = (tags[:, 0] * 64.0 + tags[:, 1]).astype(jnp.int32)
    one_hot = all_labels[None, :] == jnp.arange(class_means.shape[0])[:, None]
    class_sums = jnp.dot(one_hot.astype(BF16), all_latents, preferred_element_type=F32)
    counts = jnp.sum(one_hot.astype(F32), axis=1)
    target = jnp.where(
        counts[:, None] > 0, class_sums / jnp.maximum(counts, 1.0)[:, None], class_means
    )

    share = channels // dp_total
    weight_sums = weight_sums.reshape(dp_total * 9 * channels, share)
    weight_sums = lax.psum_scatter(weight_sums, "dp", scatter_dimension=0, tiled=True)
    weight_sums = once(weight_sums.reshape(9, channels, share), *modded_parts, g_wsq, grad_bias, target)
    thirds = in_thirds(g_style_part, share)
    sent = []
    for x in order(count):
        part_x = lax.dynamic_slice_in_dim(weight_sums, (me ^ x) * own, own, 1)
        sent.append(jnp.concatenate([part_x.reshape(9 * own, share), thirds], axis=0))
    sent = exchange(sent, "chan")
    g_weight = sum(value[: 9 * own].astype(F32) for value in sent).astype(BF16)
    style_sums = [from_thirds(value[9 * own :], styles.shape) for value in sent]
    g_style = tree_sum([style_sums[order(count).index(x)] for x in range(count)])
    sent = once(jnp.concatenate([g_weight, in_thirds(g_style, share)], axis=0), grad_features)
    met = [sent] + [swapped(sent, "dp", x) for x in range(1, dp_total)]
    if share % 128 == 0:
        me_dp_ref = me_dp.astype(jnp.int32)[None]
        grad_weight = finished_weight(me_dp_ref, weight.reshape(9, own, channels), g_wsq, met)
    else:
        blocks = lax.all_gather(met[0][: 9 * own], "dp", axis=1, tiled=True)
        grad_weight = blocks.reshape(9, own, channels).astype(F32)
        grad_weight = grad_weight + 2.0 * weight_full.reshape(9, own, channels) * g_wsq
    grad_weight = grad_weight.reshape(weight.shape)
    g_style = tree_sum([from_thirds(value[9 * own :], styles.shape) for value in met])
    grad_affine_bias = jnp.sum(g_style, axis=0)
    grad_affine = jnp.dot(latent.astype(F32).T, g_style, precision=highest)
    grad_latent = jnp.dot(g_style, affine.astype(F32).T, precision=highest)
    return (
        output,
        grad_features,
        grad_latent,
        grad_affine,
        grad_affine_bias,
        grad_weight,
        grad_bias,
        target,
    )


def solution(mesh):
    in_specs = (
        P("chan", None, "dp", None),
        P(),
        P(),
        P(),
        P(None, None, "chan", None),
        P("chan"),
        P("chan", None, "dp", None),
        P(("dp", "chan"), None),
        P(("dp", "chan")),
        P(),
    )
    out_specs = (
        P("chan", None, "dp", None),
        P("chan", None, "dp", None),
        P(),
        P(),
        P(),
        P(None, None, "chan", None),
        P("chan"),
        P(),
    )
    return jax.shard_map(
        per_device, mesh=mesh, in_specs=in_specs, out_specs=out_specs, check_vma=False
    )
```

```python
import functools

import jax
import jax.numpy as jnp
import ml_dtypes
import numpy as np
from jax import lax
from jax.experimental import pallas as pl
from jax.experimental.pallas import tpu as pltpu
from jax.sharding import PartitionSpec as P

F32 = jnp.float32
BF16 = jnp.bfloat16
IN_VMEM = pl.BlockSpec(memory_space=pltpu.VMEM)
IN_HBM = pl.BlockSpec(memory_space=pltpu.HBM)
IN_SMEM = pl.BlockSpec(memory_space=pltpu.SMEM)
PARAMS = pltpu.CompilerParams(vmem_limit_bytes=60 << 20)
RIM = 7
GROUP = 16


def struct(shape, dtype):
    return jax.ShapeDtypeStruct(shape, dtype)


def sinc_taps():
    offset = np.arange(12) - 5.5
    values = np.sinc(offset * 0.5) * (0.5 + 0.5 * np.cos(np.pi * offset / 6.0))
    return values / values.sum()


def up_table(size):
    tap = np.arange(2 * size)[None, :] - 2 * np.arange(size)[:, None] + 5
    held = (tap >= 0) & (tap < 12)
    return np.where(held, 2.0 * sinc_taps()[np.clip(tap, 0, 11)], 0.0).astype(np.float32)


def halves(table):
    high = table.astype(ml_dtypes.bfloat16)
    return [high, (table - high.astype(np.float32)).astype(ml_dtypes.bfloat16)]


def from_neighbours(value, axis, dim, width):
    size, length = lax.axis_size(axis), value.shape[dim]
    up = [(i, i + 1) for i in range(size - 1)]
    down = [(j, i) for i, j in up]
    last = lax.slice_in_dim(value, length - width, length, axis=dim)
    first = lax.slice_in_dim(value, 0, width, axis=dim)
    return lax.ppermute(last, axis, up), lax.ppermute(first, axis, down)


def swapped(value, axis, bits):
    return lax.ppermute(value, axis, [(i, i ^ bits) for i in range(lax.axis_size(axis))])


def once(value, *others):
    return lax.optimization_barrier((value,) + others)[0]


def order(count, kind):
    far, near = list(range(4, count)), list(range(1, min(4, count)))
    if kind == "far":
        return [0] + far + near
    if kind == "near":
        return [0] + near + far
    mixed = [x for pair in zip(far, near) for x in pair]
    return [0] + mixed + far[len(near) :] + near[len(far) :]


def exchange(parts, kind):
    steps = order(lax.axis_size("chan"), kind)
    return [parts[0]] + [swapped(part, "chan", x) for part, x in zip(parts[1:], steps[1:])]


def started(sems, first, pairs):
    copies = [
        pltpu.make_async_copy(source, target, sems.at[first + index])
        for index, (source, target) in enumerate(pairs)
    ]
    for copy in copies:
        copy.start()
    return copies


def finished(copies):
    for copy in copies:
        copy.wait()


def rows_kernel(count, me_ref, before, value, after, *refs):
    parts, (arrived, rows_first, sems) = refs[:count], refs[count:]
    me = me_ref[0]
    width, items, rows, _ = value.shape
    blocks = count // items
    span = rows // blocks
    finished(started(sems, 0, [(value, arrived)]))
    for item in range(items):
        for group in range(width // GROUP):
            at = slice(group * GROUP, (group + 1) * GROUP)
            rows_first[item, 1 : rows + 1, at] = jnp.swapaxes(arrived[at, item], 0, 1)
        rows_first[item, 0] = before[:, item, 0]
        rows_first[item, rows + 1] = after[:, item, 0]
    pairs = []
    for x, part in zip(order(count, "far"), parts):
        dest = me ^ x
        start = (dest % blocks) * span
        pairs.append((rows_first.at[dest // blocks, pl.ds(start, span + 2)], part))
    finished(started(sems, 1, pairs))


def row_parts(me, before, value, after, count):
    width, items, rows, columns = value.shape
    span = rows * items // count
    return pl.pallas_call(
        functools.partial(rows_kernel, count),
        out_shape=[struct((span + 2, width, columns), BF16)] * count,
        in_specs=[IN_SMEM, IN_VMEM, IN_HBM, IN_VMEM],
        out_specs=[IN_HBM] * count,
        scratch_shapes=[
            pltpu.VMEM((width, items, rows, columns), BF16),
            pltpu.VMEM((items, rows + 2, width, columns), BF16),
            pltpu.SemaphoreType.DMA((1 + count,)),
        ],
        compiler_params=PARAMS,
        name="row_parts",
    )(me, before, value, after)


def weight_pieces(weight, me_dp):
    shares = min(lax.axis_size("dp"), weight.shape[3] // 128)
    share = weight.shape[3] // shares
    held = lax.dynamic_slice_in_dim(weight, me_dp % shares * share, share, 3).reshape(1, 9, -1, share)
    places = [(0, 0)]
    bit = lax.axis_size("chan") // 2
    while bit >= 4:
        held = jnp.concatenate([held, swapped(held, "chan", bit)], axis=0)
        places += [(chan ^ bit, dp) for chan, dp in places]
        bit //= 2
    return held, places


def near_pieces(held, places):
    near = range(1, min(lax.axis_size("chan"), 4))
    held = jnp.concatenate([held] + [swapped(held, "chan", x) for x in near], axis=0)
    return held, places + [(chan ^ x, dp) for x in near for chan, dp in places]


def met_pieces(held, places, bit):
    return swapped(held, "dp", bit), [(chan, dp ^ bit) for chan, dp in places]


def tap_blocks(me, part, pieces, places, taps):
    share = pieces[0].shape[3]
    pairs = []
    for piece, blocks in zip(pieces, places):
        for index, (chan, dp) in enumerate(blocks):
            lanes = pl.ds(pl.multiple_of((part ^ dp) * share, share), share)
            pairs.append((piece.at[index], taps.at[:, me ^ chan, :, lanes]))
    return pairs


def transposed_kernel(places, me_ref, part_ref, *refs):
    pieces, (out, taps, turned, sems) = refs[:-4], refs[-4:]
    pairs = tap_blocks(me_ref[0], part_ref[0], pieces, places, taps)
    finished(started(sems, 0, pairs))
    channels = taps.shape[3]
    copies = []
    for tap in range(9):
        turned[8 - tap] = jnp.transpose(taps[tap].reshape(channels, channels))
        copies += started(sems, len(pairs) + tap, [(turned.at[8 - tap], out.at[8 - tap])])
    finished(copies)


def transposed_taps(me, part, pieces, places, channels):
    own = pieces[0].shape[2]
    blocks = sum(len(place) for place in places)
    return pl.pallas_call(
        functools.partial(transposed_kernel, places),
        out_shape=struct((9, channels, channels), BF16),
        in_specs=[IN_SMEM, IN_SMEM] + [IN_HBM] * len(pieces),
        out_specs=IN_HBM,
        scratch_shapes=[
            pltpu.VMEM((9, channels // own, own, channels), BF16),
            pltpu.VMEM((9, channels, channels), BF16),
            pltpu.SemaphoreType.DMA((blocks + 9,)),
        ],
        compiler_params=PARAMS,
        name="transposed_taps",
    )(me, part, *pieces)


def arrivals(me, parts, arrived):
    count, _, own, _ = arrived.shape
    width = parts[0].shape[1]
    steps = order(count, "near" if width < own else "far")
    return [
        (part, arrived.at[me ^ steps[index % count], :, pl.ds(index // count * width, width)])
        for index, part in enumerate(parts)
    ]


def departures(me, results, outs, kind):
    count = results.shape[1]
    return [(results.at[:, me ^ x], out) for x, out in zip(order(count, kind), outs)]


def fill_shifted(arrived, scales, shifted):
    count, rows, own, columns = arrived.shape

    def row_step(row, carry):
        column = lax.broadcasted_iota(jnp.int32, (own, columns), 1)
        for source in range(count):
            value = arrived[source, row].astype(F32)
            if scales is not None:
                value = (value * scales[source]).astype(BF16).astype(F32)
            before = jnp.where(column == 0, 0.0, pltpu.roll(value, 1, 1))
            after = jnp.where(column == columns - 1, 0.0, pltpu.roll(value, columns - 1, 1))
            shifted[row, 0, source] = before.astype(BF16)
            shifted[row, 1, source] = value.astype(BF16)
            shifted[row, 2, source] = after.astype(BF16)
        return carry

    lax.fori_loop(0, rows, row_step, 0)


def convolved(taps, shifted, row, channels, columns):
    total = None
    for i in range(3):
        for j in range(3):
            term = jnp.dot(
                taps[3 * i + j].reshape(channels, channels),
                shifted[row + i, j].reshape(channels, columns),
                preferred_element_type=F32,
            )
            total = term if total is None else total + term
    return total


def forward_kernel(count, places, me_ref, part_ref, scales, *refs):
    pieces, refs = refs[: len(places)], refs[len(places) :]
    parts, outs = refs[:count], refs[count:-7]
    arrived, shifted, taps, results, wide_scales, sems, row_sems = refs[-7:]
    me = me_ref[0]
    rows, _, own, columns = results.shape
    arriving = started(sems, 0, arrivals(me, parts, arrived))
    tapping = started(sems, count, tap_blocks(me, part_ref[0], pieces, places, taps))
    wide_scales[...] = jnp.broadcast_to(scales[...], wide_scales.shape)
    finished(arriving)
    fill_shifted(arrived, wide_scales, shifted)
    finished(tapping)

    def leaving(row):
        return [
            pltpu.make_async_copy(results.at[row, me ^ x], out.at[row], row_sems.at[row, x])
            for x, out in zip(order(count, "mixed"), outs)
        ]

    def row_step(row, carry):
        total = convolved(taps, shifted, row, count * own, columns)
        results[row] = total.astype(BF16).reshape(count, own, columns)
        for copy in leaving(row):
            copy.start()
        return carry

    lax.fori_loop(0, rows, row_step, 0)
    for row in range(rows):
        finished(leaving(row))


def conv_forward(me, part, pieces, places, scales, parts):
    count = len(parts)
    rows, own, columns = parts[0].shape
    blocks = sum(len(place) for place in places)
    return pl.pallas_call(
        functools.partial(forward_kernel, count, places),
        out_shape=[struct((rows - 2, own, columns), BF16)] * count,
        in_specs=[IN_SMEM, IN_SMEM, IN_VMEM] + [IN_HBM] * (len(pieces) + count),
        out_specs=[IN_HBM] * count,
        scratch_shapes=[
            pltpu.VMEM((count, rows, own, columns), BF16),
            pltpu.VMEM((rows, 3, count, own, columns), BF16),
            pltpu.VMEM((9, count, own, count * own), BF16),
            pltpu.VMEM((rows - 2, count, own, columns), BF16),
            pltpu.VMEM((count, own, columns), F32),
            pltpu.SemaphoreType.DMA((count + blocks,)),
            pltpu.SemaphoreType.DMA((rows - 2, count)),
        ],
        compiler_params=PARAMS,
        name="conv_forward",
    )(me, part, scales, *pieces, *parts)


def backward_kernel(count, split, me_ref, scales, taps_ref, _, *refs):
    grads, refs = refs[: count * split], refs[count * split :]
    feats, outs, (style_ref, weight_out) = refs[:count], refs[count : 2 * count], refs[2 * count : 2 * count + 2]
    arrived, arrived_feats, shifted, modded, taps, results, weight_sums, wide_scales, sems = refs[2 * count + 2 :]
    me = me_ref[0]
    rows, _, own, columns = results.shape
    channels = count * own
    shares, _, _, share = weight_sums.shape
    arriving = started(sems, 0, arrivals(me, grads, arrived))
    tapping = started(
        sems,
        count * split,
        [(taps_ref, taps)] + arrivals(me, feats, arrived_feats),
    )
    wide_scales[...] = jnp.broadcast_to(scales[...], wide_scales.shape)
    finished(arriving)
    fill_shifted(arrived, None, shifted)
    finished(tapping)
    style_ref[...] = jnp.zeros_like(style_ref)

    def row_step(row, carry):
        total = convolved(taps, shifted, row, channels, columns).reshape(count, own, columns)
        results[row] = total.astype(BF16)
        product = total * arrived_feats[:, row + 1].astype(F32)
        style_ref[...] += jnp.sum(product, axis=2, keepdims=True)
        return carry

    lax.fori_loop(0, rows, row_step, 0)
    leaving = started(sems, 0, departures(me, results, outs, "far"))

    def modded_step(row, carry):
        for source in range(count):
            value = arrived_feats[source, row].astype(F32) * wide_scales[source]
            modded[row, source] = value.astype(BF16)
        return carry

    lax.fori_loop(0, rows + 2, modded_step, 0)

    def weight_leaving(tap):
        return pltpu.make_async_copy(weight_sums.at[:, tap], weight_out.at[:, tap], sems.at[count + tap])

    def tap_step(tap, carry):
        i, j = lax.div(tap, 3), lax.rem(tap, 3)
        total = None
        for row in range(rows):
            term = lax.dot_general(
                shifted[row + 1, 2 - j].reshape(channels, columns),
                modded[row + i].reshape(channels, columns),
                (((1,), (1,)), ((), ())),
                preferred_element_type=F32,
            )
            total = term if total is None else total + term
        total = total.astype(BF16)
        for index in range(shares):
            weight_sums[index, tap] = total[:, index * share : (index + 1) * share]
        weight_leaving(tap).start()
        return carry

    lax.fori_loop(0, 9, tap_step, 0)
    finished(leaving + [weight_leaving(tap) for tap in range(9)])


def conv_backward(me, scales, taps, earlier, grads, feats, shares):
    count = len(feats)
    split = len(grads) // count
    rows, own, columns = feats[0].shape
    channels = count * own
    share = channels // shares
    outs = pl.pallas_call(
        functools.partial(backward_kernel, count, split),
        out_shape=[struct((rows - 2, own, columns), BF16)] * count
        + [struct((count, own, 1), F32), struct((shares, 9, channels, share), BF16)],
        in_specs=[IN_SMEM, IN_VMEM] + [IN_HBM] * (2 + len(grads) + count),
        out_specs=[IN_HBM] * count + [IN_VMEM, IN_HBM],
        scratch_shapes=[
            pltpu.VMEM((count, rows, own, columns), BF16),
            pltpu.VMEM((count, rows, own, columns), BF16),
            pltpu.VMEM((rows, 3, count, own, columns), BF16),
            pltpu.VMEM((rows, count, own, columns), BF16),
            pltpu.VMEM((9, channels, channels), BF16),
            pltpu.VMEM((rows - 2, count, own, columns), BF16),
            pltpu.VMEM((shares, 9, channels, share), BF16),
            pltpu.VMEM((count, own, columns), F32),
            pltpu.SemaphoreType.DMA((count + max(9, len(grads) + 1),)),
        ],
        compiler_params=PARAMS,
        name="conv_backward",
    )(me, scales, taps, earlier, *grads, *feats)
    return outs[:-2], outs[-2], outs[-1]


def finish_kernel(shares, part_ref, weight, factors, *refs):
    pieces, (out, arrived, sems) = refs[:shares], refs[shares:]
    part = part_ref[0]
    share = pieces[0].shape[1]
    taps, own, _ = out.shape
    pairs = []
    for x, piece in enumerate(pieces):
        lanes = pl.ds(pl.multiple_of((part ^ x) * share, share), share)
        pairs.append((piece.at[pl.ds(0, taps * own)], arrived.at[:, lanes]))
    finished(started(sems, 0, pairs))
    twice = 2.0 * factors[...]
    for tap in range(taps):
        out[tap] = arrived[tap * own : (tap + 1) * own].astype(F32) + twice * weight[tap].astype(F32)


def finished_weight(part, weight, factors, pieces):
    _, own, channels = weight.shape
    shares = len(pieces)
    return pl.pallas_call(
        functools.partial(finish_kernel, shares),
        out_shape=struct((9, own, channels), F32),
        in_specs=[IN_SMEM, IN_VMEM, IN_VMEM] + [IN_HBM] * shares,
        out_specs=IN_VMEM,
        scratch_shapes=[
            pltpu.VMEM((9 * own, channels), BF16),
            pltpu.SemaphoreType.DMA((shares,)),
        ],
        compiler_params=PARAMS,
        name="finished_weight",
    )(part, weight, factors, *pieces)


def row_blocks(me, parts, rows_ref, start, kind, first_channel=0):
    count = len(parts)
    blocks = count // rows_ref.shape[0]
    span = parts[0].shape[0]
    pairs = []
    channels = pl.ds(first_channel, rows_ref.shape[2])
    for x, part in zip(order(count, kind), parts):
        source = me ^ x
        at = pl.ds(start + (source % blocks) * span, span)
        pairs.append((part.at[:, channels], rows_ref.at[source // blocks, at]))
    return pairs


def rims_kernel(count, me_ref, *refs):
    parts, (first, last, arrived, sems) = refs[:count], refs[-4:]
    rows = arrived.shape[1]
    finished(started(sems, 0, row_blocks(me_ref[0], parts, arrived, 0, "mixed")))
    pairs = [
        (arrived.at[:, pl.ds(0, RIM)], first),
        (arrived.at[:, pl.ds(rows - RIM, RIM)], last),
    ]
    finished(started(sems, count, pairs))


def rims(me, parts, items, earlier):
    count = len(parts)
    span, width, columns = parts[0].shape
    rim = struct((items, RIM, width, columns), BF16)
    return pl.pallas_call(
        functools.partial(rims_kernel, count),
        out_shape=[rim, rim],
        in_specs=[IN_SMEM] + [IN_HBM] * (count + len(earlier)),
        out_specs=[IN_HBM] * 2,
        scratch_shapes=[
            pltpu.VMEM((items, span * count // items, width, columns), BF16),
            pltpu.SemaphoreType.DMA((count + 2,)),
        ],
        compiler_params=PARAMS,
        name="rims",
    )(me, *parts, *earlier)


def sinc_tile(rows, edges, wide, wide_grad, narrow):
    backward = wide_grad is not None
    spare = 1 if backward else 0
    tap = [float(value) for value in sinc_taps()[:6]]
    sums, picked = [{}, {}], {}
    for row in range(rows + 2 * RIM):
        for which, load in enumerate((wide, wide_grad) if backward else (wide,)):
            value = load(row)
            products = [value * (2.0 * tap[t]) for t in range(6)]
            for offset in range(-3, 4):
                pair = row - RIM + offset
                for parity in range(2):
                    t = 2 * offset + parity + 5
                    if -3 - spare <= pair < rows + 3 + spare and 0 <= t < 12:
                        term = products[min(t, 11 - t)]
                        key = 2 * pair + parity
                        sums[which][key] = sums[which][key] + term if key in sums[which] else term
        pair = row - RIM - 3
        if not -3 - spare <= pair < rows + 3 + spare:
            continue
        for key in (2 * pair, 2 * pair + 1):
            value = sums[0].pop(key)
            sigmoid = 0.5 + 0.5 * jnp.tanh(0.5 * value)
            result = value * sigmoid
            if backward:
                result = sums[1].pop(key) * (sigmoid + result * (1.0 - sigmoid))
            if pair < 0:
                result = result * edges[0]
            if pair >= rows:
                result = result * edges[1]
            picked[key] = result
        centre = pair - 3
        if -spare <= centre < rows + spare:
            total = None
            for t in range(6):
                term = tap[t] * (picked[2 * centre + t - 5] + picked[2 * centre + 6 - t])
                total = term if total is None else total + term
            narrow(centre + spare, total)
        for key in (2 * centre - 6, 2 * centre - 5, 2 * centre - 4):
            picked.pop(key, None)


def widened(values, up):
    columns = values.shape[-1]
    flat = values.reshape(-1, columns)
    total = jnp.dot(jnp.concatenate([flat, flat], axis=1), up, preferred_element_type=F32)
    return total.reshape(-1, GROUP, 2 * columns)


def narrowed(values, down):
    columns = values.shape[-1]
    flat = values.reshape(-1, columns)
    high = flat.astype(BF16)
    low = (flat - high.astype(F32)).astype(BF16)
    split = jnp.concatenate([high, high, low], axis=1)
    return jnp.dot(split, down, preferred_element_type=F32).reshape(-1, GROUP, columns // 2)


def filtered_rows(rows, edges, wide, wide_grad, narrow):
    lane_tiles = wide.shape[2] // 128
    first, last = edges

    def tile_step(index, carry):
        lanes = pl.ds(pl.multiple_of(lax.rem(index, lane_tiles) * 128, 128), 128)
        subs = pl.ds(pl.multiple_of(lax.div(index, lane_tiles) * 8, 8), 8)

        def store(row, value):
            narrow[row, subs, lanes] = value

        load_grad = None if wide_grad is None else lambda row: wide_grad[row, subs, lanes]
        sinc_tile(rows, (first, last), lambda row: wide[row, subs, lanes], load_grad, store)
        return carry

    lax.fori_loop(0, GROUP // 8 * lane_tiles, tile_step, 0)


def fill_wide(rows, edges, raw, scale, shift, up, wide):
    spread = widened(raw, up) * scale
    wide[:RIM] = spread[:RIM] + shift * edges[0]
    wide[RIM : RIM + rows] = spread[RIM : RIM + rows] + shift
    wide[RIM + rows :] = spread[RIM + rows :] + shift * edges[1]


def forward_sinc_kernel(count, first_channel, me_ref, edge_ref, factors, up_sums, *refs):
    before, after, up_ref, down_ref = refs[:4]
    parts, (out, raw, up, down, out_rows, wide, narrow, sems) = refs[4 : 4 + count], refs[-8:]
    items, extent, width, columns = raw.shape
    rows = extent - 2 * RIM
    edges = edge_ref[0], edge_ref[1]
    own_channels = pl.ds(first_channel, width)
    pairs = row_blocks(me_ref[0], parts, raw, RIM, "mixed", first_channel)
    pairs += [
        (up_ref, up),
        (down_ref, down),
        (before.at[:, :, own_channels], raw.at[:, pl.ds(0, RIM)]),
        (after.at[:, :, own_channels], raw.at[:, pl.ds(RIM + rows, RIM)]),
    ]
    finished(started(sems, 0, pairs))
    leaving = []
    for item in range(items):
        for group in range(width // GROUP):
            at = slice(group * GROUP, (group + 1) * GROUP)
            shift = factors[items, at] * up_sums[...]
            fill_wide(rows, edges, raw[item, :, at], factors[item, at], shift, up[...], wide)
            filtered_rows(rows, edges, wide, None, narrow)
            result = narrowed(narrow[...], down[...])
            out_rows[at, item] = jnp.swapaxes(result, 0, 1).astype(BF16)
            target = out.at[pl.ds(first_channel + group * GROUP, GROUP), item]
            source = out_rows.at[pl.ds(group * GROUP, GROUP), item]
            leaving += started(sems, len(leaving), [(source, target)])
    finished(leaving)


def forward_sinc(me, edges, factors, tables, up_sums, before, after, parts, own, out, first_channel, earlier):
    count = len(parts)
    span, _, columns = parts[0].shape
    items, width = factors.shape[0] - 1, factors.shape[1]
    rows = span * count // items
    extent = rows + 2 * RIM
    return pl.pallas_call(
        functools.partial(forward_sinc_kernel, count, first_channel),
        out_shape=struct((own, items, rows, columns), BF16),
        in_specs=[IN_SMEM, IN_SMEM] + [IN_VMEM] * 2 + [IN_HBM] * (5 + count + len(out)),
        out_specs=IN_HBM,
        input_output_aliases={9 + count: 0} if out else {},
        scratch_shapes=[
            pltpu.VMEM((items, extent, width, columns), BF16),
            pltpu.VMEM(tables[0].shape, BF16),
            pltpu.VMEM(tables[1].shape, BF16),
            pltpu.VMEM((width, items, rows, columns), BF16),
            pltpu.VMEM((extent, GROUP, 2 * columns), F32),
            pltpu.VMEM((rows, GROUP, 2 * columns), F32),
            pltpu.SemaphoreType.DMA((max(count + 4, items * width // GROUP),)),
        ],
        compiler_params=PARAMS,
        name="forward_sinc",
    )(me, edges, factors, up_sums, before, after, *tables, *parts, earlier, *out)


def backward_sinc_kernel(count, first_channel, me_ref, edge_ref, factors, up_sums, *refs):
    before, after, cotangent, up_ref, down_ref = refs[:5]
    parts, (grad_bias, grad_demod) = refs[5 : 5 + count], refs[5 + count : 7 + count]
    grad_parts = refs[7 + count : 7 + 2 * count]
    raw, cot, up, down, grad_raw, wide, wide_grad, narrow, sems = refs[7 + 2 * count :]
    me = me_ref[0]
    items, extent, width, columns = raw.shape
    rows = extent - 2 * RIM
    edges = edge_ref[0], edge_ref[1]
    own_channels = pl.ds(first_channel, width)
    pairs = row_blocks(me, parts, raw, RIM, "mixed", first_channel)
    pairs += [
        (up_ref, up),
        (down_ref, down),
        (before.at[:, :, own_channels], raw.at[:, pl.ds(0, RIM)]),
        (after.at[:, :, own_channels], raw.at[:, pl.ds(RIM + rows, RIM)]),
        (cotangent.at[:, :, own_channels], cot),
    ]
    finished(started(sems, 0, pairs))
    for item in range(items):
        for group in range(width // GROUP):
            at = slice(group * GROUP, (group + 1) * GROUP)
            scale = factors[item, at]
            fill_wide(rows, edges, raw[item, :, at], scale, factors[items, at] * up_sums[...], up[...], wide)
            wide_grad[...] = widened(cot[item, :, at], up[...])
            filtered_rows(rows, edges, wide, wide_grad, narrow)
            grad = narrowed(narrow[...], down[...])
            scaled_grad = grad * scale
            grad_raw[item, 0, at] = (scaled_grad[0] * edges[0]).astype(BF16)
            grad_raw[item, 1 : rows + 1, at] = scaled_grad[1 : rows + 1].astype(BF16)
            grad_raw[item, rows + 1, at] = (scaled_grad[rows + 1] * edges[1]).astype(BF16)
            grad = grad[1 : rows + 1]
            own = raw[item, RIM : RIM + rows, at].astype(F32)
            grad_bias[item, at] = jnp.sum(jnp.sum(grad, axis=0), axis=1, keepdims=True)
            grad_demod[item, at] = jnp.sum(jnp.sum(grad * own, axis=0), axis=1, keepdims=True)
    blocks = count // items
    span = rows // blocks
    pairs = []
    kind = "near" if width < cotangent.shape[2] else "far"
    for x, part in zip(order(count, kind), grad_parts):
        dest = me ^ x
        pairs.append((grad_raw.at[dest // blocks, pl.ds((dest % blocks) * span, span + 2)], part))
    finished(started(sems, 0, pairs))


def backward_sinc(me, edges, factors, tables, up_sums, before, after, cotangent, parts, first_channel):
    count = len(parts)
    items, extent, _, columns = cotangent.shape
    span, width = parts[0].shape[0], factors.shape[1]
    rows = extent - 2 * RIM
    wide = pltpu.VMEM((extent, GROUP, 2 * columns), F32)
    outs = pl.pallas_call(
        functools.partial(backward_sinc_kernel, count, first_channel),
        out_shape=[struct((items, width, 1), F32)] * 2 + [struct((span + 2, width, columns), BF16)] * count,
        in_specs=[IN_SMEM, IN_SMEM] + [IN_VMEM] * 2 + [IN_HBM] * (5 + count),
        out_specs=[IN_VMEM, IN_VMEM] + [IN_HBM] * count,
        scratch_shapes=[
            pltpu.VMEM((items, extent, width, columns), BF16),
            pltpu.VMEM((items, extent, width, columns), BF16),
            pltpu.VMEM(tables[0].shape, BF16),
            pltpu.VMEM(tables[1].shape, BF16),
            pltpu.VMEM((items, rows + 2, width, columns), BF16),
            wide,
            wide,
            pltpu.VMEM((rows + 2, GROUP, 2 * columns), F32),
            pltpu.SemaphoreType.DMA((count + 5,)),
        ],
        compiler_params=PARAMS,
        name="backward_sinc",
    )(me, edges, factors, up_sums, before, after, cotangent, *tables, *parts)
    return outs[0], outs[1], outs[2:]


def scale_kernel(count, me_ref, scales, *refs):
    parts, (out, arrived, results, sems) = refs[:count], refs[count:]
    width, items, _, _ = out.shape
    finished(started(sems, 0, row_blocks(me_ref[0], parts, arrived, 0, "far")))
    leaving = []
    for item in range(items):
        for group in range(width // GROUP):
            at = slice(group * GROUP, (group + 1) * GROUP)
            value = arrived[item, :, at].astype(F32) * scales[item, at]
            results[at, item] = jnp.swapaxes(value, 0, 1)
            spot = pl.ds(group * GROUP, GROUP)
            leaving += started(sems, len(leaving), [(results.at[spot, item], out.at[spot, item])])
    finished(leaving)


def scaled(me, scales, parts, items):
    count = len(parts)
    span, width, columns = parts[0].shape
    rows = span * count // items
    return pl.pallas_call(
        functools.partial(scale_kernel, count),
        out_shape=struct((width, items, rows, columns), F32),
        in_specs=[IN_SMEM, IN_VMEM] + [IN_HBM] * count,
        out_specs=IN_HBM,
        scratch_shapes=[
            pltpu.VMEM((items, rows, width, columns), BF16),
            pltpu.VMEM((width, items, rows, columns), F32),
            pltpu.SemaphoreType.DMA((max(count, items * width // GROUP),)),
        ],
        compiler_params=PARAMS,
        name="scale_features",
    )(me, scales, *parts)


def in_thirds(value, lanes):
    terms = []
    for _ in range(3):
        terms.append(lax.reduce_precision(value, 8, 7))
        value = value - terms[-1]
    rows = jnp.stack(terms).astype(BF16).reshape(-1, lanes)
    return jnp.pad(rows, ((0, -rows.shape[0] % 16), (0, 0)))


def from_thirds(rows, shape):
    terms = rows.astype(F32).reshape(-1)[: 3 * shape[0] * shape[1]].reshape((3,) + shape)
    return terms[0] + terms[1] + terms[2]


def tree_sum(values):
    while len(values) > 1:
        values = [a + b for a, b in zip(values[::2], values[1::2])]
    return values[0]


def per_device(
    features,
    latent,
    affine,
    affine_bias,
    weight,
    out_bias,
    cotangent,
    latents_all,
    labels,
    class_means,
):
    highest = lax.Precision.HIGHEST
    own, items, rows, columns = features.shape
    channels = weight.shape[3]
    count = lax.axis_size("chan")
    dp_total = lax.axis_size("dp")
    me = lax.axis_index("chan")
    me_dp = lax.axis_index("dp")
    me_ref = me.astype(jnp.int32)[None]
    blocks = count // items
    span = rows // blocks
    split = max(1, min(2, own // GROUP))
    width = own // split

    styles = jnp.dot(latent, affine, preferred_element_type=F32) + affine_bias
    own_style = lax.dynamic_slice_in_dim(styles, me * own, own, 1)
    weight_full = weight.astype(F32)
    weight_sq = jnp.sum(weight_full * weight_full, axis=(0, 1))
    demod = lax.rsqrt(jnp.dot(styles * styles, weight_sq.T, precision=highest) + 1e-08)
    item = me // blocks
    item_scales = lax.dynamic_index_in_dim(styles, item, 0, keepdims=False).reshape(count, own, 1)

    before, after = from_neighbours(features, "dp", 2, 1)
    prepared = row_parts(me_ref, before, features, after, count)
    feats = exchange(prepared, "far")
    held, places = near_pieces(*weight_pieces(once(weight, prepared[0]), me_dp))
    shares = channels // held.shape[3]
    part = (me_dp % shares).astype(jnp.int32)[None]
    held = once(held, *feats[1:3], item_scales, demod)
    bit = shares // 2
    while bit > 1:
        met, met_places = met_pieces(held, places, bit)
        held, places = jnp.concatenate([held, met], axis=0), places + met_places
        bit //= 2
    cot_before, cot_after = from_neighbours(once(cotangent, feats[3]), "dp", 2, RIM)
    held = once(held, *feats[3:7])
    met, met_places = met_pieces(held, places, 1)
    pieces, places = [held, met], (tuple(places), tuple(met_places))

    table = up_table(columns)
    down_halves = halves(0.5 * table.T)
    tables = [np.concatenate(halves(table)), np.concatenate(down_halves + down_halves[:1])]
    up_sums = np.sum(table, axis=0)[None]
    edges = jnp.stack([me_dp > 0, me_dp < dp_total - 1]).astype(F32)

    item_scales = once(item_scales, cot_before, cot_after)
    raw_parts = conv_forward(me_ref, part, pieces, places, item_scales, feats)
    taps_backward = transposed_taps(
        me_ref, part, [once(piece, raw_parts[0]) for piece in pieces], places, channels
    )
    all_maps, grad_parts, bias_parts, demod_parts = [], [], [], []
    factors = jnp.concatenate([demod, out_bias[None]])[:, :, None]
    up = [(i, i + 1) for i in range(dp_total - 1)]
    down = [(j, i) for i, j in up]
    arrived = exchange(raw_parts, "mixed")
    cot = jnp.concatenate([cot_before, cotangent, cot_after], axis=2)
    cot = jnp.transpose(cot, (1, 2, 0, 3))
    head, tail = rims(me_ref, arrived, items, [taps_backward, cot])
    before, after = lax.ppermute(tail, "dp", up), lax.ppermute(head, "dp", down)
    for h in range(split):
        at = slice(h * width, (h + 1) * width)
        maps = (factors[:, at], tables, up_sums, before, after)
        all_maps.append(maps)
        bias_part, demod_part, parts = backward_sinc(
            me_ref, edges, *maps, cot, arrived, h * width
        )
        bias_parts.append(bias_part)
        demod_parts.append(demod_part)
        if h:
            parts = [once(part, *grad_parts[-4:]) for part in parts]
        grad_parts += exchange(parts, "near" if split > 1 else "far")
    bias_part = jnp.sum(jnp.concatenate(bias_parts, axis=1)[:, :, 0], axis=0)
    g_demod = jnp.concatenate(demod_parts, axis=1)[:, :, 0]

    output = [forward_sinc(me_ref, edges, *all_maps[0], arrived, own, [], 0, bias_parts[-1])]
    modded_parts, style_part, weight_sums = conv_backward(
        me_ref, item_scales, taps_backward, output[0], grad_parts, feats, dp_total
    )
    modded_parts = exchange(modded_parts, "far")
    for h in range(1, split):
        output = [forward_sinc(me_ref, edges, *all_maps[h], arrived, own, output, h * width, style_part)]
    output = output[0]
    grad_features = scaled(me_ref, own_style[:, :, None], modded_parts, items)

    grad_bias, g_demod_sum = lax.psum((once(bias_part, style_part), g_demod), "dp")
    cube = demod * demod * demod
    g_style_part = 2.0 * styles * jnp.dot(-0.5 * g_demod * cube, weight_sq, precision=highest)
    g_style_part = g_style_part + jnp.where(
        jnp.arange(items)[:, None] == item, style_part.reshape(1, channels), 0.0
    )
    g_wsq = jnp.dot((-0.5 * g_demod_sum * cube).T, styles * styles, precision=highest)

    tags = jnp.stack([labels // 64, labels % 64], axis=1).astype(BF16)
    tagged = jnp.concatenate([once(latents_all, head), jnp.pad(tags, ((0, 0), (0, 126)))], axis=1)
    tagged = lax.all_gather(tagged, ("dp", "chan"), axis=0, tiled=True)
    all_latents, tags = tagged[:, :-128], tagged[:, -128:-126].astype(F32)
    all_labels = (tags[:, 0] * 64.0 + tags[:, 1]).astype(jnp.int32)
    one_hot = all_labels[None, :] == jnp.arange(class_means.shape[0])[:, None]
    class_sums = jnp.dot(one_hot.astype(BF16), all_latents, preferred_element_type=F32)
    counts = jnp.sum(one_hot.astype(F32), axis=1)
    target = jnp.where(
        counts[:, None] > 0, class_sums / jnp.maximum(counts, 1.0)[:, None], class_means
    )

    share = channels // dp_total
    weight_sums = weight_sums.reshape(dp_total * 9 * channels, share)
    weight_sums = lax.psum_scatter(weight_sums, "dp", scatter_dimension=0, tiled=True)
    weight_sums = once(weight_sums.reshape(9, channels, share), *modded_parts, g_wsq, grad_bias, target, output)
    thirds = in_thirds(g_style_part, share)
    sent = []
    for x in order(count, "mixed"):
        part_x = lax.dynamic_slice_in_dim(weight_sums, (me ^ x) * own, own, 1)
        sent.append(jnp.concatenate([part_x.reshape(9 * own, share), thirds], axis=0))
    sent = exchange(sent, "mixed")
    g_weight = sum(value[: 9 * own].astype(F32) for value in sent).astype(BF16)
    style_sums = [from_thirds(value[9 * own :], styles.shape) for value in sent]
    g_style = tree_sum([style_sums[order(count, "mixed").index(x)] for x in range(count)])
    sent = once(jnp.concatenate([g_weight, in_thirds(g_style, share)], axis=0), grad_features)
    met = [sent] + [swapped(sent, "dp", x) for x in range(1, dp_total)]
    if share % 128 == 0:
        me_dp_ref = me_dp.astype(jnp.int32)[None]
        grad_weight = finished_weight(me_dp_ref, weight.reshape(9, own, channels), g_wsq, met)
    else:
        blocks = lax.all_gather(met[0][: 9 * own], "dp", axis=1, tiled=True)
        grad_weight = blocks.reshape(9, own, channels).astype(F32)
        grad_weight = grad_weight + 2.0 * weight_full.reshape(9, own, channels) * g_wsq
    grad_weight = grad_weight.reshape(weight.shape)
    g_style = tree_sum([from_thirds(value[9 * own :], styles.shape) for value in met])
    grad_affine_bias = jnp.sum(g_style, axis=0)
    grad_affine = jnp.dot(latent.astype(F32).T, g_style, precision=highest)
    grad_latent = jnp.dot(g_style, affine.astype(F32).T, precision=highest)
    return (
        output,
        grad_features,
        grad_latent,
        grad_affine,
        grad_affine_bias,
        grad_weight,
        grad_bias,
        target,
    )


def solution(mesh):
    in_specs = (
        P("chan", None, "dp", None),
        P(),
        P(),
        P(),
        P(None, None, "chan", None),
        P("chan"),
        P("chan", None, "dp", None),
        P(("dp", "chan"), None),
        P(("dp", "chan")),
        P(),
    )
    out_specs = (
        P("chan", None, "dp", None),
        P("chan", None, "dp", None),
        P(),
        P(),
        P(),
        P(None, None, "chan", None),
        P("chan"),
        P(),
    )
    return jax.shard_map(
        per_device, mesh=mesh, in_specs=in_specs, out_specs=out_specs, check_vma=False
    )
```

```python
import functools

import jax
import jax.numpy as jnp
import ml_dtypes
import numpy as np
from jax import lax
from jax.experimental import pallas as pl
from jax.experimental.pallas import tpu as pltpu
from jax.sharding import PartitionSpec as P

F32 = jnp.float32
BF16 = jnp.bfloat16
IN_VMEM = pl.BlockSpec(memory_space=pltpu.VMEM)
IN_HBM = pl.BlockSpec(memory_space=pltpu.HBM)
IN_SMEM = pl.BlockSpec(memory_space=pltpu.SMEM)
PARAMS = pltpu.CompilerParams(vmem_limit_bytes=60 << 20)
RIM = 7
GROUP = 16


def struct(shape, dtype):
    return jax.ShapeDtypeStruct(shape, dtype)


def sinc_taps():
    offset = np.arange(12) - 5.5
    values = np.sinc(offset * 0.5) * (0.5 + 0.5 * np.cos(np.pi * offset / 6.0))
    return values / values.sum()


def up_table(size):
    tap = np.arange(2 * size)[None, :] - 2 * np.arange(size)[:, None] + 5
    held = (tap >= 0) & (tap < 12)
    return np.where(held, 2.0 * sinc_taps()[np.clip(tap, 0, 11)], 0.0).astype(np.float32)


def halves(table):
    high = table.astype(ml_dtypes.bfloat16)
    return [high, (table - high.astype(np.float32)).astype(ml_dtypes.bfloat16)]


def from_neighbours(value, axis, dim, width):
    size, length = lax.axis_size(axis), value.shape[dim]
    up = [(i, i + 1) for i in range(size - 1)]
    down = [(j, i) for i, j in up]
    last = lax.slice_in_dim(value, length - width, length, axis=dim)
    first = lax.slice_in_dim(value, 0, width, axis=dim)
    return lax.ppermute(last, axis, up), lax.ppermute(first, axis, down)


def swapped(value, axis, bits):
    return lax.ppermute(value, axis, [(i, i ^ bits) for i in range(lax.axis_size(axis))])


def once(value, *others):
    return lax.optimization_barrier((value,) + others)[0]


def order(count, kind):
    far, near = list(range(4, count)), list(range(1, min(4, count)))
    if kind == "far":
        return [0] + far + near
    if kind == "near":
        return [0] + near + far
    mixed = [x for pair in zip(far, near) for x in pair]
    return [0] + mixed + far[len(near) :] + near[len(far) :]


def exchange(parts, kind):
    steps = order(lax.axis_size("chan"), kind)
    return [parts[0]] + [swapped(part, "chan", x) for part, x in zip(parts[1:], steps[1:])]


def started(sems, first, pairs):
    copies = [
        pltpu.make_async_copy(source, target, sems.at[first + index])
        for index, (source, target) in enumerate(pairs)
    ]
    for copy in copies:
        copy.start()
    return copies


def finished(copies):
    for copy in copies:
        copy.wait()


def rows_kernel(count, me_ref, before, value, after, *refs):
    parts, (arrived, rows_first, sems) = refs[:count], refs[count:]
    me = me_ref[0]
    width, items, rows, _ = value.shape
    blocks = count // items
    span = rows // blocks
    finished(started(sems, 0, [(value, arrived)]))
    for item in range(items):
        for group in range(width // GROUP):
            at = slice(group * GROUP, (group + 1) * GROUP)
            rows_first[item, 1 : rows + 1, at] = jnp.swapaxes(arrived[at, item], 0, 1)
        rows_first[item, 0] = before[:, item, 0]
        rows_first[item, rows + 1] = after[:, item, 0]
    pairs = []
    for x, part in zip(order(count, "far"), parts):
        dest = me ^ x
        start = (dest % blocks) * span
        pairs.append((rows_first.at[dest // blocks, pl.ds(start, span + 2)], part))
    finished(started(sems, 1, pairs))


def row_parts(me, before, value, after, count):
    width, items, rows, columns = value.shape
    span = rows * items // count
    return pl.pallas_call(
        functools.partial(rows_kernel, count),
        out_shape=[struct((span + 2, width, columns), BF16)] * count,
        in_specs=[IN_SMEM, IN_VMEM, IN_HBM, IN_VMEM],
        out_specs=[IN_HBM] * count,
        scratch_shapes=[
            pltpu.VMEM((width, items, rows, columns), BF16),
            pltpu.VMEM((items, rows + 2, width, columns), BF16),
            pltpu.SemaphoreType.DMA((1 + count,)),
        ],
        compiler_params=PARAMS,
        name="row_parts",
    )(me, before, value, after)


def weight_pieces(weight, me_dp):
    shares = min(lax.axis_size("dp"), weight.shape[3] // 128)
    share = weight.shape[3] // shares
    held = lax.dynamic_slice_in_dim(weight, me_dp % shares * share, share, 3).reshape(1, 9, -1, share)
    places = [(0, 0)]
    bit = lax.axis_size("chan") // 2
    while bit >= 4:
        held = jnp.concatenate([held, swapped(held, "chan", bit)], axis=0)
        places += [(chan ^ bit, dp) for chan, dp in places]
        bit //= 2
    return held, places


def near_pieces(held, places):
    near = range(1, min(lax.axis_size("chan"), 4))
    held = jnp.concatenate([held] + [swapped(held, "chan", x) for x in near], axis=0)
    return held, places + [(chan ^ x, dp) for x in near for chan, dp in places]


def met_pieces(held, places, bit):
    return swapped(held, "dp", bit), [(chan, dp ^ bit) for chan, dp in places]


def tap_blocks(me, part, pieces, places, taps):
    share = pieces[0].shape[3]
    pairs = []
    for piece, blocks in zip(pieces, places):
        for index, (chan, dp) in enumerate(blocks):
            lanes = pl.ds(pl.multiple_of((part ^ dp) * share, share), share)
            pairs.append((piece.at[index], taps.at[:, me ^ chan, :, lanes]))
    return pairs


def transposed_kernel(places, me_ref, part_ref, *refs):
    pieces, (out, taps, turned, sems) = refs[:-4], refs[-4:]
    pairs = tap_blocks(me_ref[0], part_ref[0], pieces, places, taps)
    finished(started(sems, 0, pairs))
    channels = taps.shape[3]
    copies = []
    for tap in range(9):
        turned[8 - tap] = jnp.transpose(taps[tap].reshape(channels, channels))
        copies += started(sems, len(pairs) + tap, [(turned.at[8 - tap], out.at[8 - tap])])
    finished(copies)


def transposed_taps(me, part, pieces, places, channels):
    own = pieces[0].shape[2]
    blocks = sum(len(place) for place in places)
    return pl.pallas_call(
        functools.partial(transposed_kernel, places),
        out_shape=struct((9, channels, channels), BF16),
        in_specs=[IN_SMEM, IN_SMEM] + [IN_HBM] * len(pieces),
        out_specs=IN_HBM,
        scratch_shapes=[
            pltpu.VMEM((9, channels // own, own, channels), BF16),
            pltpu.VMEM((9, channels, channels), BF16),
            pltpu.SemaphoreType.DMA((blocks + 9,)),
        ],
        compiler_params=PARAMS,
        name="transposed_taps",
    )(me, part, *pieces)


def arrivals(me, parts, arrived):
    count, _, own, _ = arrived.shape
    width = parts[0].shape[1]
    steps = order(count, "near" if width < own else "far")
    return [
        (part, arrived.at[me ^ steps[index % count], :, pl.ds(index // count * width, width)])
        for index, part in enumerate(parts)
    ]


def departures(me, results, outs, kind):
    count = results.shape[1]
    return [(results.at[:, me ^ x], out) for x, out in zip(order(count, kind), outs)]


def fill_shifted(arrived, scales, shifted):
    count, rows, own, columns = arrived.shape

    def row_step(row, carry):
        column = lax.broadcasted_iota(jnp.int32, (own, columns), 1)
        for source in range(count):
            value = arrived[source, row].astype(F32)
            if scales is not None:
                value = (value * scales[source]).astype(BF16).astype(F32)
            before = jnp.where(column == 0, 0.0, pltpu.roll(value, 1, 1))
            after = jnp.where(column == columns - 1, 0.0, pltpu.roll(value, columns - 1, 1))
            shifted[row, 0, source] = before.astype(BF16)
            shifted[row, 1, source] = value.astype(BF16)
            shifted[row, 2, source] = after.astype(BF16)
        return carry

    lax.fori_loop(0, rows, row_step, 0)


def convolved(taps, shifted, row, channels, columns):
    total = None
    for i in range(3):
        for j in range(3):
            term = jnp.dot(
                taps[3 * i + j].reshape(channels, channels),
                shifted[row + i, j].reshape(channels, columns),
                preferred_element_type=F32,
            )
            total = term if total is None else total + term
    return total


def forward_kernel(count, places, me_ref, part_ref, scales, *refs):
    pieces, refs = refs[: len(places)], refs[len(places) :]
    parts, outs = refs[:count], refs[count:-7]
    arrived, shifted, taps, results, wide_scales, sems, row_sems = refs[-7:]
    me = me_ref[0]
    rows, _, own, columns = results.shape
    arriving = started(sems, 0, arrivals(me, parts, arrived))
    tapping = started(sems, count, tap_blocks(me, part_ref[0], pieces, places, taps))
    wide_scales[...] = jnp.broadcast_to(scales[...], wide_scales.shape)
    finished(arriving)
    fill_shifted(arrived, wide_scales, shifted)
    finished(tapping)

    def leaving(row):
        return [
            pltpu.make_async_copy(results.at[row, me ^ x], out.at[row], row_sems.at[row, x])
            for x, out in zip(order(count, "mixed"), outs)
        ]

    def row_step(row, carry):
        total = convolved(taps, shifted, row, count * own, columns)
        results[row] = total.astype(BF16).reshape(count, own, columns)
        for copy in leaving(row):
            copy.start()
        return carry

    lax.fori_loop(0, rows, row_step, 0, unroll=min(4, rows))
    for row in range(rows):
        finished(leaving(row))


def conv_forward(me, part, pieces, places, scales, parts):
    count = len(parts)
    rows, own, columns = parts[0].shape
    blocks = sum(len(place) for place in places)
    return pl.pallas_call(
        functools.partial(forward_kernel, count, places),
        out_shape=[struct((rows - 2, own, columns), BF16)] * count,
        in_specs=[IN_SMEM, IN_SMEM, IN_VMEM] + [IN_HBM] * (len(pieces) + count),
        out_specs=[IN_HBM] * count,
        scratch_shapes=[
            pltpu.VMEM((count, rows, own, columns), BF16),
            pltpu.VMEM((rows, 3, count, own, columns), BF16),
            pltpu.VMEM((9, count, own, count * own), BF16),
            pltpu.VMEM((rows - 2, count, own, columns), BF16),
            pltpu.VMEM((count, own, columns), F32),
            pltpu.SemaphoreType.DMA((count + blocks,)),
            pltpu.SemaphoreType.DMA((rows - 2, count)),
        ],
        compiler_params=PARAMS,
        name="conv_forward",
    )(me, part, scales, *pieces, *parts)


def backward_kernel(count, split, me_ref, scales, taps_ref, _, *refs):
    grads, refs = refs[: count * split], refs[count * split :]
    feats, outs, (style_ref, weight_out) = refs[:count], refs[count : 2 * count], refs[2 * count : 2 * count + 2]
    arrived, arrived_feats, shifted, modded, taps, results, weight_sums, wide_scales, sems = refs[2 * count + 2 :]
    me = me_ref[0]
    rows, _, own, columns = results.shape
    channels = count * own
    shares, _, _, share = weight_sums.shape
    arriving = started(sems, 0, arrivals(me, grads, arrived))
    tapping = started(
        sems,
        count * split,
        [(taps_ref, taps)] + arrivals(me, feats, arrived_feats),
    )
    wide_scales[...] = jnp.broadcast_to(scales[...], wide_scales.shape)
    finished(arriving)
    fill_shifted(arrived, None, shifted)
    finished(tapping)
    style_ref[...] = jnp.zeros_like(style_ref)

    def row_step(row, carry):
        total = convolved(taps, shifted, row, channels, columns).reshape(count, own, columns)
        results[row] = total.astype(BF16)
        product = total * arrived_feats[:, row + 1].astype(F32)
        style_ref[...] += jnp.sum(product, axis=2, keepdims=True)
        return carry

    lax.fori_loop(0, rows, row_step, 0, unroll=min(4, rows))
    leaving = started(sems, 0, departures(me, results, outs, "far"))

    def modded_step(row, carry):
        for source in range(count):
            value = arrived_feats[source, row].astype(F32) * wide_scales[source]
            modded[row, source] = value.astype(BF16)
        return carry

    lax.fori_loop(0, rows + 2, modded_step, 0)

    def weight_leaving(tap):
        return pltpu.make_async_copy(weight_sums.at[:, tap], weight_out.at[:, tap], sems.at[count + tap])

    def tap_step(tap, carry):
        i, j = lax.div(tap, 3), lax.rem(tap, 3)
        total = None
        for row in range(rows):
            term = lax.dot_general(
                shifted[row + 1, 2 - j].reshape(channels, columns),
                modded[row + i].reshape(channels, columns),
                (((1,), (1,)), ((), ())),
                preferred_element_type=F32,
            )
            total = term if total is None else total + term
        total = total.astype(BF16)
        for index in range(shares):
            weight_sums[index, tap] = total[:, index * share : (index + 1) * share]
        weight_leaving(tap).start()
        return carry

    lax.fori_loop(0, 9, tap_step, 0, unroll=3)
    finished(leaving + [weight_leaving(tap) for tap in range(9)])


def conv_backward(me, scales, taps, earlier, grads, feats, shares):
    count = len(feats)
    split = len(grads) // count
    rows, own, columns = feats[0].shape
    channels = count * own
    share = channels // shares
    outs = pl.pallas_call(
        functools.partial(backward_kernel, count, split),
        out_shape=[struct((rows - 2, own, columns), BF16)] * count
        + [struct((count, own, 1), F32), struct((shares, 9, channels, share), BF16)],
        in_specs=[IN_SMEM, IN_VMEM] + [IN_HBM] * (2 + len(grads) + count),
        out_specs=[IN_HBM] * count + [IN_VMEM, IN_HBM],
        scratch_shapes=[
            pltpu.VMEM((count, rows, own, columns), BF16),
            pltpu.VMEM((count, rows, own, columns), BF16),
            pltpu.VMEM((rows, 3, count, own, columns), BF16),
            pltpu.VMEM((rows, count, own, columns), BF16),
            pltpu.VMEM((9, channels, channels), BF16),
            pltpu.VMEM((rows - 2, count, own, columns), BF16),
            pltpu.VMEM((shares, 9, channels, share), BF16),
            pltpu.VMEM((count, own, columns), F32),
            pltpu.SemaphoreType.DMA((count + max(9, len(grads) + 1),)),
        ],
        compiler_params=PARAMS,
        name="conv_backward",
    )(me, scales, taps, earlier, *grads, *feats)
    return outs[:-2], outs[-2], outs[-1]


def finish_kernel(shares, part_ref, weight, factors, *refs):
    pieces, (out, arrived, sems) = refs[:shares], refs[shares:]
    part = part_ref[0]
    share = pieces[0].shape[1]
    taps, own, _ = out.shape
    pairs = []
    for x, piece in enumerate(pieces):
        lanes = pl.ds(pl.multiple_of((part ^ x) * share, share), share)
        pairs.append((piece.at[pl.ds(0, taps * own)], arrived.at[:, lanes]))
    finished(started(sems, 0, pairs))
    twice = 2.0 * factors[...]
    for tap in range(taps):
        out[tap] = arrived[tap * own : (tap + 1) * own].astype(F32) + twice * weight[tap].astype(F32)


def finished_weight(part, weight, factors, pieces):
    _, own, channels = weight.shape
    shares = len(pieces)
    return pl.pallas_call(
        functools.partial(finish_kernel, shares),
        out_shape=struct((9, own, channels), F32),
        in_specs=[IN_SMEM, IN_VMEM, IN_VMEM] + [IN_HBM] * shares,
        out_specs=IN_VMEM,
        scratch_shapes=[
            pltpu.VMEM((9 * own, channels), BF16),
            pltpu.SemaphoreType.DMA((shares,)),
        ],
        compiler_params=PARAMS,
        name="finished_weight",
    )(part, weight, factors, *pieces)


def row_blocks(me, parts, rows_ref, start, kind, first_channel=0):
    count = len(parts)
    blocks = count // rows_ref.shape[0]
    span = parts[0].shape[0]
    pairs = []
    channels = pl.ds(first_channel, rows_ref.shape[2])
    for x, part in zip(order(count, kind), parts):
        source = me ^ x
        at = pl.ds(start + (source % blocks) * span, span)
        pairs.append((part.at[:, channels], rows_ref.at[source // blocks, at]))
    return pairs


def rims_kernel(count, me_ref, *refs):
    parts, (first, last, arrived, sems) = refs[:count], refs[-4:]
    rows = arrived.shape[1]
    finished(started(sems, 0, row_blocks(me_ref[0], parts, arrived, 0, "mixed")))
    pairs = [
        (arrived.at[:, pl.ds(0, RIM)], first),
        (arrived.at[:, pl.ds(rows - RIM, RIM)], last),
    ]
    finished(started(sems, count, pairs))


def rims(me, parts, items, earlier):
    count = len(parts)
    span, width, columns = parts[0].shape
    rim = struct((items, RIM, width, columns), BF16)
    return pl.pallas_call(
        functools.partial(rims_kernel, count),
        out_shape=[rim, rim],
        in_specs=[IN_SMEM] + [IN_HBM] * (count + len(earlier)),
        out_specs=[IN_HBM] * 2,
        scratch_shapes=[
            pltpu.VMEM((items, span * count // items, width, columns), BF16),
            pltpu.SemaphoreType.DMA((count + 2,)),
        ],
        compiler_params=PARAMS,
        name="rims",
    )(me, *parts, *earlier)


def sinc_tile(rows, edges, wide, wide_grad, narrow):
    backward = wide_grad is not None
    spare = 1 if backward else 0
    tap = [float(value) for value in sinc_taps()[:6]]
    sums, picked = [{}, {}], {}
    for row in range(rows + 2 * RIM):
        for which, load in enumerate((wide, wide_grad) if backward else (wide,)):
            value = load(row)
            products = [value * (2.0 * tap[t]) for t in range(6)]
            for offset in range(-3, 4):
                pair = row - RIM + offset
                for parity in range(2):
                    t = 2 * offset + parity + 5
                    if -3 - spare <= pair < rows + 3 + spare and 0 <= t < 12:
                        term = products[min(t, 11 - t)]
                        key = 2 * pair + parity
                        sums[which][key] = sums[which][key] + term if key in sums[which] else term
        pair = row - RIM - 3
        if not -3 - spare <= pair < rows + 3 + spare:
            continue
        for key in (2 * pair, 2 * pair + 1):
            value = sums[0].pop(key)
            sigmoid = 0.5 + 0.5 * jnp.tanh(0.5 * value)
            result = value * sigmoid
            if backward:
                result = sums[1].pop(key) * (sigmoid + result * (1.0 - sigmoid))
            if pair < 0:
                result = result * edges[0]
            if pair >= rows:
                result = result * edges[1]
            picked[key] = result
        centre = pair - 3
        if -spare <= centre < rows + spare:
            total = None
            for t in range(6):
                term = tap[t] * (picked[2 * centre + t - 5] + picked[2 * centre + 6 - t])
                total = term if total is None else total + term
            narrow(centre + spare, total)
        for key in (2 * centre - 6, 2 * centre - 5, 2 * centre - 4):
            picked.pop(key, None)


def widened(values, up):
    columns = values.shape[-1]
    flat = values.reshape(-1, columns)
    total = jnp.dot(jnp.concatenate([flat, flat], axis=1), up, preferred_element_type=F32)
    return total.reshape(-1, GROUP, 2 * columns)


def narrowed(values, down):
    columns = values.shape[-1]
    flat = values.reshape(-1, columns)
    high = flat.astype(BF16)
    low = (flat - high.astype(F32)).astype(BF16)
    split = jnp.concatenate([high, high, low], axis=1)
    return jnp.dot(split, down, preferred_element_type=F32).reshape(-1, GROUP, columns // 2)


def filtered_rows(rows, edges, wide, wide_grad, narrow):
    lane_tiles = wide.shape[2] // 128
    first, last = edges

    def tile_step(index, carry):
        lanes = pl.ds(pl.multiple_of(lax.rem(index, lane_tiles) * 128, 128), 128)
        subs = pl.ds(pl.multiple_of(lax.div(index, lane_tiles) * 8, 8), 8)

        def store(row, value):
            narrow[row, subs, lanes] = value

        load_grad = None if wide_grad is None else lambda row: wide_grad[row, subs, lanes]
        sinc_tile(rows, (first, last), lambda row: wide[row, subs, lanes], load_grad, store)
        return carry

    lax.fori_loop(0, GROUP // 8 * lane_tiles, tile_step, 0)


def fill_wide(rows, edges, raw, scale, shift, up, wide):
    spread = widened(raw, up) * scale
    wide[:RIM] = spread[:RIM] + shift * edges[0]
    wide[RIM : RIM + rows] = spread[RIM : RIM + rows] + shift
    wide[RIM + rows :] = spread[RIM + rows :] + shift * edges[1]


def forward_sinc_kernel(count, first_channel, me_ref, edge_ref, factors, up_sums, *refs):
    before, after, up_ref, down_ref = refs[:4]
    parts, (out, raw, up, down, out_rows, wide, narrow, sems) = refs[4 : 4 + count], refs[-8:]
    items, extent, width, columns = raw.shape
    rows = extent - 2 * RIM
    edges = edge_ref[0], edge_ref[1]
    own_channels = pl.ds(first_channel, width)
    pairs = row_blocks(me_ref[0], parts, raw, RIM, "mixed", first_channel)
    pairs += [
        (up_ref, up),
        (down_ref, down),
        (before.at[:, :, own_channels], raw.at[:, pl.ds(0, RIM)]),
        (after.at[:, :, own_channels], raw.at[:, pl.ds(RIM + rows, RIM)]),
    ]
    finished(started(sems, 0, pairs))
    leaving = []
    for item in range(items):
        for group in range(width // GROUP):
            at = slice(group * GROUP, (group + 1) * GROUP)
            shift = factors[items, at] * up_sums[...]
            fill_wide(rows, edges, raw[item, :, at], factors[item, at], shift, up[...], wide)
            filtered_rows(rows, edges, wide, None, narrow)
            result = narrowed(narrow[...], down[...])
            out_rows[at, item] = jnp.swapaxes(result, 0, 1).astype(BF16)
            target = out.at[pl.ds(first_channel + group * GROUP, GROUP), item]
            source = out_rows.at[pl.ds(group * GROUP, GROUP), item]
            leaving += started(sems, len(leaving), [(source, target)])
    finished(leaving)


def forward_sinc(me, edges, factors, tables, up_sums, before, after, parts, own, out, first_channel, earlier):
    count = len(parts)
    span, _, columns = parts[0].shape
    items, width = factors.shape[0] - 1, factors.shape[1]
    rows = span * count // items
    extent = rows + 2 * RIM
    return pl.pallas_call(
        functools.partial(forward_sinc_kernel, count, first_channel),
        out_shape=struct((own, items, rows, columns), BF16),
        in_specs=[IN_SMEM, IN_SMEM] + [IN_VMEM] * 2 + [IN_HBM] * (5 + count + len(out)),
        out_specs=IN_HBM,
        input_output_aliases={9 + count: 0} if out else {},
        scratch_shapes=[
            pltpu.VMEM((items, extent, width, columns), BF16),
            pltpu.VMEM(tables[0].shape, BF16),
            pltpu.VMEM(tables[1].shape, BF16),
            pltpu.VMEM((width, items, rows, columns), BF16),
            pltpu.VMEM((extent, GROUP, 2 * columns), F32),
            pltpu.VMEM((rows, GROUP, 2 * columns), F32),
            pltpu.SemaphoreType.DMA((max(count + 4, items * width // GROUP),)),
        ],
        compiler_params=PARAMS,
        name="forward_sinc",
    )(me, edges, factors, up_sums, before, after, *tables, *parts, earlier, *out)


def backward_sinc_kernel(count, first_channel, me_ref, edge_ref, factors, up_sums, *refs):
    before, after, cotangent, up_ref, down_ref = refs[:5]
    parts, (grad_bias, grad_demod) = refs[5 : 5 + count], refs[5 + count : 7 + count]
    grad_parts = refs[7 + count : 7 + 2 * count]
    raw, cot, up, down, grad_raw, wide, wide_grad, narrow, sems = refs[7 + 2 * count :]
    me = me_ref[0]
    items, extent, width, columns = raw.shape
    rows = extent - 2 * RIM
    edges = edge_ref[0], edge_ref[1]
    own_channels = pl.ds(first_channel, width)
    pairs = row_blocks(me, parts, raw, RIM, "mixed", first_channel)
    pairs += [
        (up_ref, up),
        (down_ref, down),
        (before.at[:, :, own_channels], raw.at[:, pl.ds(0, RIM)]),
        (after.at[:, :, own_channels], raw.at[:, pl.ds(RIM + rows, RIM)]),
        (cotangent.at[:, :, own_channels], cot),
    ]
    finished(started(sems, 0, pairs))
    for item in range(items):
        for group in range(width // GROUP):
            at = slice(group * GROUP, (group + 1) * GROUP)
            scale = factors[item, at]
            fill_wide(rows, edges, raw[item, :, at], scale, factors[items, at] * up_sums[...], up[...], wide)
            wide_grad[...] = widened(cot[item, :, at], up[...])
            filtered_rows(rows, edges, wide, wide_grad, narrow)
            grad = narrowed(narrow[...], down[...])
            scaled_grad = grad * scale
            grad_raw[item, 0, at] = (scaled_grad[0] * edges[0]).astype(BF16)
            grad_raw[item, 1 : rows + 1, at] = scaled_grad[1 : rows + 1].astype(BF16)
            grad_raw[item, rows + 1, at] = (scaled_grad[rows + 1] * edges[1]).astype(BF16)
            grad = grad[1 : rows + 1]
            own = raw[item, RIM : RIM + rows, at].astype(F32)
            grad_bias[item, at] = jnp.sum(jnp.sum(grad, axis=0), axis=1, keepdims=True)
            grad_demod[item, at] = jnp.sum(jnp.sum(grad * own, axis=0), axis=1, keepdims=True)
    blocks = count // items
    span = rows // blocks
    pairs = []
    kind = "near" if width < cotangent.shape[2] else "far"
    for x, part in zip(order(count, kind), grad_parts):
        dest = me ^ x
        pairs.append((grad_raw.at[dest // blocks, pl.ds((dest % blocks) * span, span + 2)], part))
    finished(started(sems, 0, pairs))


def backward_sinc(me, edges, factors, tables, up_sums, before, after, cotangent, parts, first_channel):
    count = len(parts)
    items, extent, _, columns = cotangent.shape
    span, width = parts[0].shape[0], factors.shape[1]
    rows = extent - 2 * RIM
    wide = pltpu.VMEM((extent, GROUP, 2 * columns), F32)
    outs = pl.pallas_call(
        functools.partial(backward_sinc_kernel, count, first_channel),
        out_shape=[struct((items, width, 1), F32)] * 2 + [struct((span + 2, width, columns), BF16)] * count,
        in_specs=[IN_SMEM, IN_SMEM] + [IN_VMEM] * 2 + [IN_HBM] * (5 + count),
        out_specs=[IN_VMEM, IN_VMEM] + [IN_HBM] * count,
        scratch_shapes=[
            pltpu.VMEM((items, extent, width, columns), BF16),
            pltpu.VMEM((items, extent, width, columns), BF16),
            pltpu.VMEM(tables[0].shape, BF16),
            pltpu.VMEM(tables[1].shape, BF16),
            pltpu.VMEM((items, rows + 2, width, columns), BF16),
            wide,
            wide,
            pltpu.VMEM((rows + 2, GROUP, 2 * columns), F32),
            pltpu.SemaphoreType.DMA((count + 5,)),
        ],
        compiler_params=PARAMS,
        name="backward_sinc",
    )(me, edges, factors, up_sums, before, after, cotangent, *tables, *parts)
    return outs[0], outs[1], outs[2:]


def scale_kernel(count, me_ref, scales, *refs):
    parts, (out, arrived, results, sems) = refs[:count], refs[count:]
    width, items, _, _ = out.shape
    finished(started(sems, 0, row_blocks(me_ref[0], parts, arrived, 0, "far")))
    leaving = []
    for item in range(items):
        for group in range(width // GROUP):
            at = slice(group * GROUP, (group + 1) * GROUP)
            value = arrived[item, :, at].astype(F32) * scales[item, at]
            results[at, item] = jnp.swapaxes(value, 0, 1)
            spot = pl.ds(group * GROUP, GROUP)
            leaving += started(sems, len(leaving), [(results.at[spot, item], out.at[spot, item])])
    finished(leaving)


def scaled(me, scales, parts, items):
    count = len(parts)
    span, width, columns = parts[0].shape
    rows = span * count // items
    return pl.pallas_call(
        functools.partial(scale_kernel, count),
        out_shape=struct((width, items, rows, columns), F32),
        in_specs=[IN_SMEM, IN_VMEM] + [IN_HBM] * count,
        out_specs=IN_HBM,
        scratch_shapes=[
            pltpu.VMEM((items, rows, width, columns), BF16),
            pltpu.VMEM((width, items, rows, columns), F32),
            pltpu.SemaphoreType.DMA((max(count, items * width // GROUP),)),
        ],
        compiler_params=PARAMS,
        name="scale_features",
    )(me, scales, *parts)


def in_thirds(value, lanes):
    terms = []
    for _ in range(3):
        terms.append(lax.reduce_precision(value, 8, 7))
        value = value - terms[-1]
    rows = jnp.stack(terms).astype(BF16).reshape(-1, lanes)
    return jnp.pad(rows, ((0, -rows.shape[0] % 16), (0, 0)))


def from_thirds(rows, shape):
    terms = rows.astype(F32).reshape(-1)[: 3 * shape[0] * shape[1]].reshape((3,) + shape)
    return terms[0] + terms[1] + terms[2]


def tree_sum(values):
    while len(values) > 1:
        values = [a + b for a, b in zip(values[::2], values[1::2])]
    return values[0]


def per_device(
    features,
    latent,
    affine,
    affine_bias,
    weight,
    out_bias,
    cotangent,
    latents_all,
    labels,
    class_means,
):
    highest = lax.Precision.HIGHEST
    own, items, rows, columns = features.shape
    channels = weight.shape[3]
    count = lax.axis_size("chan")
    dp_total = lax.axis_size("dp")
    me = lax.axis_index("chan")
    me_dp = lax.axis_index("dp")
    me_ref = me.astype(jnp.int32)[None]
    blocks = count // items
    span = rows // blocks
    split = max(1, min(2, own // GROUP))
    width = own // split

    styles = jnp.dot(latent, affine, preferred_element_type=F32) + affine_bias
    own_style = lax.dynamic_slice_in_dim(styles, me * own, own, 1)
    weight_full = weight.astype(F32)
    weight_sq = jnp.sum(weight_full * weight_full, axis=(0, 1))
    demod = lax.rsqrt(jnp.dot(styles * styles, weight_sq.T, precision=highest) + 1e-08)
    item = me // blocks
    item_scales = lax.dynamic_index_in_dim(styles, item, 0, keepdims=False).reshape(count, own, 1)

    before, after = from_neighbours(features, "dp", 2, 1)
    prepared = row_parts(me_ref, before, features, after, count)
    feats = exchange(prepared, "far")
    held, places = near_pieces(*weight_pieces(once(weight, prepared[0]), me_dp))
    shares = channels // held.shape[3]
    part = (me_dp % shares).astype(jnp.int32)[None]
    held = once(held, *feats[1:3], item_scales, demod)
    bit = shares // 2
    while bit > 1:
        met, met_places = met_pieces(held, places, bit)
        held, places = jnp.concatenate([held, met], axis=0), places + met_places
        bit //= 2
    cot_before, cot_after = from_neighbours(once(cotangent, feats[3]), "dp", 2, RIM)
    held = once(held, *feats[3:7])
    met, met_places = met_pieces(held, places, 1)
    pieces, places = [held, met], (tuple(places), tuple(met_places))

    table = up_table(columns)
    down_halves = halves(0.5 * table.T)
    tables = [np.concatenate(halves(table)), np.concatenate(down_halves + down_halves[:1])]
    up_sums = np.sum(table, axis=0)[None]
    edges = jnp.stack([me_dp > 0, me_dp < dp_total - 1]).astype(F32)

    item_scales = once(item_scales, cot_before, cot_after)
    raw_parts = conv_forward(me_ref, part, pieces, places, item_scales, feats)
    taps_backward = transposed_taps(
        me_ref, part, [once(piece, raw_parts[0]) for piece in pieces], places, channels
    )
    all_maps, grad_parts, bias_parts, demod_parts = [], [], [], []
    factors = jnp.concatenate([demod, out_bias[None]])[:, :, None]
    up = [(i, i + 1) for i in range(dp_total - 1)]
    down = [(j, i) for i, j in up]
    arrived = exchange(raw_parts, "mixed")
    cot = jnp.concatenate([cot_before, cotangent, cot_after], axis=2)
    cot = jnp.transpose(cot, (1, 2, 0, 3))
    head, tail = rims(me_ref, arrived, items, [taps_backward, cot])
    before, after = lax.ppermute(tail, "dp", up), lax.ppermute(head, "dp", down)
    for h in range(split):
        at = slice(h * width, (h + 1) * width)
        maps = (factors[:, at], tables, up_sums, before, after)
        all_maps.append(maps)
        bias_part, demod_part, parts = backward_sinc(
            me_ref, edges, *maps, cot, arrived, h * width
        )
        bias_parts.append(bias_part)
        demod_parts.append(demod_part)
        if h:
            parts = [once(part, *grad_parts[-4:]) for part in parts]
        grad_parts += exchange(parts, "near" if split > 1 else "far")
    bias_part = jnp.sum(jnp.concatenate(bias_parts, axis=1)[:, :, 0], axis=0)
    g_demod = jnp.concatenate(demod_parts, axis=1)[:, :, 0]

    output = [forward_sinc(me_ref, edges, *all_maps[0], arrived, own, [], 0, bias_parts[-1])]
    modded_parts, style_part, weight_sums = conv_backward(
        me_ref, item_scales, taps_backward, output[0], grad_parts, feats, dp_total
    )
    modded_parts = exchange(modded_parts, "far")
    for h in range(1, split):
        output = [forward_sinc(me_ref, edges, *all_maps[h], arrived, own, output, h * width, style_part)]
    output = output[0]
    grad_features = scaled(me_ref, own_style[:, :, None], modded_parts, items)

    grad_bias, g_demod_sum = lax.psum((once(bias_part, style_part), g_demod), "dp")
    cube = demod * demod * demod
    g_style_part = 2.0 * styles * jnp.dot(-0.5 * g_demod * cube, weight_sq, precision=highest)
    g_style_part = g_style_part + jnp.where(
        jnp.arange(items)[:, None] == item, style_part.reshape(1, channels), 0.0
    )
    g_wsq = jnp.dot((-0.5 * g_demod_sum * cube).T, styles * styles, precision=highest)

    tags = jnp.stack([labels // 64, labels % 64], axis=1).astype(BF16)
    tagged = jnp.concatenate([once(latents_all, head), jnp.pad(tags, ((0, 0), (0, 126)))], axis=1)
    tagged = lax.all_gather(tagged, ("dp", "chan"), axis=0, tiled=True)
    all_latents, tags = tagged[:, :-128], tagged[:, -128:-126].astype(F32)
    all_labels = (tags[:, 0] * 64.0 + tags[:, 1]).astype(jnp.int32)
    one_hot = all_labels[None, :] == jnp.arange(class_means.shape[0])[:, None]
    class_sums = jnp.dot(one_hot.astype(BF16), all_latents, preferred_element_type=F32)
    counts = jnp.sum(one_hot.astype(F32), axis=1)
    target = jnp.where(
        counts[:, None] > 0, class_sums / jnp.maximum(counts, 1.0)[:, None], class_means
    )

    share = channels // dp_total
    weight_sums = weight_sums.reshape(dp_total * 9 * channels, share)
    weight_sums = lax.psum_scatter(weight_sums, "dp", scatter_dimension=0, tiled=True)
    weight_sums = once(weight_sums.reshape(9, channels, share), *modded_parts, g_wsq, grad_bias, target, output)
    thirds = in_thirds(g_style_part, share)
    sent = []
    for x in order(count, "mixed"):
        part_x = lax.dynamic_slice_in_dim(weight_sums, (me ^ x) * own, own, 1)
        sent.append(jnp.concatenate([part_x.reshape(9 * own, share), thirds], axis=0))
    sent = exchange(sent, "mixed")
    g_weight = sum(value[: 9 * own].astype(F32) for value in sent).astype(BF16)
    style_sums = [from_thirds(value[9 * own :], styles.shape) for value in sent]
    g_style = tree_sum([style_sums[order(count, "mixed").index(x)] for x in range(count)])
    sent = once(jnp.concatenate([g_weight, in_thirds(g_style, share)], axis=0), grad_features)
    met = [sent] + [swapped(sent, "dp", x) for x in range(1, dp_total)]
    if share % 128 == 0:
        me_dp_ref = me_dp.astype(jnp.int32)[None]
        grad_weight = finished_weight(me_dp_ref, weight.reshape(9, own, channels), g_wsq, met)
    else:
        blocks = lax.all_gather(met[0][: 9 * own], "dp", axis=1, tiled=True)
        grad_weight = blocks.reshape(9, own, channels).astype(F32)
        grad_weight = grad_weight + 2.0 * weight_full.reshape(9, own, channels) * g_wsq
    grad_weight = grad_weight.reshape(weight.shape)
    g_style = tree_sum([from_thirds(value[9 * own :], styles.shape) for value in met])
    grad_affine_bias = jnp.sum(g_style, axis=0)
    grad_affine = jnp.dot(latent.astype(F32).T, g_style, precision=highest)
    grad_latent = jnp.dot(g_style, affine.astype(F32).T, precision=highest)
    return (
        output,
        grad_features,
        grad_latent,
        grad_affine,
        grad_affine_bias,
        grad_weight,
        grad_bias,
        target,
    )


def solution(mesh):
    in_specs = (
        P("chan", None, "dp", None),
        P(),
        P(),
        P(),
        P(None, None, "chan", None),
        P("chan"),
        P("chan", None, "dp", None),
        P(("dp", "chan"), None),
        P(("dp", "chan")),
        P(),
    )
    out_specs = (
        P("chan", None, "dp", None),
        P("chan", None, "dp", None),
        P(),
        P(),
        P(),
        P(None, None, "chan", None),
        P("chan"),
        P(),
    )
    return jax.shard_map(
        per_device, mesh=mesh, in_specs=in_specs, out_specs=out_specs, check_vma=False
    )
```

```python
import functools

import jax
import jax.numpy as jnp
import ml_dtypes
import numpy as np
from jax import lax
from jax.experimental import pallas as pl
from jax.experimental.pallas import tpu as pltpu
from jax.sharding import PartitionSpec as P

F32 = jnp.float32
BF16 = jnp.bfloat16
IN_VMEM = pl.BlockSpec(memory_space=pltpu.VMEM)
IN_HBM = pl.BlockSpec(memory_space=pltpu.HBM)
IN_SMEM = pl.BlockSpec(memory_space=pltpu.SMEM)
PARAMS = pltpu.CompilerParams(vmem_limit_bytes=60 << 20)
RIM = 7
GROUP = 16


def struct(shape, dtype):
    return jax.ShapeDtypeStruct(shape, dtype)


def sinc_taps():
    offset = np.arange(12) - 5.5
    values = np.sinc(offset * 0.5) * (0.5 + 0.5 * np.cos(np.pi * offset / 6.0))
    return values / values.sum()


def up_table(size):
    tap = np.arange(2 * size)[None, :] - 2 * np.arange(size)[:, None] + 5
    held = (tap >= 0) & (tap < 12)
    return np.where(held, 2.0 * sinc_taps()[np.clip(tap, 0, 11)], 0.0).astype(np.float32)


def halves(table):
    high = table.astype(ml_dtypes.bfloat16)
    return [high, (table - high.astype(np.float32)).astype(ml_dtypes.bfloat16)]


def from_neighbours(value, axis, dim, width):
    size, length = lax.axis_size(axis), value.shape[dim]
    up = [(i, i + 1) for i in range(size - 1)]
    down = [(j, i) for i, j in up]
    last = lax.slice_in_dim(value, length - width, length, axis=dim)
    first = lax.slice_in_dim(value, 0, width, axis=dim)
    return lax.ppermute(last, axis, up), lax.ppermute(first, axis, down)


def swapped(value, axis, bits):
    return lax.ppermute(value, axis, [(i, i ^ bits) for i in range(lax.axis_size(axis))])


def once(value, *others):
    return lax.optimization_barrier((value,) + others)[0]


def order(count, kind):
    far, near = list(range(4, count)), list(range(1, min(4, count)))
    if kind == "far":
        return [0] + far + near
    if kind == "near":
        return [0] + near + far
    mixed = [x for pair in zip(far, near) for x in pair]
    return [0] + mixed + far[len(near) :] + near[len(far) :]


def exchange(parts, kind):
    steps = order(lax.axis_size("chan"), kind)
    return [parts[0]] + [swapped(part, "chan", x) for part, x in zip(parts[1:], steps[1:])]


def started(sems, first, pairs):
    copies = [
        pltpu.make_async_copy(source, target, sems.at[first + index])
        for index, (source, target) in enumerate(pairs)
    ]
    for copy in copies:
        copy.start()
    return copies


def finished(copies):
    for copy in copies:
        copy.wait()


def rows_kernel(count, me_ref, before, value, after, *refs):
    parts, (arrived, rows_first, sems) = refs[:count], refs[count:]
    me = me_ref[0]
    width, items, rows, _ = value.shape
    blocks = count // items
    span = rows // blocks
    finished(started(sems, 0, [(value, arrived)]))
    for item in range(items):
        for group in range(width // GROUP):
            at = slice(group * GROUP, (group + 1) * GROUP)
            rows_first[item, 1 : rows + 1, at] = jnp.swapaxes(arrived[at, item], 0, 1)
        rows_first[item, 0] = before[:, item, 0]
        rows_first[item, rows + 1] = after[:, item, 0]
    pairs = []
    for x, part in zip(order(count, "far"), parts):
        dest = me ^ x
        start = (dest % blocks) * span
        pairs.append((rows_first.at[dest // blocks, pl.ds(start, span + 2)], part))
    finished(started(sems, 1, pairs))


def row_parts(me, before, value, after, count):
    width, items, rows, columns = value.shape
    span = rows * items // count
    return pl.pallas_call(
        functools.partial(rows_kernel, count),
        out_shape=[struct((span + 2, width, columns), BF16)] * count,
        in_specs=[IN_SMEM, IN_VMEM, IN_HBM, IN_VMEM],
        out_specs=[IN_HBM] * count,
        scratch_shapes=[
            pltpu.VMEM((width, items, rows, columns), BF16),
            pltpu.VMEM((items, rows + 2, width, columns), BF16),
            pltpu.SemaphoreType.DMA((1 + count,)),
        ],
        compiler_params=PARAMS,
        name="row_parts",
    )(me, before, value, after)


def weight_pieces(weight, me_dp):
    shares = min(lax.axis_size("dp"), weight.shape[3] // 128)
    share = weight.shape[3] // shares
    held = lax.dynamic_slice_in_dim(weight, me_dp % shares * share, share, 3).reshape(1, 9, -1, share)
    places = [(0, 0)]
    bit = lax.axis_size("chan") // 2
    while bit >= 4:
        held = jnp.concatenate([held, swapped(held, "chan", bit)], axis=0)
        places += [(chan ^ bit, dp) for chan, dp in places]
        bit //= 2
    return held, places


def near_pieces(held, places):
    near = range(1, min(lax.axis_size("chan"), 4))
    held = jnp.concatenate([held] + [swapped(held, "chan", x) for x in near], axis=0)
    return held, places + [(chan ^ x, dp) for x in near for chan, dp in places]


def met_pieces(held, places, bit):
    return swapped(held, "dp", bit), [(chan, dp ^ bit) for chan, dp in places]


def tap_blocks(me, part, pieces, places, taps):
    share = pieces[0].shape[3]
    pairs = []
    for piece, blocks in zip(pieces, places):
        for index, (chan, dp) in enumerate(blocks):
            lanes = pl.ds(pl.multiple_of((part ^ dp) * share, share), share)
            pairs.append((piece.at[index], taps.at[:, me ^ chan, :, lanes]))
    return pairs


def transposed_kernel(places, me_ref, part_ref, *refs):
    pieces, (out, taps, turned, sems) = refs[:-4], refs[-4:]
    pairs = tap_blocks(me_ref[0], part_ref[0], pieces, places, taps)
    finished(started(sems, 0, pairs))
    channels = taps.shape[3]
    copies = []
    for tap in range(9):
        turned[8 - tap] = jnp.transpose(taps[tap].reshape(channels, channels))
        copies += started(sems, len(pairs) + tap, [(turned.at[8 - tap], out.at[8 - tap])])
    finished(copies)


def transposed_taps(me, part, pieces, places, channels):
    own = pieces[0].shape[2]
    blocks = sum(len(place) for place in places)
    return pl.pallas_call(
        functools.partial(transposed_kernel, places),
        out_shape=struct((9, channels, channels), BF16),
        in_specs=[IN_SMEM, IN_SMEM] + [IN_HBM] * len(pieces),
        out_specs=IN_HBM,
        scratch_shapes=[
            pltpu.VMEM((9, channels // own, own, channels), BF16),
            pltpu.VMEM((9, channels, channels), BF16),
            pltpu.SemaphoreType.DMA((blocks + 9,)),
        ],
        compiler_params=PARAMS,
        name="transposed_taps",
    )(me, part, *pieces)


def arrivals(me, parts, arrived):
    count, _, own, _ = arrived.shape
    width = parts[0].shape[1]
    steps = order(count, "near" if width < own else "far")
    return [
        (part, arrived.at[me ^ steps[index % count], :, pl.ds(index // count * width, width)])
        for index, part in enumerate(parts)
    ]


def departures(me, results, outs, kind):
    count = results.shape[1]
    return [(results.at[:, me ^ x], out) for x, out in zip(order(count, kind), outs)]


def fill_shifted(arrived, scales, shifted):
    count, rows, own, columns = arrived.shape

    def row_step(row, carry):
        column = lax.broadcasted_iota(jnp.int32, (own, columns), 1)
        for source in range(count):
            value = arrived[source, row].astype(F32)
            if scales is not None:
                value = (value * scales[source]).astype(BF16).astype(F32)
            before = jnp.where(column == 0, 0.0, pltpu.roll(value, 1, 1))
            after = jnp.where(column == columns - 1, 0.0, pltpu.roll(value, columns - 1, 1))
            shifted[row, 0, source] = before.astype(BF16)
            shifted[row, 1, source] = value.astype(BF16)
            shifted[row, 2, source] = after.astype(BF16)
        return carry

    lax.fori_loop(0, rows, row_step, 0, unroll=2)


def convolved(taps, shifted, row, channels, columns):
    total = None
    for i in range(3):
        for j in range(3):
            term = jnp.dot(
                taps[3 * i + j].reshape(channels, channels),
                shifted[row + i, j].reshape(channels, columns),
                preferred_element_type=F32,
            )
            total = term if total is None else total + term
    return total


def forward_kernel(count, places, me_ref, part_ref, scales, *refs):
    pieces, refs = refs[: len(places)], refs[len(places) :]
    parts, outs = refs[:count], refs[count:-7]
    arrived, shifted, taps, results, wide_scales, sems, row_sems = refs[-7:]
    me = me_ref[0]
    rows, _, own, columns = results.shape
    arriving = started(sems, 0, arrivals(me, parts, arrived))
    tapping = started(sems, count, tap_blocks(me, part_ref[0], pieces, places, taps))
    wide_scales[...] = jnp.broadcast_to(scales[...], wide_scales.shape)
    finished(arriving)
    fill_shifted(arrived, wide_scales, shifted)
    finished(tapping)

    def leaving(row):
        return [
            pltpu.make_async_copy(results.at[row, me ^ x], out.at[row], row_sems.at[row, x])
            for x, out in zip(order(count, "mixed"), outs)
        ]

    def row_step(row, carry):
        total = convolved(taps, shifted, row, count * own, columns)
        results[row] = total.astype(BF16).reshape(count, own, columns)
        for copy in leaving(row):
            copy.start()
        return carry

    lax.fori_loop(0, rows, row_step, 0, unroll=min(4, rows))
    for row in range(rows):
        finished(leaving(row))


def conv_forward(me, part, pieces, places, scales, parts):
    count = len(parts)
    rows, own, columns = parts[0].shape
    blocks = sum(len(place) for place in places)
    return pl.pallas_call(
        functools.partial(forward_kernel, count, places),
        out_shape=[struct((rows - 2, own, columns), BF16)] * count,
        in_specs=[IN_SMEM, IN_SMEM, IN_VMEM] + [IN_HBM] * (len(pieces) + count),
        out_specs=[IN_HBM] * count,
        scratch_shapes=[
            pltpu.VMEM((count, rows, own, columns), BF16),
            pltpu.VMEM((rows, 3, count, own, columns), BF16),
            pltpu.VMEM((9, count, own, count * own), BF16),
            pltpu.VMEM((rows - 2, count, own, columns), BF16),
            pltpu.VMEM((count, own, columns), F32),
            pltpu.SemaphoreType.DMA((count + blocks,)),
            pltpu.SemaphoreType.DMA((rows - 2, count)),
        ],
        compiler_params=PARAMS,
        name="conv_forward",
    )(me, part, scales, *pieces, *parts)


def backward_kernel(count, split, me_ref, scales, taps_ref, _, *refs):
    grads, refs = refs[: count * split], refs[count * split :]
    feats, outs, (style_ref, weight_out) = refs[:count], refs[count : 2 * count], refs[2 * count : 2 * count + 2]
    arrived, arrived_feats, shifted, modded, taps, results, weight_sums, wide_scales, sems = refs[2 * count + 2 :]
    me = me_ref[0]
    rows, _, own, columns = results.shape
    channels = count * own
    shares, _, _, share = weight_sums.shape
    arriving = started(sems, 0, arrivals(me, grads, arrived))
    tapping = started(
        sems,
        count * split,
        [(taps_ref, taps)] + arrivals(me, feats, arrived_feats),
    )
    wide_scales[...] = jnp.broadcast_to(scales[...], wide_scales.shape)
    finished(arriving)
    fill_shifted(arrived, None, shifted)
    finished(tapping)
    style_ref[...] = jnp.zeros_like(style_ref)

    def row_step(row, carry):
        total = convolved(taps, shifted, row, channels, columns).reshape(count, own, columns)
        results[row] = total.astype(BF16)
        product = total * arrived_feats[:, row + 1].astype(F32)
        style_ref[...] += jnp.sum(product, axis=2, keepdims=True)
        return carry

    lax.fori_loop(0, rows, row_step, 0, unroll=min(4, rows))
    leaving = started(sems, 0, departures(me, results, outs, "far"))

    def modded_step(row, carry):
        for source in range(count):
            value = arrived_feats[source, row].astype(F32) * wide_scales[source]
            modded[row, source] = value.astype(BF16)
        return carry

    lax.fori_loop(0, rows + 2, modded_step, 0)

    def weight_leaving(tap):
        return pltpu.make_async_copy(weight_sums.at[:, tap], weight_out.at[:, tap], sems.at[count + tap])

    def tap_step(tap, carry):
        i, j = lax.div(tap, 3), lax.rem(tap, 3)
        total = None
        for row in range(rows):
            term = lax.dot_general(
                shifted[row + 1, 2 - j].reshape(channels, columns),
                modded[row + i].reshape(channels, columns),
                (((1,), (1,)), ((), ())),
                preferred_element_type=F32,
            )
            total = term if total is None else total + term
        total = total.astype(BF16)
        for index in range(shares):
            weight_sums[index, tap] = total[:, index * share : (index + 1) * share]
        weight_leaving(tap).start()
        return carry

    lax.fori_loop(0, 9, tap_step, 0, unroll=3)
    finished(leaving + [weight_leaving(tap) for tap in range(9)])


def conv_backward(me, scales, taps, earlier, grads, feats, shares):
    count = len(feats)
    split = len(grads) // count
    rows, own, columns = feats[0].shape
    channels = count * own
    share = channels // shares
    outs = pl.pallas_call(
        functools.partial(backward_kernel, count, split),
        out_shape=[struct((rows - 2, own, columns), BF16)] * count
        + [struct((count, own, 1), F32), struct((shares, 9, channels, share), BF16)],
        in_specs=[IN_SMEM, IN_VMEM] + [IN_HBM] * (2 + len(grads) + count),
        out_specs=[IN_HBM] * count + [IN_VMEM, IN_HBM],
        scratch_shapes=[
            pltpu.VMEM((count, rows, own, columns), BF16),
            pltpu.VMEM((count, rows, own, columns), BF16),
            pltpu.VMEM((rows, 3, count, own, columns), BF16),
            pltpu.VMEM((rows, count, own, columns), BF16),
            pltpu.VMEM((9, channels, channels), BF16),
            pltpu.VMEM((rows - 2, count, own, columns), BF16),
            pltpu.VMEM((shares, 9, channels, share), BF16),
            pltpu.VMEM((count, own, columns), F32),
            pltpu.SemaphoreType.DMA((count + max(9, len(grads) + 1),)),
        ],
        compiler_params=PARAMS,
        name="conv_backward",
    )(me, scales, taps, earlier, *grads, *feats)
    return outs[:-2], outs[-2], outs[-1]


def finish_kernel(shares, part_ref, weight, factors, *refs):
    pieces, (out, arrived, sems) = refs[:shares], refs[shares:]
    part = part_ref[0]
    share = pieces[0].shape[1]
    taps, own, _ = out.shape
    pairs = []
    for x, piece in enumerate(pieces):
        lanes = pl.ds(pl.multiple_of((part ^ x) * share, share), share)
        pairs.append((piece.at[pl.ds(0, taps * own)], arrived.at[:, lanes]))
    finished(started(sems, 0, pairs))
    twice = 2.0 * factors[...]
    for tap in range(taps):
        out[tap] = arrived[tap * own : (tap + 1) * own].astype(F32) + twice * weight[tap].astype(F32)


def finished_weight(part, weight, factors, pieces):
    _, own, channels = weight.shape
    shares = len(pieces)
    return pl.pallas_call(
        functools.partial(finish_kernel, shares),
        out_shape=struct((9, own, channels), F32),
        in_specs=[IN_SMEM, IN_VMEM, IN_VMEM] + [IN_HBM] * shares,
        out_specs=IN_VMEM,
        scratch_shapes=[
            pltpu.VMEM((9 * own, channels), BF16),
            pltpu.SemaphoreType.DMA((shares,)),
        ],
        compiler_params=PARAMS,
        name="finished_weight",
    )(part, weight, factors, *pieces)


def row_blocks(me, parts, rows_ref, start, kind, first_channel=0):
    count = len(parts)
    blocks = count // rows_ref.shape[0]
    span = parts[0].shape[0]
    pairs = []
    channels = pl.ds(first_channel, rows_ref.shape[2])
    for x, part in zip(order(count, kind), parts):
        source = me ^ x
        at = pl.ds(start + (source % blocks) * span, span)
        pairs.append((part.at[:, channels], rows_ref.at[source // blocks, at]))
    return pairs


def rims_kernel(count, me_ref, *refs):
    parts, (first, last, arrived, sems) = refs[:count], refs[-4:]
    rows = arrived.shape[1]
    finished(started(sems, 0, row_blocks(me_ref[0], parts, arrived, 0, "mixed")))
    pairs = [
        (arrived.at[:, pl.ds(0, RIM)], first),
        (arrived.at[:, pl.ds(rows - RIM, RIM)], last),
    ]
    finished(started(sems, count, pairs))


def rims(me, parts, items, earlier):
    count = len(parts)
    span, width, columns = parts[0].shape
    rim = struct((items, RIM, width, columns), BF16)
    return pl.pallas_call(
        functools.partial(rims_kernel, count),
        out_shape=[rim, rim],
        in_specs=[IN_SMEM] + [IN_HBM] * (count + len(earlier)),
        out_specs=[IN_HBM] * 2,
        scratch_shapes=[
            pltpu.VMEM((items, span * count // items, width, columns), BF16),
            pltpu.SemaphoreType.DMA((count + 2,)),
        ],
        compiler_params=PARAMS,
        name="rims",
    )(me, *parts, *earlier)


def sinc_tile(rows, edges, wide, wide_grad, narrow):
    backward = wide_grad is not None
    spare = 1 if backward else 0
    tap = [float(value) for value in sinc_taps()[:6]]
    sums, picked = [{}, {}], {}
    for row in range(rows + 2 * RIM):
        for which, load in enumerate((wide, wide_grad) if backward else (wide,)):
            value = load(row)
            products = [value * (2.0 * tap[t]) for t in range(6)]
            for offset in range(-3, 4):
                pair = row - RIM + offset
                for parity in range(2):
                    t = 2 * offset + parity + 5
                    if -3 - spare <= pair < rows + 3 + spare and 0 <= t < 12:
                        term = products[min(t, 11 - t)]
                        key = 2 * pair + parity
                        sums[which][key] = sums[which][key] + term if key in sums[which] else term
        pair = row - RIM - 3
        if not -3 - spare <= pair < rows + 3 + spare:
            continue
        for key in (2 * pair, 2 * pair + 1):
            value = sums[0].pop(key)
            sigmoid = 0.5 + 0.5 * jnp.tanh(0.5 * value)
            result = value * sigmoid
            if backward:
                result = sums[1].pop(key) * (sigmoid + result * (1.0 - sigmoid))
            if pair < 0:
                result = result * edges[0]
            if pair >= rows:
                result = result * edges[1]
            picked[key] = result
        centre = pair - 3
        if -spare <= centre < rows + spare:
            total = None
            for t in range(6):
                term = tap[t] * (picked[2 * centre + t - 5] + picked[2 * centre + 6 - t])
                total = term if total is None else total + term
            narrow(centre + spare, total)
        for key in (2 * centre - 6, 2 * centre - 5, 2 * centre - 4):
            picked.pop(key, None)


def widened(values, up):
    columns = values.shape[-1]
    flat = values.reshape(-1, columns)
    total = jnp.dot(jnp.concatenate([flat, flat], axis=1), up, preferred_element_type=F32)
    return total.reshape(-1, GROUP, 2 * columns)


def narrowed(values, down):
    columns = values.shape[-1]
    flat = values.reshape(-1, columns)
    high = flat.astype(BF16)
    low = (flat - high.astype(F32)).astype(BF16)
    split = jnp.concatenate([high, high, low], axis=1)
    return jnp.dot(split, down, preferred_element_type=F32).reshape(-1, GROUP, columns // 2)


def filtered_rows(rows, edges, wide, wide_grad, narrow):
    lane_tiles = wide.shape[2] // 128
    first, last = edges

    def tile_step(index, carry):
        lanes = pl.ds(pl.multiple_of(lax.rem(index, lane_tiles) * 128, 128), 128)
        subs = pl.ds(pl.multiple_of(lax.div(index, lane_tiles) * 8, 8), 8)

        def store(row, value):
            narrow[row, subs, lanes] = value

        load_grad = None if wide_grad is None else lambda row: wide_grad[row, subs, lanes]
        sinc_tile(rows, (first, last), lambda row: wide[row, subs, lanes], load_grad, store)
        return carry

    lax.fori_loop(0, GROUP // 8 * lane_tiles, tile_step, 0)


def fill_wide(rows, edges, raw, scale, shift, up, wide):
    spread = widened(raw, up) * scale
    wide[:RIM] = spread[:RIM] + shift * edges[0]
    wide[RIM : RIM + rows] = spread[RIM : RIM + rows] + shift
    wide[RIM + rows :] = spread[RIM + rows :] + shift * edges[1]


def forward_sinc_kernel(count, first_channel, me_ref, edge_ref, factors, up_sums, *refs):
    before, after, up_ref, down_ref = refs[:4]
    parts, (out, raw, up, down, out_rows, wide, narrow, sems) = refs[4 : 4 + count], refs[-8:]
    items, extent, width, columns = raw.shape
    rows = extent - 2 * RIM
    edges = edge_ref[0], edge_ref[1]
    own_channels = pl.ds(first_channel, width)
    pairs = row_blocks(me_ref[0], parts, raw, RIM, "mixed", first_channel)
    pairs += [
        (up_ref, up),
        (down_ref, down),
        (before.at[:, :, own_channels], raw.at[:, pl.ds(0, RIM)]),
        (after.at[:, :, own_channels], raw.at[:, pl.ds(RIM + rows, RIM)]),
    ]
    finished(started(sems, 0, pairs))
    leaving = []
    for item in range(items):
        for group in range(width // GROUP):
            at = slice(group * GROUP, (group + 1) * GROUP)
            shift = factors[items, at] * up_sums[...]
            fill_wide(rows, edges, raw[item, :, at], factors[item, at], shift, up[...], wide)
            filtered_rows(rows, edges, wide, None, narrow)
            result = narrowed(narrow[...], down[...])
            out_rows[at, item] = jnp.swapaxes(result, 0, 1).astype(BF16)
            target = out.at[pl.ds(first_channel + group * GROUP, GROUP), item]
            source = out_rows.at[pl.ds(group * GROUP, GROUP), item]
            leaving += started(sems, len(leaving), [(source, target)])
    finished(leaving)


def forward_sinc(me, edges, factors, tables, up_sums, before, after, parts, own, out, first_channel, earlier):
    count = len(parts)
    span, _, columns = parts[0].shape
    items, width = factors.shape[0] - 1, factors.shape[1]
    rows = span * count // items
    extent = rows + 2 * RIM
    return pl.pallas_call(
        functools.partial(forward_sinc_kernel, count, first_channel),
        out_shape=struct((own, items, rows, columns), BF16),
        in_specs=[IN_SMEM, IN_SMEM] + [IN_VMEM] * 2 + [IN_HBM] * (5 + count + len(out)),
        out_specs=IN_HBM,
        input_output_aliases={9 + count: 0} if out else {},
        scratch_shapes=[
            pltpu.VMEM((items, extent, width, columns), BF16),
            pltpu.VMEM(tables[0].shape, BF16),
            pltpu.VMEM(tables[1].shape, BF16),
            pltpu.VMEM((width, items, rows, columns), BF16),
            pltpu.VMEM((extent, GROUP, 2 * columns), F32),
            pltpu.VMEM((rows, GROUP, 2 * columns), F32),
            pltpu.SemaphoreType.DMA((max(count + 4, items * width // GROUP),)),
        ],
        compiler_params=PARAMS,
        name="forward_sinc",
    )(me, edges, factors, up_sums, before, after, *tables, *parts, earlier, *out)


def backward_sinc_kernel(count, first_channel, me_ref, edge_ref, factors, up_sums, *refs):
    before, after, cotangent, up_ref, down_ref = refs[:5]
    parts, (grad_bias, grad_demod) = refs[5 : 5 + count], refs[5 + count : 7 + count]
    grad_parts = refs[7 + count : 7 + 2 * count]
    raw, cot, up, down, grad_raw, wide, wide_grad, narrow, sems = refs[7 + 2 * count :]
    me = me_ref[0]
    items, extent, width, columns = raw.shape
    rows = extent - 2 * RIM
    edges = edge_ref[0], edge_ref[1]
    own_channels = pl.ds(first_channel, width)
    pairs = row_blocks(me, parts, raw, RIM, "mixed", first_channel)
    pairs += [
        (up_ref, up),
        (down_ref, down),
        (before.at[:, :, own_channels], raw.at[:, pl.ds(0, RIM)]),
        (after.at[:, :, own_channels], raw.at[:, pl.ds(RIM + rows, RIM)]),
        (cotangent.at[:, :, own_channels], cot),
    ]
    finished(started(sems, 0, pairs))
    for item in range(items):
        for group in range(width // GROUP):
            at = slice(group * GROUP, (group + 1) * GROUP)
            scale = factors[item, at]
            fill_wide(rows, edges, raw[item, :, at], scale, factors[items, at] * up_sums[...], up[...], wide)
            wide_grad[...] = widened(cot[item, :, at], up[...])
            filtered_rows(rows, edges, wide, wide_grad, narrow)
            grad = narrowed(narrow[...], down[...])
            scaled_grad = grad * scale
            grad_raw[item, 0, at] = (scaled_grad[0] * edges[0]).astype(BF16)
            grad_raw[item, 1 : rows + 1, at] = scaled_grad[1 : rows + 1].astype(BF16)
            grad_raw[item, rows + 1, at] = (scaled_grad[rows + 1] * edges[1]).astype(BF16)
            grad = grad[1 : rows + 1]
            own = raw[item, RIM : RIM + rows, at].astype(F32)
            grad_bias[item, at] = jnp.sum(jnp.sum(grad, axis=0), axis=1, keepdims=True)
            grad_demod[item, at] = jnp.sum(jnp.sum(grad * own, axis=0), axis=1, keepdims=True)
    blocks = count // items
    span = rows // blocks
    pairs = []
    kind = "near" if width < cotangent.shape[2] else "far"
    for x, part in zip(order(count, kind), grad_parts):
        dest = me ^ x
        pairs.append((grad_raw.at[dest // blocks, pl.ds((dest % blocks) * span, span + 2)], part))
    finished(started(sems, 0, pairs))


def backward_sinc(me, edges, factors, tables, up_sums, before, after, cotangent, parts, first_channel):
    count = len(parts)
    items, extent, _, columns = cotangent.shape
    span, width = parts[0].shape[0], factors.shape[1]
    rows = extent - 2 * RIM
    wide = pltpu.VMEM((extent, GROUP, 2 * columns), F32)
    outs = pl.pallas_call(
        functools.partial(backward_sinc_kernel, count, first_channel),
        out_shape=[struct((items, width, 1), F32)] * 2 + [struct((span + 2, width, columns), BF16)] * count,
        in_specs=[IN_SMEM, IN_SMEM] + [IN_VMEM] * 2 + [IN_HBM] * (5 + count),
        out_specs=[IN_VMEM, IN_VMEM] + [IN_HBM] * count,
        scratch_shapes=[
            pltpu.VMEM((items, extent, width, columns), BF16),
            pltpu.VMEM((items, extent, width, columns), BF16),
            pltpu.VMEM(tables[0].shape, BF16),
            pltpu.VMEM(tables[1].shape, BF16),
            pltpu.VMEM((items, rows + 2, width, columns), BF16),
            wide,
            wide,
            pltpu.VMEM((rows + 2, GROUP, 2 * columns), F32),
            pltpu.SemaphoreType.DMA((count + 5,)),
        ],
        compiler_params=PARAMS,
        name="backward_sinc",
    )(me, edges, factors, up_sums, before, after, cotangent, *tables, *parts)
    return outs[0], outs[1], outs[2:]


def scale_kernel(count, me_ref, scales, *refs):
    parts, (out, arrived, results, sems) = refs[:count], refs[count:]
    width, items, _, _ = out.shape
    finished(started(sems, 0, row_blocks(me_ref[0], parts, arrived, 0, "far")))
    leaving = []
    for item in range(items):
        for group in range(width // GROUP):
            at = slice(group * GROUP, (group + 1) * GROUP)
            value = arrived[item, :, at].astype(F32) * scales[item, at]
            results[at, item] = jnp.swapaxes(value, 0, 1)
            spot = pl.ds(group * GROUP, GROUP)
            leaving += started(sems, len(leaving), [(results.at[spot, item], out.at[spot, item])])
    finished(leaving)


def scaled(me, scales, parts, items):
    count = len(parts)
    span, width, columns = parts[0].shape
    rows = span * count // items
    return pl.pallas_call(
        functools.partial(scale_kernel, count),
        out_shape=struct((width, items, rows, columns), F32),
        in_specs=[IN_SMEM, IN_VMEM] + [IN_HBM] * count,
        out_specs=IN_HBM,
        scratch_shapes=[
            pltpu.VMEM((items, rows, width, columns), BF16),
            pltpu.VMEM((width, items, rows, columns), F32),
            pltpu.SemaphoreType.DMA((max(count, items * width // GROUP),)),
        ],
        compiler_params=PARAMS,
        name="scale_features",
    )(me, scales, *parts)


def in_thirds(value, lanes):
    terms = []
    for _ in range(3):
        terms.append(lax.reduce_precision(value, 8, 7))
        value = value - terms[-1]
    rows = jnp.stack(terms).astype(BF16).reshape(-1, lanes)
    return jnp.pad(rows, ((0, -rows.shape[0] % 16), (0, 0)))


def from_thirds(rows, shape):
    terms = rows.astype(F32).reshape(-1)[: 3 * shape[0] * shape[1]].reshape((3,) + shape)
    return terms[0] + terms[1] + terms[2]


def tree_sum(values):
    while len(values) > 1:
        values = [a + b for a, b in zip(values[::2], values[1::2])]
    return values[0]


def per_device(
    features,
    latent,
    affine,
    affine_bias,
    weight,
    out_bias,
    cotangent,
    latents_all,
    labels,
    class_means,
):
    highest = lax.Precision.HIGHEST
    own, items, rows, columns = features.shape
    channels = weight.shape[3]
    count = lax.axis_size("chan")
    dp_total = lax.axis_size("dp")
    me = lax.axis_index("chan")
    me_dp = lax.axis_index("dp")
    me_ref = me.astype(jnp.int32)[None]
    blocks = count // items
    span = rows // blocks
    split = max(1, min(2, own // GROUP))
    width = own // split

    styles = jnp.dot(latent, affine, preferred_element_type=F32) + affine_bias
    own_style = lax.dynamic_slice_in_dim(styles, me * own, own, 1)
    weight_full = weight.astype(F32)
    weight_sq = jnp.sum(weight_full * weight_full, axis=(0, 1))
    demod = lax.rsqrt(jnp.dot(styles * styles, weight_sq.T, precision=highest) + 1e-08)
    item = me // blocks
    item_scales = lax.dynamic_index_in_dim(styles, item, 0, keepdims=False).reshape(count, own, 1)

    before, after = from_neighbours(features, "dp", 2, 1)
    prepared = row_parts(me_ref, before, features, after, count)
    feats = exchange(prepared, "far")
    held, places = near_pieces(*weight_pieces(once(weight, prepared[0]), me_dp))
    shares = channels // held.shape[3]
    part = (me_dp % shares).astype(jnp.int32)[None]
    held = once(held, *feats[1:3], item_scales, demod)
    bit = shares // 2
    while bit > 1:
        met, met_places = met_pieces(held, places, bit)
        held, places = jnp.concatenate([held, met], axis=0), places + met_places
        bit //= 2
    cot_before, cot_after = from_neighbours(once(cotangent, feats[3]), "dp", 2, RIM)
    held = once(held, *feats[3:7])
    met, met_places = met_pieces(held, places, 1)
    pieces, places = [held, met], (tuple(places), tuple(met_places))

    table = up_table(columns)
    down_halves = halves(0.5 * table.T)
    tables = [np.concatenate(halves(table)), np.concatenate(down_halves + down_halves[:1])]
    up_sums = np.sum(table, axis=0)[None]
    edges = jnp.stack([me_dp > 0, me_dp < dp_total - 1]).astype(F32)

    item_scales = once(item_scales, cot_before, cot_after)
    raw_parts = conv_forward(me_ref, part, pieces, places, item_scales, feats)
    taps_backward = transposed_taps(
        me_ref, part, [once(piece, raw_parts[0]) for piece in pieces], places, channels
    )
    all_maps, grad_parts, bias_parts, demod_parts = [], [], [], []
    factors = jnp.concatenate([demod, out_bias[None]])[:, :, None]
    up = [(i, i + 1) for i in range(dp_total - 1)]
    down = [(j, i) for i, j in up]
    arrived = exchange(raw_parts, "mixed")
    cot = jnp.concatenate([cot_before, cotangent, cot_after], axis=2)
    cot = jnp.transpose(cot, (1, 2, 0, 3))
    head, tail = rims(me_ref, arrived, items, [taps_backward, cot])
    before, after = lax.ppermute(tail, "dp", up), lax.ppermute(head, "dp", down)
    for h in range(split):
        at = slice(h * width, (h + 1) * width)
        maps = (factors[:, at], tables, up_sums, before, after)
        all_maps.append(maps)
        bias_part, demod_part, parts = backward_sinc(
            me_ref, edges, *maps, cot, arrived, h * width
        )
        bias_parts.append(bias_part)
        demod_parts.append(demod_part)
        if h:
            parts = [once(part, *grad_parts[-4:]) for part in parts]
        grad_parts += exchange(parts, "near" if split > 1 else "far")
    bias_part = jnp.sum(jnp.concatenate(bias_parts, axis=1)[:, :, 0], axis=0)
    g_demod = jnp.concatenate(demod_parts, axis=1)[:, :, 0]

    output = [forward_sinc(me_ref, edges, *all_maps[0], arrived, own, [], 0, bias_parts[-1])]
    modded_parts, style_part, weight_sums = conv_backward(
        me_ref, item_scales, taps_backward, output[0], grad_parts, feats, dp_total
    )
    modded_parts = exchange(modded_parts, "far")
    for h in range(1, split):
        output = [forward_sinc(me_ref, edges, *all_maps[h], arrived, own, output, h * width, style_part)]
    output = output[0]
    grad_features = scaled(me_ref, own_style[:, :, None], modded_parts, items)

    grad_bias, g_demod_sum = lax.psum((once(bias_part, style_part), g_demod), "dp")
    cube = demod * demod * demod
    g_style_part = 2.0 * styles * jnp.dot(-0.5 * g_demod * cube, weight_sq, precision=highest)
    g_style_part = g_style_part + jnp.where(
        jnp.arange(items)[:, None] == item, style_part.reshape(1, channels), 0.0
    )
    g_wsq = jnp.dot((-0.5 * g_demod_sum * cube).T, styles * styles, precision=highest)

    tags = jnp.stack([labels // 64, labels % 64], axis=1).astype(BF16)
    tagged = jnp.concatenate([once(latents_all, head), jnp.pad(tags, ((0, 0), (0, 126)))], axis=1)
    tagged = lax.all_gather(tagged, ("dp", "chan"), axis=0, tiled=True)
    all_latents, tags = tagged[:, :-128], tagged[:, -128:-126].astype(F32)
    all_labels = (tags[:, 0] * 64.0 + tags[:, 1]).astype(jnp.int32)
    one_hot = all_labels[None, :] == jnp.arange(class_means.shape[0])[:, None]
    class_sums = jnp.dot(one_hot.astype(BF16), all_latents, preferred_element_type=F32)
    counts = jnp.sum(one_hot.astype(F32), axis=1)
    target = jnp.where(
        counts[:, None] > 0, class_sums / jnp.maximum(counts, 1.0)[:, None], class_means
    )

    share = channels // dp_total
    weight_sums = weight_sums.reshape(dp_total * 9 * channels, share)
    weight_sums = lax.psum_scatter(weight_sums, "dp", scatter_dimension=0, tiled=True)
    weight_sums = once(weight_sums.reshape(9, channels, share), *modded_parts, g_wsq, grad_bias, target, output)
    thirds = in_thirds(g_style_part, share)
    sent = []
    for x in order(count, "mixed"):
        part_x = lax.dynamic_slice_in_dim(weight_sums, (me ^ x) * own, own, 1)
        sent.append(jnp.concatenate([part_x.reshape(9 * own, share), thirds], axis=0))
    sent = exchange(sent, "mixed")
    g_weight = sum(value[: 9 * own].astype(F32) for value in sent).astype(BF16)
    style_sums = [from_thirds(value[9 * own :], styles.shape) for value in sent]
    g_style = tree_sum([style_sums[order(count, "mixed").index(x)] for x in range(count)])
    sent = once(jnp.concatenate([g_weight, in_thirds(g_style, share)], axis=0), grad_features)
    met = [sent] + [swapped(sent, "dp", x) for x in range(1, dp_total)]
    if share % 128 == 0:
        me_dp_ref = me_dp.astype(jnp.int32)[None]
        grad_weight = finished_weight(me_dp_ref, weight.reshape(9, own, channels), g_wsq, met)
    else:
        blocks = lax.all_gather(met[0][: 9 * own], "dp", axis=1, tiled=True)
        grad_weight = blocks.reshape(9, own, channels).astype(F32)
        grad_weight = grad_weight + 2.0 * weight_full.reshape(9, own, channels) * g_wsq
    grad_weight = grad_weight.reshape(weight.shape)
    g_style = tree_sum([from_thirds(value[9 * own :], styles.shape) for value in met])
    grad_affine_bias = jnp.sum(g_style, axis=0)
    grad_affine = jnp.dot(latent.astype(F32).T, g_style, precision=highest)
    grad_latent = jnp.dot(g_style, affine.astype(F32).T, precision=highest)
    return (
        output,
        grad_features,
        grad_latent,
        grad_affine,
        grad_affine_bias,
        grad_weight,
        grad_bias,
        target,
    )


def solution(mesh):
    in_specs = (
        P("chan", None, "dp", None),
        P(),
        P(),
        P(),
        P(None, None, "chan", None),
        P("chan"),
        P("chan", None, "dp", None),
        P(("dp", "chan"), None),
        P(("dp", "chan")),
        P(),
    )
    out_specs = (
        P("chan", None, "dp", None),
        P("chan", None, "dp", None),
        P(),
        P(),
        P(),
        P(None, None, "chan", None),
        P("chan"),
        P(),
    )
    return jax.shard_map(
        per_device, mesh=mesh, in_specs=in_specs, out_specs=out_specs, check_vma=False
    )
```
